32 devices in a mesh: span: 8 (over z, core), wall: 4 (over y, x).
Axes of the slice: x: 2, y: 2, z: 4, core: 2. Of those that a mesh axis runs over, the one named last changes fastest.
Arguments:
- noise: bfloat16 [3, 32, 256, 1024], P(None, None, 'wall', 'span'), may hold values from -6 to 6
- wall_scale: float32 [3], replicated, may hold values from 4 to 12
- span_scale: float32 [3], replicated, may hold values from 4 to 12
- lund_factor: float32 [6, 256], P(None, 'wall'), may hold values from 0.2 to 1
- mean_velocity: float32 [256], P('wall'), may hold values from 0.2 to 1
- owner_map: int32 [4, 8, 512, 1], P('wall', 'span'), may hold values from 0 to 31; in each aligned block of 512 rows (0 to 511, 512 to 1023, ..., all dimensions but the last counted through in order) at most 32 rows name the same one
Outputs:
- face_state: bfloat16 [32, 1024, 1536], P(('span', 'wall'))
The draws below stay inside these ranges and needn't reach their ends.
Inputs may be any that keep to these rules, and one draw needn't show every extreme that they name: `owner_map`: within one tile no owner receives more than 32 elements, and in every draw some tile sends exactly 32 elements to some owner; every device owns some element.
All inputs are finite; a program needn't handle non-finite values.
Results may differ from the reference program's by a relative error of at most 0.001.
Values may be sent and summed in bfloat16 or wider, within the bound.
No kernel may reach another device: no remote copies, remote signals or barrier semaphores. Data moves between devices by JAX's collectives and lax.ppermute only.
A program may use at most 64 MiB of HBM per device.

```python
import math
import jax
import jax.numpy as jnp
import numpy as np
from jax import lax

CY = 64
CZ = 128
TPL = 32
HALO = 24
EDGE = 4
NY = 256
NZ = 1024
ELEM_DEV = 512
CAP = 32
PAY = 1536
N_SPAN = 8
N_WALL = 4
DEVICES = 32


def filter_lengths(key, salt):
    base = jax.random.fold_in(key, salt)
    order = jax.random.permutation(jax.random.fold_in(base, 1), 3)
    frac = jax.random.uniform(jax.random.fold_in(base, 2), (3,), jnp.float32)
    return 4.0 * jnp.exp(math.log(3.0) * (order.astype(jnp.float32) + frac) / 3.0)


def draw_wall_scale(key, part):
    return filter_lengths(key, 7001)


def draw_span_scale(key, part):
    return filter_lengths(key, 7002)


def levels(own_key, shape, split, low, top_value):
    gain = 1.0
    for axis_at, blocks in split:
        steps = jax.random.uniform(jax.random.fold_in(jax.random.fold_in(own_key, 6), axis_at), (blocks,), jnp.float32, low / len(split), top_value / len(split))
        gain = gain * jnp.repeat(jnp.exp(steps), shape[axis_at] // blocks).reshape((-1,) + (1,) * (len(shape) - 1 - axis_at))
    return gain


def shared_out(key, own, number, rows, amount, top, most, skew):
    sequence = jax.random.permutation(key, amount)
    heavy_load, usual = load_shares(amount, rows * top, most, skew, True), load_shares(amount, rows * top, most, skew, False)
    places = jnp.arange(amount)

    def named(lengths, turn):
        used = int((lengths > 0).sum())
        fixed = max(1, used // 4)
        passed = fixed + (places - fixed + turn * (used - fixed)) % max(1, amount - fixed)
        return jnp.zeros((amount,), jnp.int32).at[sequence[jnp.where(places < fixed, places, passed)]].set(jnp.asarray(lengths, jnp.int32))

    lengths = jnp.where(number % 4 == 0, named(heavy_load, number // 4), named(usual, number - number // 4 - 1))
    mixed = jax.random.permutation(jax.random.fold_in(own, 3), amount)
    source_of, taker = mixed[0:amount // 2 * 2:2], mixed[1:amount // 2 * 2:2]
    slack = jnp.minimum(lengths[source_of] - 1, most - lengths[taker]) // 2
    slack = jnp.where((source_of == sequence[0]) | (taker == sequence[0]) | (lengths[taker] == 0), 0, jnp.maximum(slack, 0))
    passed = jax.random.randint(jax.random.fold_in(own, 4), (amount // 2,), 0, 1 << 20) % (slack + 1)
    lengths = lengths.at[source_of].add(-passed).at[taker].add(passed)
    items = jnp.searchsorted(jnp.cumsum(lengths), jnp.arange(rows * top), side="right").astype(jnp.int32)
    table = items.reshape(top, rows).T
    table = table[jax.random.permutation(jax.random.fold_in(own, 1), rows)]
    turn = jax.random.randint(jax.random.fold_in(own, 2), (rows, 1), 0, top)
    return jnp.take_along_axis(table, (jnp.arange(top)[None, :] + turn) % top, axis=1)


def load_shares(amount, total, bound, lean, full):
    weights = [(1 << 20) // math.isqrt(grade ** lean) + 1 for grade in range(1, amount + 1)]
    largest = bound if full else min(bound, max(-(-total // amount), total * weights[0] // sum(weights)))
    least = 1 if total - largest >= amount - 1 else 0
    counts, spare = [largest] + [least] * (amount - 1), total - largest - least * (amount - 1)
    while spare > 0:
        free = [i for i in range(1, amount) if counts[i] < largest] or [i for i in range(1, amount) if counts[i] < bound]
        whole, left = sum([weights[i] for i in free]), spare
        for i in free:
            more = min(bound - counts[i], max(1, left * weights[i] // whole), spare)
            counts[i] = counts[i] + more
            spare = spare - more
    return np.array(counts)


def centred(own_key, extent, width, bound, cuts=(), held_as=jnp.bfloat16):
    drawn = jax.random.normal(own_key, extent, jnp.float32) * width
    if len(cuts) > 0:
        drawn = levels(own_key, extent, cuts, -0.22, 0.18) * drawn
    return jnp.clip(drawn, min=-bound, max=bound).astype(held_as)


def setup_inputs(seed: int = 0) -> dict:
    keys = jax.random.split(jax.random.key(seed), 7)
    noise = centred(keys[0], (3, TPL, NY, NZ), 1.0, 6.0, ((2, 4), (3, 8)))
    wall_scale = draw_wall_scale(jax.random.fold_in(keys[6], 71), 0)
    span_scale = draw_span_scale(jax.random.fold_in(keys[6], 71), 0)
    lund_factor = jnp.clip(0.2 + 0.8 * jax.random.uniform(keys[3], (6, NY), jnp.float32) ** levels(keys[3], (6, NY), ((1, 4),), -0.2, 0.2), 0.2, 1.0)
    mean_velocity = jnp.clip(0.2 + 0.8 * jax.random.uniform(keys[4], (NY,), jnp.float32) ** levels(keys[4], (NY,), ((0, 4),), -0.2, 0.2), 0.2, 1.0)
    owner_map_keys = jax.random.split(jax.random.fold_in(keys[5], 1), N_WALL * N_SPAN * ELEM_DEV // ELEM_DEV)
    owner_map_turns = jax.random.permutation(jax.random.fold_in(keys[5], 3), N_WALL * N_SPAN * ELEM_DEV // ELEM_DEV)
    owner_map = jax.vmap(lambda own, number: shared_out(jax.random.fold_in(keys[5], 2), own, number, ELEM_DEV, DEVICES, 1, CAP, 2))(owner_map_keys, owner_map_turns).reshape((N_WALL, N_SPAN, ELEM_DEV, 1))
    return dict(noise=noise, wall_scale=wall_scale, span_scale=span_scale, lund_factor=lund_factor, mean_velocity=mean_velocity, owner_map=owner_map)


def klein_taps(scale):
    offsets = jnp.arange(-HALO, HALO + 1).astype(jnp.float32)
    raw = jnp.exp(-math.pi * offsets * offsets / (2.0 * scale[:, None] * scale[:, None]))
    return raw / jnp.sqrt(lax.optimization_barrier(jnp.sum(raw * raw, axis=1, keepdims=True)))

def filter_plane(packed):
    plane, wall_row, span_row = packed
    padded = jnp.pad(plane, ((HALO, HALO), (0, 0)))
    smooth = jnp.zeros_like(plane)
    for k in range(2 * HALO + 1):
        smooth = smooth + wall_row[k] * padded[k:k + NY]
    result = jnp.zeros_like(plane)
    for k in range(2 * HALO + 1):
        result = result + span_row[k] * jnp.roll(smooth, -(k - HALO), axis=1)
    return result

def reference(noise, wall_scale, span_scale, lund_factor, mean_velocity, owner_map):
    wall_taps = jnp.repeat(klein_taps(wall_scale), TPL, axis=0)
    span_taps = jnp.repeat(klein_taps(span_scale), TPL, axis=0)
    planes = noise.astype(jnp.float32).reshape(3 * TPL, NY, NZ)
    psi = lax.map(filter_plane, (planes, wall_taps, span_taps)).reshape(3, TPL, NY, NZ)
    fac = lund_factor[:, None, :, None]
    along = mean_velocity[None, :, None] + fac[0] * psi[0]
    normal = fac[1] * psi[0] + fac[2] * psi[1]
    spanwise = fac[3] * psi[0] + fac[4] * psi[1] + fac[5] * psi[2]
    velocity = jnp.stack([along, normal, spanwise]).astype(jnp.bfloat16)
    n_wall = NY // CY
    n_span = NZ // CZ
    devices = n_wall * n_span
    cells = velocity.reshape(3, TPL, n_wall, CY // EDGE, EDGE, n_span, CZ // EDGE, EDGE)
    cells = jnp.transpose(cells, (2, 5, 3, 6, 0, 1, 4, 7)).reshape(n_wall, n_span, ELEM_DEV, PAY)
    owners = owner_map[..., 0]
    onehot = (owners[..., None] == jnp.arange(devices, dtype=jnp.int32)).astype(jnp.int32)
    rank = lax.optimization_barrier(jnp.sum(onehot * (jnp.cumsum(onehot, axis=2) - 1), axis=3))
    source = jnp.arange(n_span, dtype=jnp.int32)[None, :] * n_wall + jnp.arange(n_wall, dtype=jnp.int32)[:, None]
    target = owners * (devices * CAP) + source[:, :, None] * CAP + rank
    flat = jnp.zeros((devices * devices * CAP, PAY), jnp.bfloat16)
    flat = flat.at[target.reshape(-1)].set(cells.reshape(-1, PAY))
    return flat.reshape(devices, devices * CAP, PAY)
```

```python
import functools
import math

import jax
import jax.numpy as jnp
from jax import lax
from jax.experimental import pallas as pl
from jax.experimental.pallas import tpu as pltpu
from jax.sharding import PartitionSpec as P

HALO = 24
EDGE = 4
LANES = 128
F32 = jnp.float32
BF16 = jnp.bfloat16
VMEM = pl.BlockSpec(memory_space=pltpu.VMEM)
SMEM = pl.BlockSpec(memory_space=pltpu.SMEM)
ROWS_BY_ROWS = (((1,), (1,)), ((), ()))


def iota(shape, dim):
    return lax.broadcasted_iota(jnp.int32, shape, dim)


def tap_values(scale, distance, valid):
    scale = jnp.full((1, 1), scale, F32)
    k = iota((1, LANES), 1) - HALO
    squares = jnp.where(k <= HALO, jnp.exp(-math.pi * (k * k).astype(F32) / (scale * scale)), 0.0)
    norm = jnp.sqrt(jnp.sum(squares, axis=1, keepdims=True))
    d = distance.astype(F32)
    raw = jnp.exp(-math.pi * (d * d) / (2.0 * scale * scale))
    inside = valid & (distance >= -HALO) & (distance <= HALO)
    return jnp.where(inside, raw, 0.0) / norm


def split(x):
    high = x.astype(BF16)
    return high, (x - high.astype(F32)).astype(BF16)


def taps_kernel(wall_scale, span_scale, wall_ref, span_ref):
    trio, twice, rows = wall_ref.shape
    faces = rows // (EDGE * EDGE)
    cols = span_ref.shape[3] // 2
    i = iota((rows, rows), 0)
    y = (i % faces) * (EDGE * EDGE) + (i // (faces * EDGE)) * EDGE + (i // faces) % EDGE
    k = iota((2 * cols, cols), 0)
    q = k - cols
    side, odd, r = q // (2 * HALO), (q // HALO) % 2, q % HALO
    z = jnp.where(q < 0, k, jnp.where(side == 0, r - HALO, cols + r))
    n = iota((2 * cols, cols), 1)
    target = (n % (cols // EDGE)) * EDGE + n // (cols // EDGE)
    everywhere = i >= 0
    for c in range(trio):
        high, low = split(tap_values(wall_scale[c], iota((rows, rows), 1) - y, everywhere))
        wall_ref[c, :rows] = high
        wall_ref[c, rows:] = low
        for parity in range(2):
            valid = (q < 0) | ((q < 4 * HALO) & (odd == parity))
            high, low = split(tap_values(span_scale[c], z - target, valid))
            span_ref[c, parity] = jnp.concatenate([high, low], axis=1)


def edges_kernel(noise_ref, low_ref, high_ref):
    walls, trio, planes, rows, cols = noise_ref.shape
    wide = 2 * HALO
    row, col = iota((wide, cols), 0), iota((wide, cols), 1)
    pick = jnp.where(col == jnp.where(row < HALO, row, cols - wide + row), 1.0, 0.0).astype(BF16)
    for c in range(trio):
        for pair in range(planes // 2):
            edges = []
            for t in (2 * pair, 2 * pair + 1):
                plane = jnp.concatenate([noise_ref[w, c, t] for w in range(walls)], axis=0)
                edges.append(lax.dot_general(pick, plane, ROWS_BY_ROWS, preferred_element_type=F32))
            at = pl.ds((c * planes // 2 + pair) * wide, wide)
            low_ref[at] = jnp.concatenate([e[:HALO] for e in edges], axis=0).astype(BF16)
            high_ref[at] = jnp.concatenate([e[HALO:] for e in edges], axis=0).astype(BF16)


def swap_blocks(blocks, cols):
    part = cols // EDGE
    lane = iota(blocks[0].shape, 1)
    for step in (2, 1):
        first = (lane // (part * step)) % 2 == 0
        out = list(blocks)
        for a in range(EDGE):
            if a & step:
                continue
            one, two = blocks[a], blocks[a + step]
            out[a] = jnp.where(first, one, pltpu.roll(two, part * step, 1))
            out[a + step] = jnp.where(first, pltpu.roll(one, cols - part * step, 1), two)
        blocks = out
    return blocks


def main_kernel(noise_ref, low_ref, high_ref, wall_ref, span_ref, factor_ref, target_ref, out_ref, cells_ref):
    walls, trio, planes, rows, cols = noise_ref.shape
    full = walls * rows
    faces = full // (EDGE * EDGE)
    tile_faces = faces // walls
    devices, _, slots, _ = out_ref.shape
    values = planes * EDGE * EDGE
    wide = 2 * HALO

    def pair_step(pair, carry):
        psi = [[], []]
        for c in range(trio):
            at = pl.ds(pl.multiple_of((c * planes // 2 + pair) * wide, wide), wide)
            halo = jnp.concatenate(
                [low_ref[at], high_ref[at], jnp.zeros((cols - 2 * wide, full), BF16)], axis=0
            )
            both = jnp.concatenate(
                [
                    jnp.concatenate([noise_ref[w, c, 2 * pair + odd] for w in range(walls)], axis=0)
                    for odd in range(2)
                ],
                axis=1,
            )
            smooth = jnp.dot(wall_ref[c], both, preferred_element_type=F32)
            smooth = smooth[:full] + smooth[full:]
            beside = lax.dot_general(wall_ref[c], halo, ROWS_BY_ROWS, preferred_element_type=F32)
            beside = beside[:full] + beside[full:]
            for odd in range(2):
                high, low = split(
                    jnp.concatenate([smooth[:, odd * cols : (odd + 1) * cols], beside], axis=1)
                )
                matrix = span_ref[c, odd]
                broad = jnp.dot(high, matrix, preferred_element_type=F32)
                small = jnp.dot(low, matrix[:, :cols], preferred_element_type=F32)
                psi[odd].append(broad[:, :cols] + (broad[:, cols:] + small))
        for odd in range(2):
            p = psi[odd]
            velocity = (
                factor_ref[6] + factor_ref[0] * p[0],
                factor_ref[1] * p[0] + factor_ref[2] * p[1],
                factor_ref[3] * p[0] + factor_ref[4] * p[1] + factor_ref[5] * p[2],
            )
            quarter = full // EDGE
            for c in range(trio):
                blocks = [velocity[c][a * quarter : (a + 1) * quarter] for a in range(EDGE)]
                for dz, block in enumerate(swap_blocks(blocks, cols)):
                    for dy in range(EDGE):
                        j = (2 * pair + odd) * EDGE * EDGE + dy * EDGE + dz
                        cells_ref[c, pl.ds(j, faces, stride=values), :] = block[dy * faces : (dy + 1) * faces]
        return carry

    lax.fori_loop(0, planes // 2, pair_step, 0)

    for w in range(walls):
        payload = jnp.concatenate(
            [
                jnp.concatenate(
                    [
                        cells_ref[c, pl.ds((w * tile_faces + f) * values, values), :].astype(BF16)
                        for f in range(tile_faces)
                    ],
                    axis=1,
                )
                for c in range(trio)
            ],
            axis=0,
        )
        target = target_ref[pl.ds(w, 1), :]
        onehot = iota((devices * slots, target.shape[1]), 0) == target
        onehot = jnp.where(onehot, 1.0, 0.0).astype(BF16)
        sent = lax.dot_general(onehot, payload, ROWS_BY_ROWS, preferred_element_type=F32)
        out_ref[:, w] = sent.astype(BF16).reshape(devices, slots, trio * values)


def join_kernel(trio, in_ref, out_ref):
    walls, rows, width = in_ref.shape
    values = width // trio
    for c in range(trio):
        for w in range(walls):
            start = (c * walls + w) * values
            out_ref[0, :, start : start + values] = in_ref[w, :, c * values : (c + 1) * values]


def per_device(noise, wall_scale, span_scale, lund_factor, mean_velocity, owner_map):
    trio, all_planes, rows, cols = noise.shape
    n_span = lax.axis_size("span")
    n_wall = lax.axis_size("wall")
    devices = n_span * n_wall
    planes = all_planes // n_wall
    full = rows * n_wall
    faces = full // (EDGE * EDGE)
    values = planes * EDGE * EDGE
    big = pltpu.CompilerParams(vmem_limit_bytes=56 * 1024 * 1024)

    owners = owner_map.reshape(-1)
    elements = owners.shape[0]
    slots = max(8, 2 * elements // devices)
    same = (owners[:, None] == owners[None, :]) & (
        jnp.arange(elements)[None, :] < jnp.arange(elements)[:, None]
    )
    target = owners * slots + jnp.sum(same.astype(jnp.int32), axis=1)
    small = jnp.concatenate([lund_factor.reshape(-1), mean_velocity, target.astype(F32)])
    small = lax.all_gather(small, "wall")
    target = small[:, 7 * rows :].astype(jnp.int32)
    factor = small[:, : 7 * rows].reshape(n_wall, 7, rows).transpose(1, 0, 2)
    factor = factor.reshape(7, faces, EDGE, EDGE).transpose(0, 2, 3, 1).reshape(7, full)
    factor = jnp.broadcast_to(factor[:, :, None], (7, full, cols))

    wall_taps, span_taps = pl.pallas_call(
        taps_kernel,
        in_specs=[SMEM, SMEM],
        out_specs=[VMEM, VMEM],
        out_shape=[
            jax.ShapeDtypeStruct((trio, 2 * full, full), BF16),
            jax.ShapeDtypeStruct((trio, 2, 2 * cols, 2 * cols), BF16),
        ],
        compiler_params=big,
        name="taps",
    )(wall_scale, span_scale)

    swapped = noise.reshape(trio, n_wall, planes, rows, cols).transpose(1, 0, 2, 3, 4)
    swapped = lax.all_to_all(swapped, "wall", 0, 0, tiled=True)
    edge = jax.ShapeDtypeStruct((trio * planes * HALO, full), BF16)
    first, last = pl.pallas_call(
        edges_kernel,
        in_specs=[VMEM],
        out_specs=[VMEM, VMEM],
        out_shape=[edge, edge],
        compiler_params=big,
        name="edges",
    )(swapped)
    up = [(i, (i + 1) % n_span) for i in range(n_span)]
    low = lax.ppermute(last, "span", up)
    high = lax.ppermute(first, "span", [(b, a) for a, b in up])

    outgoing = pl.pallas_call(
        main_kernel,
        in_specs=[VMEM] * 7,
        out_specs=VMEM,
        out_shape=jax.ShapeDtypeStruct((devices, n_wall, slots, trio * values), BF16),
        scratch_shapes=[pltpu.VMEM((trio, faces * values, cols), F32)],
        compiler_params=big,
        name="filter",
    )(swapped, low, high, wall_taps, span_taps, factor, target)

    received = lax.all_to_all(outgoing, ("span", "wall"), 0, 0, tiled=True)
    return pl.pallas_call(
        functools.partial(join_kernel, trio),
        grid=(n_span,),
        in_specs=[pl.BlockSpec((n_wall, n_wall * slots, trio * values), lambda s: (s, 0, 0))],
        out_specs=pl.BlockSpec((1, n_wall * slots, trio * values * n_wall), lambda s: (0, s, 0)),
        out_shape=jax.ShapeDtypeStruct((1, devices * slots, trio * values * n_wall), BF16),
        compiler_params=big,
        name="join",
    )(received.reshape(devices, n_wall * slots, trio * values))


def solution(mesh):
    return jax.shard_map(
        per_device,
        mesh=mesh,
        in_specs=(
            P(None, None, "wall", "span"),
            P(),
            P(),
            P(None, "wall"),
            P("wall"),
            P("wall", "span", None, None),
        ),
        out_specs=P(("span", "wall"), None, None),
        check_vma=False,
    )
```

```python
import functools
import math

import jax
import jax.numpy as jnp
from jax import lax
from jax.experimental import pallas as pl
from jax.experimental.pallas import tpu as pltpu
from jax.sharding import PartitionSpec as P

HALO = 24
EDGE = 4
LANES = 128
FACTORS = 7
F32 = jnp.float32
BF16 = jnp.bfloat16
VMEM = pl.BlockSpec(memory_space=pltpu.VMEM)
SMEM = pl.BlockSpec(memory_space=pltpu.SMEM)
ROWS_BY_ROWS = (((1,), (1,)), ((), ()))
LIMIT = pltpu.CompilerParams(vmem_limit_bytes=40 * 1024 * 1024)


def iota(shape, dim):
    return lax.broadcasted_iota(jnp.int32, shape, dim)


def split(x):
    high = x.astype(BF16)
    return high, (x - high.astype(F32)).astype(BF16)


def tap_values(scale, distance, valid):
    scale = jnp.full((1, 1), scale, F32)
    k = iota((1, LANES), 1) - HALO
    squares = jnp.where(k <= HALO, jnp.exp(-math.pi * (k * k).astype(F32) / (scale * scale)), 0.0)
    norm = jnp.sqrt(jnp.sum(squares, axis=1, keepdims=True))
    d = distance.astype(F32)
    raw = jnp.exp(-math.pi * (d * d) / (2.0 * scale * scale))
    inside = valid & (distance >= -HALO) & (distance <= HALO)
    return jnp.where(inside, raw, 0.0) / norm


def cell_row(i, faces):
    return (i % faces) * (EDGE * EDGE) + (i // (faces * EDGE)) * EDGE + (i // faces) % EDGE


def taps_kernel(wall_scale, span_scale, wall_first, wall_rest, span_first, span_rest):
    full = wall_first.shape[2]
    cols = span_first.shape[3] // 2
    i = iota((full, full), 0)
    y = cell_row(i, full // (EDGE * EDGE))
    k = iota((2 * cols, cols), 0)
    q = k - cols
    side, odd, r = q // (2 * HALO), (q // HALO) % 2, q % HALO
    z = jnp.where(q < 0, k, jnp.where(side == 0, r - HALO, cols + r))
    n = iota((2 * cols, cols), 1)
    target = (n % (cols // EDGE)) * EDGE + n // (cols // EDGE)
    for c in range(wall_first.shape[0] + wall_rest.shape[0]):
        wall_ref, span_ref, at = (wall_first, span_first, 0) if c == 0 else (wall_rest, span_rest, c - 1)
        high, low = split(tap_values(wall_scale[c], iota((full, full), 1) - y, i >= 0))
        wall_ref[at, :full] = high
        wall_ref[at, full:] = low
        for parity in range(2):
            valid = (q < 0) | ((q < 4 * HALO) & (odd == parity))
            high, low = split(tap_values(span_scale[c], z - target, valid))
            span_ref[at, parity] = jnp.concatenate([high, low], axis=1)


def pack_kernel(devices, noise_ref, lund_ref, mean_ref, owner_ref, out_ref):
    walls, height, cols = out_ref.shape
    planes = noise_ref.shape[1] // walls
    rows = noise_ref.shape[2]
    for w in range(walls):
        for t in range(planes):
            out_ref[w, t * rows : (t + 1) * rows] = noise_ref[0, w * planes + t]
    owner = owner_ref[...]
    elements = owner.shape[1]
    mine = jnp.where(iota((devices, elements), 0) == owner, 1.0, 0.0)
    before = jnp.where(iota((elements, elements), 0) < iota((elements, elements), 1), 1.0, 0.0)
    count = jnp.dot(mine.astype(BF16), before.astype(BF16), preferred_element_type=F32)
    rank = jnp.sum(mine * count, axis=0, keepdims=True)
    pieces = [owner.astype(F32), rank]
    pieces = [p[:, at : at + cols] for p in pieces for at in range(0, elements, cols)]
    factor = jnp.concatenate([lund_ref[...], mean_ref[...]], axis=0)
    factor = jnp.concatenate([factor, jnp.zeros((FACTORS, cols - rows), F32)], axis=1)
    for _ in range(3):
        part = factor.astype(BF16).astype(F32)
        pieces.append(part)
        factor = factor - part
    tail = height - planes * rows
    pieces.append(jnp.zeros((tail - sum(p.shape[0] for p in pieces), cols), F32))
    small = jnp.concatenate(pieces, axis=0).astype(BF16)
    for w in range(walls):
        out_ref[w, planes * rows :] = small


def small_kernel(slots, in_ref, factor_ref, target_ref):
    walls, tail, cols = in_ref.shape
    full = factor_ref.shape[1]
    rows = full // walls
    count = target_ref.shape[1]
    columns = jnp.zeros((full, tail), F32)
    y = cell_row(iota((full, cols), 0), full // (EDGE * EDGE))
    for w in range(walls):
        small = in_ref[w]
        pick = jnp.where(y == iota((full, cols), 1) + w * rows, 1.0, 0.0)
        pick = jnp.where(iota((full, cols), 1) < rows, pick, 0.0).astype(BF16)
        columns = columns + lax.dot_general(pick, small, ROWS_BY_ROWS, preferred_element_type=F32)
        numbers = small.astype(F32)
        target = numbers[:count] * slots + numbers[count : 2 * count]
        target_ref[w] = target.astype(jnp.int32)
    for f in range(FACTORS):
        at = 2 * count + f
        total = sum(columns[:, at + p * FACTORS : at + p * FACTORS + 1] for p in range(3))
        factor_ref[f] = jnp.broadcast_to(total, (full, cols))


def plane_of(noise_ref, c, t, rows):
    walls = noise_ref.shape[0]
    return jnp.concatenate(
        [noise_ref[w, c, t * rows : (t + 1) * rows] for w in range(walls)], axis=0
    )


def edges_kernel(planes, noise_ref, low_ref, high_ref):
    walls, some, _, cols = noise_ref.shape
    rows = low_ref.shape[1] // walls
    wide = 2 * HALO
    row, col = iota((wide, cols), 0), iota((wide, cols), 1)
    pick = jnp.where(col == jnp.where(row < HALO, row, cols - wide + row), 1.0, 0.0).astype(BF16)
    for c in range(some):
        for pair in range(planes // 2):
            edges = [
                lax.dot_general(
                    pick, plane_of(noise_ref, c, t, rows), ROWS_BY_ROWS, preferred_element_type=F32
                )
                for t in (2 * pair, 2 * pair + 1)
            ]
            at = pl.ds((c * planes // 2 + pair) * wide, wide)
            low_ref[at] = jnp.concatenate([e[:HALO] for e in edges], axis=0).astype(BF16)
            high_ref[at] = jnp.concatenate([e[HALO:] for e in edges], axis=0).astype(BF16)


def swap_blocks(blocks, cols):
    part = cols // EDGE
    lane = iota(blocks[0].shape, 1)
    for step in (2, 1):
        first = (lane // (part * step)) % 2 == 0
        out = list(blocks)
        for a in range(EDGE):
            if a & step:
                continue
            one, two = blocks[a], blocks[a + step]
            out[a] = jnp.where(first, one, pltpu.roll(two, part * step, 1))
            out[a + step] = jnp.where(first, pltpu.roll(one, cols - part * step, 1), two)
        blocks = out
    return blocks


def filter_kernel(first, planes, noise_ref, low_ref, high_ref, wall_ref, span_ref, factor_ref, target_ref, *rest):
    if first:
        out_ref, psi_ref, cells_ref = rest
    else:
        psi_ref, out_ref, cells_ref = rest
    walls, some, _, cols = noise_ref.shape
    full = wall_ref.shape[2]
    rows = full // walls
    faces = full // (EDGE * EDGE)
    tile_faces = faces // walls
    devices, _, slots, _ = out_ref.shape
    values = planes * EDGE * EDGE
    wide = 2 * HALO

    def pair_step(pair, carry):
        psi = [[], []]
        for c in range(some):
            at = pl.ds(pl.multiple_of((c * planes // 2 + pair) * wide, wide), wide)
            halo = jnp.concatenate(
                [low_ref[at], high_ref[at], jnp.zeros((cols - 2 * wide, full), BF16)], axis=0
            )
            both = []
            for odd in range(2):
                at = pl.ds(pl.multiple_of((2 * pair + odd) * rows, rows), rows)
                both.append(jnp.concatenate([noise_ref[w, c, at] for w in range(walls)], axis=0))
            both = jnp.concatenate(both, axis=1)
            smooth = jnp.dot(wall_ref[c], both, preferred_element_type=F32)
            smooth = smooth[:full] + smooth[full:]
            beside = lax.dot_general(wall_ref[c], halo, ROWS_BY_ROWS, preferred_element_type=F32)
            beside = beside[:full] + beside[full:]
            for odd in range(2):
                high, low = split(
                    jnp.concatenate([smooth[:, odd * cols : (odd + 1) * cols], beside], axis=1)
                )
                matrix = span_ref[c, odd]
                broad = jnp.dot(high, matrix, preferred_element_type=F32)
                small = jnp.dot(low, matrix[:, :cols], preferred_element_type=F32)
                psi[odd].append(broad[:, :cols] + (broad[:, cols:] + small))
        for odd in range(2):
            t = 2 * pair + odd
            if first:
                p = psi[odd][0]
                psi_ref[t] = p
                velocity = (factor_ref[6] + factor_ref[0] * p,)
            else:
                p, q, r = psi_ref[t], *psi[odd]
                velocity = (
                    factor_ref[1] * p + factor_ref[2] * q,
                    factor_ref[3] * p + factor_ref[4] * q + factor_ref[5] * r,
                )
            quarter = full // EDGE
            for c in range(some):
                blocks = [velocity[c][a * quarter : (a + 1) * quarter] for a in range(EDGE)]
                for dz, block in enumerate(swap_blocks(blocks, cols)):
                    for dy in range(EDGE):
                        j = t * EDGE * EDGE + dy * EDGE + dz
                        cells_ref[c, pl.ds(j, faces, stride=values), :] = block[dy * faces : (dy + 1) * faces]
        return carry

    lax.fori_loop(0, planes // 2, pair_step, 0)

    for w in range(walls):
        payload = [
            [
                cells_ref[c, pl.ds((w * tile_faces + f) * values, values), :].astype(BF16)
                for f in range(tile_faces)
            ]
            for c in range(some)
        ]
        payload = jnp.concatenate([jnp.concatenate(p, axis=1) for p in payload], axis=0)
        slot = iota((devices * slots, cols), 0)
        onehot = [
            jnp.where(slot == target_ref[w, f : f + 1], 1.0, 0.0).astype(BF16)
            for f in range(tile_faces)
        ]
        onehot = jnp.concatenate(onehot, axis=1)
        sent = lax.dot_general(onehot, payload, ROWS_BY_ROWS, preferred_element_type=F32)
        out_ref[:, w] = sent.astype(BF16).reshape(devices, slots, some * values)


def join_kernel(some, in_ref, *rest):
    out_ref = rest[-1]
    walls, _, width = in_ref.shape
    values = width // some
    for c in range(some):

        @pl.when(pl.program_id(1) == c)
        def _():
            for w in range(walls):
                out_ref[0, :, w * values : (w + 1) * values] = in_ref[w, :, c * values : (c + 1) * values]


def per_device(noise, wall_scale, span_scale, lund_factor, mean_velocity, owner_map):
    trio, all_planes, rows, cols = noise.shape
    n_span = lax.axis_size("span")
    n_wall = lax.axis_size("wall")
    devices = n_span * n_wall
    planes = all_planes // n_wall
    full = rows * n_wall
    faces = full // (EDGE * EDGE)
    values = planes * EDGE * EDGE
    owners = owner_map.reshape(1, -1)
    elements = owners.shape[1]
    slots = max(8, 2 * elements // devices)
    count = elements // cols
    tail = -(-(2 * count + 3 * FACTORS) // 16) * 16
    rest = trio - 1
    struct = jax.ShapeDtypeStruct

    def call(kernel, n_in, outs, name, scratch=(), grid=()):
        specs = [VMEM] * len(outs)
        return pl.pallas_call(
            kernel,
            grid=grid,
            in_specs=n_in if isinstance(n_in, list) else [VMEM] * n_in,
            out_specs=specs if len(outs) > 1 else specs[0],
            out_shape=outs if len(outs) > 1 else outs[0],
            scratch_shapes=scratch,
            compiler_params=LIMIT,
            name=name,
        )

    packed = call(
        functools.partial(pack_kernel, devices),
        [pl.BlockSpec((1, all_planes, rows, cols), lambda i: (0, 0, 0, 0)), VMEM, VMEM, VMEM],
        [struct((n_wall, planes * rows + tail, cols), BF16)],
        "pack",
        grid=(1,),
    )(noise, lund_factor, mean_velocity.reshape(1, rows), owners)
    packed = lax.all_to_all(packed, "wall", 0, 0, tiled=True)
    others = noise[1:].reshape(rest, n_wall, planes * rows, cols).transpose(1, 0, 2, 3)
    others = lax.all_to_all(others, "wall", 0, 0, tiled=True)

    wall_first, wall_rest, span_first, span_rest = call(
        taps_kernel,
        [SMEM, SMEM],
        [
            struct((1, 2 * full, full), BF16),
            struct((rest, 2 * full, full), BF16),
            struct((1, 2, 2 * cols, 2 * cols), BF16),
            struct((rest, 2, 2 * cols, 2 * cols), BF16),
        ],
        "taps",
    )(wall_scale, span_scale)
    factor, target = call(
        functools.partial(small_kernel, slots),
        1,
        [struct((FACTORS, full, cols), F32), struct((n_wall, count, cols), jnp.int32)],
        "small",
    )(packed[:, planes * rows :])

    up = [(i, (i + 1) % n_span) for i in range(n_span)]
    down = [(b, a) for a, b in up]

    def beside(swapped, some, name):
        edge = struct((some * planes * HALO, full), BF16)
        first, last = call(functools.partial(edges_kernel, planes), 1, [edge, edge], name)(swapped)
        return lax.ppermute(last, "span", up), lax.ppermute(first, "span", down)

    def send(x):
        return lax.all_to_all(x, ("span", "wall"), 0, 0, tiled=True).reshape(devices, n_wall * slots, -1)

    def out(some):
        return struct((devices, n_wall, slots, some * values), BF16)

    def cells(some):
        return [pltpu.VMEM((some, faces * values, cols), F32)]

    packed = packed[:, None]
    low, high = beside(packed, 1, "edges_first")
    sent, psi = call(
        functools.partial(filter_kernel, True, planes),
        7,
        [out(1), struct((planes, full, cols), F32)],
        "filter_first",
        cells(1),
    )(packed, low, high, wall_first, span_first, factor, target)
    got_first = send(sent)
    low, high = beside(others, rest, "edges_rest")
    sent = call(
        functools.partial(filter_kernel, False, planes), 8, [out(rest)], "filter_rest", cells(rest)
    )(others, low, high, wall_rest, span_rest, factor, target, psi)
    got_rest = send(sent)

    whole = struct((1, devices * slots, trio * values * n_wall), BF16)
    block = (1, n_wall * slots, values * n_wall)
    def join(received, some, before):
        keep = [] if before is None else [before]
        return pl.pallas_call(
            functools.partial(join_kernel, some),
            grid=(n_span, some),
            in_specs=[pl.BlockSpec((n_wall, n_wall * slots, some * values), lambda s, c: (s, 0, 0))]
            + [pl.BlockSpec(memory_space=pl.ANY)] * len(keep),
            out_specs=pl.BlockSpec(block, lambda s, c: (0, s, c + len(keep))),
            out_shape=whole,
            input_output_aliases={1: 0} if keep else {},
            compiler_params=LIMIT,
            name="join",
        )(received, *keep)

    return join(got_rest, rest, join(got_first, 1, None))


def solution(mesh):
    return jax.shard_map(
        per_device,
        mesh=mesh,
        in_specs=(
            P(None, None, "wall", "span"),
            P(),
            P(),
            P(None, "wall"),
            P("wall"),
            P("wall", "span", None, None),
        ),
        out_specs=P(("span", "wall"), None, None),
        check_vma=False,
    )
```

```python
import functools
import math

import jax
import jax.numpy as jnp
from jax import lax
from jax.experimental import pallas as pl
from jax.experimental.pallas import tpu as pltpu
from jax.sharding import PartitionSpec as P

HALO = 24
EDGE = 4
LANES = 128
FACTORS = 7
F32 = jnp.float32
BF16 = jnp.bfloat16
VMEM = pl.BlockSpec(memory_space=pltpu.VMEM)
SMEM = pl.BlockSpec(memory_space=pltpu.SMEM)
ROWS_BY_ROWS = (((1,), (1,)), ((), ()))
LIMIT = pltpu.CompilerParams(vmem_limit_bytes=40 * 1024 * 1024)


def iota(shape, dim):
    return lax.broadcasted_iota(jnp.int32, shape, dim)


def split(x):
    high = x.astype(BF16)
    return high, (x - high.astype(F32)).astype(BF16)


def tap_values(scale, distance, valid):
    scale = jnp.full((1, 1), scale, F32)
    k = iota((1, LANES), 1) - HALO
    squares = jnp.where(k <= HALO, jnp.exp(-math.pi * (k * k).astype(F32) / (scale * scale)), 0.0)
    norm = jnp.sqrt(jnp.sum(squares, axis=1, keepdims=True))
    d = distance.astype(F32)
    raw = jnp.exp(-math.pi * (d * d) / (2.0 * scale * scale))
    inside = valid & (distance >= -HALO) & (distance <= HALO)
    return jnp.where(inside, raw, 0.0) / norm


def tail_rows(count):
    return -(-(2 * count + 3 * FACTORS) // 16) * 16


def cell_row(i, faces):
    return (i % faces) * (EDGE * EDGE) + (i // (faces * EDGE)) * EDGE + (i // faces) % EDGE


def taps_kernel(wall_scale, span_scale, wall_first, wall_rest, span_first, span_rest):
    full = wall_first.shape[2]
    cols = span_first.shape[3] // 2
    i = iota((full, full), 0)
    y = cell_row(i, full // (EDGE * EDGE))
    k = iota((2 * cols, cols), 0)
    q = k - cols
    side, odd, r = q // (2 * HALO), (q // HALO) % 2, q % HALO
    z = jnp.where(q < 0, k, jnp.where(side == 0, r - HALO, cols + r))
    n = iota((2 * cols, cols), 1)
    target = (n % (cols // EDGE)) * EDGE + n // (cols // EDGE)
    for c in range(wall_first.shape[0] + wall_rest.shape[0]):
        wall_ref, span_ref, at = (wall_first, span_first, 0) if c == 0 else (wall_rest, span_rest, c - 1)
        high, low = split(tap_values(wall_scale[c], iota((full, full), 1) - y, i >= 0))
        wall_ref[at, :full] = high
        wall_ref[at, full:] = low
        for parity in range(2):
            valid = (q < 0) | ((q < 4 * HALO) & (odd == parity))
            high, low = split(tap_values(span_scale[c], z - target, valid))
            span_ref[at, parity] = jnp.concatenate([high, low], axis=1)


def pack_kernel(devices, noise_ref, lund_ref, mean_ref, owner_ref, out_ref):
    walls, height, cols = out_ref.shape
    planes = noise_ref.shape[1] // walls
    rows = noise_ref.shape[2]
    for w in range(walls):
        for t in range(planes):
            out_ref[w, t * rows : (t + 1) * rows] = noise_ref[0, w * planes + t]
    owner = owner_ref[...]
    elements = owner.shape[1]
    mine = jnp.where(iota((devices, elements), 0) == owner, 1.0, 0.0)
    before = jnp.where(iota((elements, elements), 0) < iota((elements, elements), 1), 1.0, 0.0)
    count = jnp.dot(mine.astype(BF16), before.astype(BF16), preferred_element_type=F32)
    rank = jnp.sum(mine * count, axis=0, keepdims=True)
    pieces = [owner.astype(F32), rank]
    pieces = [p[:, at : at + cols] for p in pieces for at in range(0, elements, cols)]
    factor = jnp.concatenate([lund_ref[...], mean_ref[...]], axis=0)
    factor = jnp.concatenate([factor, jnp.zeros((FACTORS, cols - rows), F32)], axis=1)
    for _ in range(3):
        part = factor.astype(BF16).astype(F32)
        pieces.append(part)
        factor = factor - part
    tail = height - planes * rows
    pieces.append(jnp.zeros((tail - sum(p.shape[0] for p in pieces), cols), F32))
    small = jnp.concatenate(pieces, axis=0).astype(BF16)
    for w in range(walls):
        out_ref[w, planes * rows :] = small


def small_kernel(slots, in_ref, factor_ref, target_ref):
    walls, height, cols = in_ref.shape
    full = factor_ref.shape[0]
    rows = full // walls
    count = target_ref.shape[1]
    tail = tail_rows(count)
    columns = jnp.zeros((full, tail), F32)
    y = cell_row(iota((full, cols), 0), full // (EDGE * EDGE))
    for w in range(walls):
        small = in_ref[w, height - tail :]
        pick = jnp.where(y == iota((full, cols), 1) + w * rows, 1.0, 0.0)
        pick = jnp.where(iota((full, cols), 1) < rows, pick, 0.0).astype(BF16)
        columns = columns + lax.dot_general(pick, small, ROWS_BY_ROWS, preferred_element_type=F32)
        numbers = small.astype(F32)
        target = numbers[:count] * slots + numbers[count : 2 * count]
        target_ref[w] = target.astype(jnp.int32)
    at = 2 * count
    factor = sum(columns[:, at + p * FACTORS : at + (p + 1) * FACTORS] for p in range(3))
    factor_ref[...] = jnp.concatenate([factor, jnp.zeros((full, cols - FACTORS), F32)], axis=1)


def plane_of(noise_ref, c, t, rows):
    walls = noise_ref.shape[0]
    return jnp.concatenate(
        [noise_ref[w, c, t * rows : (t + 1) * rows] for w in range(walls)], axis=0
    )


def edge_picker(cols):
    wide = 2 * HALO
    row, col = iota((wide, cols), 0), iota((wide, cols), 1)
    return jnp.where(col == jnp.where(row < HALO, row, cols - wide + row), 1.0, 0.0).astype(BF16)


def edges_kernel(planes, noise_ref, low_ref, high_ref):
    walls, _, cols = noise_ref.shape
    rows = low_ref.shape[1] // walls
    wide = 2 * HALO
    pick = edge_picker(cols)
    for pair in range(planes // 2):
        edges = []
        for t in (2 * pair, 2 * pair + 1):
            plane = [noise_ref[w, t * rows : (t + 1) * rows] for w in range(walls)]
            plane = jnp.concatenate(plane, axis=0)
            edges.append(lax.dot_general(pick, plane, ROWS_BY_ROWS, preferred_element_type=F32))
        at = pl.ds(pair * wide, wide)
        low_ref[at] = jnp.concatenate([e[:HALO] for e in edges], axis=0).astype(BF16)
        high_ref[at] = jnp.concatenate([e[HALO:] for e in edges], axis=0).astype(BF16)


def raw_edges_kernel(noise_ref, low_ref, high_ref):
    _, all_planes, rows, cols = noise_ref.shape
    walls = low_ref.shape[0]
    pairs = all_planes // walls // 2
    pick = edge_picker(cols)
    for w in range(walls):
        edges = []
        for pair in range(pairs):
            t = 2 * (w * pairs + pair)
            plane = jnp.concatenate([noise_ref[0, t], noise_ref[0, t + 1]], axis=0)
            edges.append(lax.dot_general(pick, plane, ROWS_BY_ROWS, preferred_element_type=F32))
        low_ref[w] = jnp.concatenate([e[:HALO] for e in edges], axis=0).astype(BF16)
        high_ref[w] = jnp.concatenate([e[HALO:] for e in edges], axis=0).astype(BF16)


def swap_blocks(blocks, cols):
    part = cols // EDGE
    lane = iota(blocks[0].shape, 1)
    for step in (2, 1):
        first = (lane // (part * step)) % 2 == 0
        out = list(blocks)
        for a in range(EDGE):
            if a & step:
                continue
            one, two = blocks[a], blocks[a + step]
            out[a] = jnp.where(first, one, pltpu.roll(two, part * step, 1))
            out[a + step] = jnp.where(first, pltpu.roll(one, cols - part * step, 1), two)
        blocks = out
    return blocks


def halo_tiles(parts, cols):
    half = cols // 2
    sides = []
    for side in parts:
        planes = [[], []]
        for one, two in zip(side[::2], side[1::2]):
            lower = iota(one.shape, 1) < half
            planes[0].append(jnp.where(lower, one, pltpu.roll(two, half, 1)))
            planes[1].append(jnp.where(lower, pltpu.roll(one, half, 1), two))
        sides.append([jnp.concatenate(p, axis=1) for p in planes])
    pairs = sides[0][0].shape[0] // HALO
    zeros = jnp.zeros((cols - 4 * HALO, sides[0][0].shape[1]), F32)
    for pair in range(pairs):
        at = slice(pair * HALO, (pair + 1) * HALO)
        tile = [sides[s][odd][at] for s in range(2) for odd in range(2)]
        yield jnp.concatenate(tile + [zeros], axis=0).astype(BF16)


def filter_kernel(count, planes, noise_ref, low_ref, high_ref, factor_ref, target_ref, *rest):
    taps, (out_ref, cells_ref, halo_ref, wide_ref) = rest[:-4], rest[-4:]
    if count > 1:
        others_ref, taps = taps[0], taps[1:]
    wall_of = lambda c: taps[0][0] if c == 0 else taps[2][c - 1]
    span_of = lambda c, odd: taps[1][0, odd] if c == 0 else taps[3][c - 1, odd]
    kept = range(count) if count == 1 else range(1, count)
    walls, _, cols = noise_ref.shape
    full = low_ref.shape[1]
    rows = full // walls
    faces = full // (EDGE * EDGE)
    tile_faces = faces // walls
    devices, _, slots, _ = out_ref.shape
    values = planes * EDGE * EDGE
    wide = 2 * HALO
    pairs = planes // 2

    for f in range(FACTORS):
        wide_ref[f] = jnp.broadcast_to(factor_ref[:, f : f + 1], (full, cols))
    for pair in range(pairs):
        at = pl.ds(pair * wide, wide)
        halo_ref[pair, :wide] = low_ref[at]
        halo_ref[pair, wide : 2 * wide] = high_ref[at]
        halo_ref[pair, 2 * wide :] = jnp.zeros((cols - 2 * wide, full), BF16)
    for c in range(1, count):
        height = pairs * HALO
        start = (count - 1) * planes * rows
        parts = [
            [
                others_ref[w, pl.ds(start + (side * (count - 1) + c - 1) * height, height)].astype(F32)
                for w in range(walls)
            ]
            for side in range(2)
        ]
        for pair, tile in enumerate(halo_tiles(parts, cols)):
            halo_ref[c * pairs + pair] = tile

    def plane(c, t):
        ref, start = (noise_ref, 0) if c == 0 else (others_ref, (c - 1) * planes * rows)
        at = pl.ds(pl.multiple_of(start + t * rows, rows), rows)
        return jnp.concatenate([ref[w, at] for w in range(walls)], axis=0)

    def pair_step(pair, carry):
        psi = [[], []]
        for c in range(count):
            both = jnp.concatenate([plane(c, 2 * pair), plane(c, 2 * pair + 1)], axis=1)
            smooth = jnp.dot(wall_of(c), both, preferred_element_type=F32)
            smooth = smooth[:full] + smooth[full:]
            halo = halo_ref[c * pairs + pair]
            beside = lax.dot_general(wall_of(c), halo, ROWS_BY_ROWS, preferred_element_type=F32)
            beside = beside[:full] + beside[full:]
            for odd in range(2):
                high, low = split(
                    jnp.concatenate([smooth[:, odd * cols : (odd + 1) * cols], beside], axis=1)
                )
                matrix = span_of(c, odd)
                broad = jnp.dot(high, matrix, preferred_element_type=F32)
                small = jnp.dot(low, matrix[:, :cols], preferred_element_type=F32)
                psi[odd].append(broad[:, :cols] + (broad[:, cols:] + small))
        for odd in range(2):
            t = 2 * pair + odd
            p = psi[odd]
            if count == 1:
                velocity = (wide_ref[6] + wide_ref[0] * p[0],)
            else:
                velocity = (
                    wide_ref[1] * p[0] + wide_ref[2] * p[1],
                    wide_ref[3] * p[0] + wide_ref[4] * p[1] + wide_ref[5] * p[2],
                )
            quarter = full // EDGE
            for at, value in enumerate(velocity):
                blocks = [value[a * quarter : (a + 1) * quarter] for a in range(EDGE)]
                for dz, block in enumerate(swap_blocks(blocks, cols)):
                    for dy in range(EDGE):
                        j = t * EDGE * EDGE + dy * EDGE + dz
                        cells_ref[at, pl.ds(j, faces, stride=values), :] = block[dy * faces : (dy + 1) * faces]
        return carry

    lax.fori_loop(0, pairs, pair_step, 0)

    for w in range(walls):
        payload = [
            [
                cells_ref[at, pl.ds((w * tile_faces + f) * values, values), :].astype(BF16)
                for f in range(tile_faces)
            ]
            for at in range(len(kept))
        ]
        payload = jnp.concatenate([jnp.concatenate(p, axis=1) for p in payload], axis=0)
        slot = iota((devices * slots, cols), 0)
        onehot = [
            jnp.where(slot == target_ref[w, f : f + 1], 1.0, 0.0).astype(BF16)
            for f in range(tile_faces)
        ]
        onehot = jnp.concatenate(onehot, axis=1)
        sent = lax.dot_general(onehot, payload, ROWS_BY_ROWS, preferred_element_type=F32)
        out_ref[:, w] = sent.astype(BF16).reshape(devices, slots, len(kept) * values)


def join_kernel(first, some, walls, in_ref, *rest):
    out_ref, sems = rest[-2:]
    devices, height, width = in_ref.shape
    values = width // some
    copies = []
    for c in range(some):
        for s in range(devices // walls):
            for w in range(walls):
                copies.append(
                    pltpu.make_async_copy(
                        in_ref.at[s * walls + w, :, pl.ds(c * values, values)],
                        out_ref.at[0, pl.ds(s * height, height), pl.ds(((c + first) * walls + w) * values, values)],
                        sems.at[c, s * walls + w],
                    )
                )
    for copy in copies:
        copy.start()
    for copy in copies:
        copy.wait()


def join_narrow_kernel(some, in_ref, *rest):
    out_ref = rest[-1]
    walls, _, width = in_ref.shape
    values = width // some
    for c in range(some):

        @pl.when(pl.program_id(1) == c)
        def _():
            for w in range(walls):
                out_ref[0, :, w * values : (w + 1) * values] = in_ref[w, :, c * values : (c + 1) * values]


def per_device(noise, wall_scale, span_scale, lund_factor, mean_velocity, owner_map):
    trio, all_planes, rows, cols = noise.shape
    n_span = lax.axis_size("span")
    n_wall = lax.axis_size("wall")
    devices = n_span * n_wall
    planes = all_planes // n_wall
    pairs = planes // 2
    full = rows * n_wall
    faces = full // (EDGE * EDGE)
    values = planes * EDGE * EDGE
    owners = owner_map.reshape(1, -1)
    elements = owners.shape[1]
    slots = max(8, 2 * elements // devices)
    count = elements // cols
    rest = trio - 1
    struct = jax.ShapeDtypeStruct
    hbm = pltpu.MemorySpace.HBM

    def call(kernel, ins, outs, name, limit, scratch=(), grid=(), out_specs=None):
        specs = out_specs or [VMEM] * len(outs)
        return pl.pallas_call(
            kernel,
            grid=grid,
            in_specs=ins,
            out_specs=specs if len(outs) > 1 else specs[0],
            out_shape=outs if len(outs) > 1 else outs[0],
            scratch_shapes=scratch,
            compiler_params=pltpu.CompilerParams(vmem_limit_bytes=limit * 1024 * 1024),
            name=name,
        )

    up = [(i, (i + 1) % n_span) for i in range(n_span)]
    down = [(b, a) for a, b in up]

    def swap(x):
        return lax.all_to_all(x, "wall", 0, 0, tiled=True)

    def send(x):
        return lax.all_to_all(x, ("span", "wall"), 0, 0, tiled=True).reshape(devices, n_wall * slots, -1)

    packed = call(
        functools.partial(pack_kernel, devices),
        [pl.BlockSpec((1, all_planes, rows, cols), lambda i: (0, 0, 0, 0)), VMEM, VMEM, VMEM],
        [hbm((n_wall, planes * rows + tail_rows(count), cols), BF16)],
        "pack",
        56,
        grid=(1,),
    )(noise, lund_factor, mean_velocity.reshape(1, rows), owners)
    packed = swap(packed)

    height = pairs * HALO
    edge = hbm((n_wall, rest * height, cols), BF16)
    spec = pl.BlockSpec((n_wall, height, cols), lambda c: (0, c, 0))
    first, last = call(
        raw_edges_kernel,
        [pl.BlockSpec((1, all_planes, rows, cols), lambda c: (c + 1, 0, 0, 0))],
        [edge, edge],
        "edges_rest",
        56,
        grid=(rest,),
        out_specs=[spec, spec],
    )(noise)
    others = noise[1:].reshape(rest, n_wall, planes * rows, cols).transpose(1, 0, 2, 3)
    others = others.reshape(n_wall, rest * planes * rows, cols)
    low, high = lax.ppermute(last, "span", up), lax.ppermute(first, "span", down)
    others = swap(jnp.concatenate([others, low, high], axis=1))

    wall_first, wall_rest, span_first, span_rest = call(
        taps_kernel,
        [SMEM, SMEM],
        [
            struct((1, 2 * full, full), BF16),
            struct((rest, 2 * full, full), BF16),
            struct((1, 2, 2 * cols, 2 * cols), BF16),
            struct((rest, 2, 2 * cols, 2 * cols), BF16),
        ],
        "taps",
        16,
    )(wall_scale, span_scale)
    factor, target = call(
        functools.partial(small_kernel, slots),
        [VMEM],
        [struct((full, cols), F32), struct((n_wall, count, cols), jnp.int32)],
        "small",
        16,
    )(packed)

    edge = struct((planes * HALO, full), BF16)
    first, last = call(
        functools.partial(edges_kernel, planes), [VMEM], [edge, edge], "edges_first", 16
    )(packed)
    low, high = lax.ppermute(last, "span", up), lax.ppermute(first, "span", down)

    def filtered(n, some, extra, name):
        return call(
            functools.partial(filter_kernel, n, planes),
            [VMEM] * (5 + len(extra)),
            [hbm((devices, n_wall, slots, some * values), BF16)],
            name,
            32,
            [
                pltpu.VMEM((some, faces * values, cols), F32),
                pltpu.VMEM((n * pairs, cols, full), BF16),
                pltpu.VMEM((FACTORS, full, cols), F32),
            ],
        )(packed, low, high, factor, target, *extra)

    got_first = send(filtered(1, 1, (wall_first, span_first), "filter_first"))
    got_rest = send(
        filtered(trio, rest, (others, wall_first, span_first, wall_rest, span_rest), "filter_rest")
    )

    whole = hbm((1, devices * slots, trio * values * n_wall), BF16)
    block = (1, n_wall * slots, values * n_wall)

    def join(received, some, before):
        keep = [] if before is None else [before]
        anywhere = pl.BlockSpec(memory_space=pl.ANY)
        narrow = values % LANES != 0
        return pl.pallas_call(
            functools.partial(join_narrow_kernel, some)
            if narrow
            else functools.partial(join_kernel, len(keep), some, n_wall),
            grid=(n_span, some) if narrow else (),
            in_specs=[
                pl.BlockSpec((n_wall, n_wall * slots, some * values), lambda s, c: (s, 0, 0)) if narrow else anywhere
            ]
            + [anywhere] * len(keep),
            out_specs=pl.BlockSpec(block, lambda s, c: (0, s, c + len(keep))) if narrow else anywhere,
            out_shape=whole,
            scratch_shapes=[] if narrow else [pltpu.SemaphoreType.DMA((some, devices))],
            input_output_aliases={1: 0} if keep else {},
            compiler_params=pltpu.CompilerParams(vmem_limit_bytes=16 * 1024 * 1024),
            name="join",
        )(received, *keep)

    return join(got_rest, rest, join(got_first, 1, None))


def solution(mesh):
    return jax.shard_map(
        per_device,
        mesh=mesh,
        in_specs=(
            P(None, None, "wall", "span"),
            P(),
            P(),
            P(None, "wall"),
            P("wall"),
            P("wall", "span", None, None),
        ),
        out_specs=P(("span", "wall"), None, None),
        check_vma=False,
    )
```

```python
import functools
import math

import jax
import jax.numpy as jnp
from jax import lax
from jax.experimental import pallas as pl
from jax.experimental.pallas import tpu as pltpu
from jax.sharding import PartitionSpec as P

HALO = 24
EDGE = 4
LANES = 128
FACTORS = 7
F32 = jnp.float32
BF16 = jnp.bfloat16
VMEM = pl.BlockSpec(memory_space=pltpu.VMEM)
ANYWHERE = pl.BlockSpec(memory_space=pl.ANY)
SMEM = pl.BlockSpec(memory_space=pltpu.SMEM)
ROWS_BY_ROWS = (((1,), (1,)), ((), ()))


def iota(shape, dim):
    return lax.broadcasted_iota(jnp.int32, shape, dim)


def split(x):
    high = x.astype(BF16)
    return high, (x - high.astype(F32)).astype(BF16)


def tap_values(scale, distance, valid):
    scale = jnp.full((1, 1), scale, F32)
    k = iota((1, LANES), 1) - HALO
    squares = jnp.where(k <= HALO, jnp.exp(-math.pi * (k * k).astype(F32) / (scale * scale)), 0.0)
    norm = jnp.sqrt(jnp.sum(squares, axis=1, keepdims=True))
    d = distance.astype(F32)
    raw = jnp.exp(-math.pi * (d * d) / (2.0 * scale * scale))
    inside = valid & (distance >= -HALO) & (distance <= HALO)
    return jnp.where(inside, raw, 0.0) / norm


def tail_rows(count):
    return -(-(2 * count + 3 * FACTORS) // 16) * 16


def cell_row(i, faces):
    return (i % faces) * (EDGE * EDGE) + (i // (faces * EDGE)) * EDGE + (i // faces) % EDGE


def taps_kernel(first, wall_scale, span_scale, wall_ref, main_ref, halo_ref):
    some, full, _ = wall_ref.shape
    cols = main_ref.shape[1] // 2
    walls = lax.axis_size("wall")
    rows = full // walls
    i, j = iota((full, full), 0), iota((full, full), 1)
    y = cell_row(i, full // (EDGE * EDGE))
    source = lax.rem(lax.axis_index("wall") + walls - j // rows, walls)
    column = source * rows + j % rows if first else j
    n = iota((cols, cols), 1)
    target = (n % (cols // EDGE)) * EDGE + n // (cols // EDGE)
    k = iota((cols, cols), 0)
    side, odd, r = k // (2 * HALO), (k // HALO) % 2, k % HALO
    z = jnp.where(side == 0, r - HALO, cols + r)

    def span_matrix(scale, distance, valid):
        high, low = split(tap_values(scale, distance, valid))
        top = jnp.concatenate([high, low], axis=1)
        return jnp.concatenate([top, jnp.concatenate([high, jnp.zeros_like(high)], axis=1)], axis=0)

    for c in range(some):
        high, low = split(tap_values(wall_scale[first + c], column - y, i >= 0))
        wall_ref[c, :, :full] = high
        wall_ref[c, :, full:] = low
        scale = span_scale[first + c]
        main_ref[c] = span_matrix(scale, k - target, k >= 0)
        for parity in range(2):
            valid = (k < 4 * HALO) & (odd == parity)
            halo_ref[c, parity] = span_matrix(scale, z - target, valid)


def run(copies):
    for copy in copies:
        copy.start()
    for copy in copies:
        copy.wait()


def pack_kernel(devices, noise_ref, lund_ref, mean_ref, owner_ref, out_ref, small_ref, noise_sems, small_sems):
    walls, height, cols = out_ref.shape
    tail = small_ref.shape[0]
    block = height - tail
    rows = mean_ref.shape[1]
    copies = [
        pltpu.make_async_copy(
            noise_ref.at[0, pl.ds(w * block, block)], out_ref.at[w, pl.ds(0, block)], noise_sems.at[w]
        )
        for w in range(walls)
    ]
    for copy in copies:
        copy.start()
    owner = owner_ref[...]
    elements = owner.shape[1]
    mine = jnp.where(iota((devices, elements), 0) == owner, 1.0, 0.0)
    before = jnp.where(iota((elements, elements), 0) < iota((elements, elements), 1), 1.0, 0.0)
    count = jnp.dot(mine.astype(BF16), before.astype(BF16), preferred_element_type=F32)
    rank = jnp.sum(mine * count, axis=0, keepdims=True)
    pieces = [owner.astype(F32), rank]
    pieces = [p[:, at : at + cols] for p in pieces for at in range(0, elements, cols)]
    factor = jnp.concatenate([lund_ref[...], mean_ref[...]], axis=0)
    factor = jnp.concatenate([factor, jnp.zeros((FACTORS, cols - rows), F32)], axis=1)
    for _ in range(3):
        part = factor.astype(BF16).astype(F32)
        pieces.append(part)
        factor = factor - part
    pieces.append(jnp.zeros((tail - sum(p.shape[0] for p in pieces), cols), F32))
    small_ref[...] = jnp.concatenate(pieces, axis=0).astype(BF16)
    run(
        [
            pltpu.make_async_copy(small_ref, out_ref.at[w, pl.ds(block, tail)], small_sems.at[w])
            for w in range(walls)
        ]
    )
    for copy in copies:
        copy.wait()


def pack_planes_kernel(noise_ref, *rest):
    out_refs, sems = rest[:-1], rest[-1]
    walls = len(out_refs)
    block = noise_ref.shape[1] // walls
    me = lax.axis_index("wall")
    copies = []
    for step, out_ref in enumerate(out_refs):
        start = pl.multiple_of(lax.rem(me + step, walls) * block, block)
        copies.append(pltpu.make_async_copy(noise_ref.at[0, pl.ds(start, block)], out_ref, sems.at[step]))
    run(copies)


def pack_late_kernel(noise_ref, low_ref, high_ref, *rest):
    out_refs, sems = rest[:-1], rest[-1]
    walls, some, height, _ = low_ref.shape
    block = noise_ref.shape[1] // walls
    me = lax.axis_index("wall")
    copies = []
    for step, out_ref in enumerate(out_refs):
        to = lax.rem(me + step, walls)
        parts = [(noise_ref.at[0, pl.ds(pl.multiple_of(to * block, block), block)], 0, block)]
        for side, ref in enumerate((low_ref, high_ref)):
            for c in range(some):
                parts.append((ref.at[to, c], block + (side * some + c) * height, height))
        for part, (ref, start, size) in enumerate(parts):
            copies.append(
                pltpu.make_async_copy(ref, out_ref.at[pl.ds(start, size)], sems.at[step, part])
            )
    run(copies)


def small_kernel(slots, in_ref, factor_ref, target_ref):
    walls, height, cols = in_ref.shape
    full = factor_ref.shape[0]
    rows = full // walls
    count = target_ref.shape[1]
    tail = tail_rows(count)
    columns = jnp.zeros((full, tail), F32)
    y = cell_row(iota((full, cols), 0), full // (EDGE * EDGE))
    for w in range(walls):
        small = in_ref[w, height - tail :]
        pick = jnp.where(y == iota((full, cols), 1) + w * rows, 1.0, 0.0)
        pick = jnp.where(iota((full, cols), 1) < rows, pick, 0.0).astype(BF16)
        columns = columns + lax.dot_general(pick, small, ROWS_BY_ROWS, preferred_element_type=F32)
        numbers = small.astype(F32)
        target = numbers[:count] * slots + numbers[count : 2 * count]
        target_ref[w] = target.astype(jnp.int32)
    at = 2 * count
    factor = sum(columns[:, at + p * FACTORS : at + (p + 1) * FACTORS] for p in range(3))
    factor_ref[...] = jnp.concatenate([factor, jnp.zeros((full, cols - FACTORS), F32)], axis=1)


def edge_picker(cols):
    wide = 2 * HALO
    row, col = iota((wide, cols), 0), iota((wide, cols), 1)
    return jnp.where(col == jnp.where(row < HALO, row, cols - wide + row), 1.0, 0.0).astype(BF16)


def edges_kernel(planes, noise_ref, low_ref, high_ref):
    walls, _, cols = noise_ref.shape
    rows = low_ref.shape[1] // walls
    wide = 2 * HALO
    pick = edge_picker(cols)
    for pair in range(planes // 2):
        edges = []
        for t in (2 * pair, 2 * pair + 1):
            plane = [noise_ref[w, t * rows : (t + 1) * rows] for w in range(walls)]
            plane = jnp.concatenate(plane, axis=0)
            edges.append(lax.dot_general(pick, plane, ROWS_BY_ROWS, preferred_element_type=F32))
        at = pl.ds(pair * wide, wide)
        low_ref[at] = jnp.concatenate([e[:HALO] for e in edges], axis=0).astype(BF16)
        high_ref[at] = jnp.concatenate([e[HALO:] for e in edges], axis=0).astype(BF16)


def raw_edges_kernel(noise_ref, low_ref, high_ref):
    walls, _, height, cols = low_ref.shape
    pairs = height // HALO
    pick = edge_picker(cols)
    for w in range(walls):
        edges = []
        for pair in range(pairs):
            plane = noise_ref[0, (w * pairs + pair) * cols : (w * pairs + pair + 1) * cols]
            edges.append(lax.dot_general(pick, plane, ROWS_BY_ROWS, preferred_element_type=F32))
        low_ref[w, 0] = jnp.concatenate([e[:HALO] for e in edges], axis=0).astype(BF16)
        high_ref[w, 0] = jnp.concatenate([e[HALO:] for e in edges], axis=0).astype(BF16)


def swap_blocks(blocks, cols):
    part = cols // EDGE
    lane = iota(blocks[0].shape, 1)
    for step in (2, 1):
        first = (lane // (part * step)) % 2 == 0
        out = list(blocks)
        for a in range(EDGE):
            if a & step:
                continue
            one, two = blocks[a], blocks[a + step]
            out[a] = jnp.where(first, one, pltpu.roll(two, part * step, 1))
            out[a + step] = jnp.where(first, pltpu.roll(one, cols - part * step, 1), two)
        blocks = out
    return blocks


def halo_tiles(parts, cols):
    half = cols // 2
    sides = []
    for side in parts:
        planes = [[], []]
        for one, two in zip(side[::2], side[1::2]):
            lower = iota(one.shape, 1) < half
            planes[0].append(jnp.where(lower, one, pltpu.roll(two, half, 1)))
            planes[1].append(jnp.where(lower, pltpu.roll(one, half, 1), two))
        sides.append([jnp.concatenate(p, axis=1) for p in planes])
    pairs = sides[0][0].shape[0] // HALO
    zeros = jnp.zeros((cols - 4 * HALO, sides[0][0].shape[1]), F32)
    for pair in range(pairs):
        at = slice(pair * HALO, (pair + 1) * HALO)
        tile = [sides[s][odd][at] for s in range(2) for odd in range(2)]
        yield jnp.concatenate(tile + [zeros], axis=0).astype(BF16)


def span_product(x, matrix):
    cols = x.shape[1]
    both = jnp.dot(jnp.concatenate(split(x), axis=1), matrix, preferred_element_type=F32)
    return both[:, :cols] + both[:, cols:]


def main_part(planes, wall, matrix):
    both = jnp.concatenate(planes, axis=1)
    cols = planes[0].shape[1]
    smooth = jnp.dot(wall, jnp.concatenate([both, both], axis=0), preferred_element_type=F32)
    return [span_product(smooth[:, odd * cols : (odd + 1) * cols], matrix) for odd in range(2)]


def halo_part(tile, wall, halo_ref):
    smooth = lax.dot_general(
        wall, jnp.concatenate([tile, tile], axis=1), ROWS_BY_ROWS, preferred_element_type=F32
    )
    return [span_product(smooth, halo_ref[odd]) for odd in range(2)]


def main_kernel(planes, noise_ref, wall_ref, main_ref, psi_ref):
    walls = noise_ref.shape[0]
    rows = psi_ref.shape[1] // walls

    def pair_step(pair, carry):
        pair_planes = []
        for odd in range(2):
            at = pl.ds(pl.multiple_of((2 * pair + odd) * rows, rows), rows)
            pair_planes.append(jnp.concatenate([noise_ref[w, at] for w in range(walls)], axis=0))
        for odd, psi in enumerate(main_part(pair_planes, wall_ref[0], main_ref[0])):
            psi_ref[2 * pair + odd] = psi
        return carry

    lax.fori_loop(0, planes // 2, pair_step, 0, unroll=True)


def widen(factor_ref, wide_ref, which):
    for f in which:
        wide_ref[f] = jnp.broadcast_to(factor_ref[:, f : f + 1], wide_ref.shape[1:])


def place_cells(velocity, t, cells_ref, at):
    full, cols = velocity.shape
    quarter, faces = full // EDGE, full // (EDGE * EDGE)
    values = cells_ref.shape[1] // faces
    blocks = [velocity[a * quarter : (a + 1) * quarter] for a in range(EDGE)]
    for dz, block in enumerate(swap_blocks(blocks, cols)):
        for dy in range(EDGE):
            j = t * EDGE * EDGE + dy * EDGE + dz
            cells_ref[at, pl.ds(j, faces, stride=values), :] = block[dy * faces : (dy + 1) * faces]


def scatter_cells(cells_ref, target_ref, sent_ref, out_ref, sems):
    walls, tile_faces, cols = target_ref.shape
    some = cells_ref.shape[0]
    values = cells_ref.shape[1] // (walls * tile_faces)
    _, devices, slots, width = sent_ref.shape
    copies = []
    for w in range(walls):
        payload = [
            [
                cells_ref[at, pl.ds((w * tile_faces + f) * values, values), :].astype(BF16)
                for f in range(tile_faces)
            ]
            for at in range(some)
        ]
        payload = jnp.concatenate([jnp.concatenate(p, axis=1) for p in payload], axis=0)
        slot = iota((devices * slots, cols), 0)
        onehot = [
            jnp.where(slot == target_ref[w, f : f + 1], 1.0, 0.0).astype(BF16)
            for f in range(tile_faces)
        ]
        onehot = jnp.concatenate(onehot, axis=1)
        sent = lax.dot_general(onehot, payload, ROWS_BY_ROWS, preferred_element_type=F32)
        sent_ref[w] = sent.astype(BF16).reshape(devices, slots, width)
        copies.append(pltpu.make_async_copy(sent_ref.at[w], out_ref.at[:, w], sems.at[w]))
        copies[-1].start()
    for copy in copies:
        copy.wait()


def first_kernel(
    planes, psi_in, low_ref, high_ref, factor_ref, target_ref, wall_ref, halo_ref,
    out_ref, psi_out, psi_ref, cells_ref, wide_ref, sent_ref, sems, psi_sem,
):
    full, cols = psi_ref.shape[1:]
    wide = 2 * HALO
    widen(factor_ref, wide_ref, (0, 6))

    def pair_step(pair, carry):
        at = pl.ds(pl.multiple_of(pair * wide, wide), wide)
        tile = [low_ref[at], high_ref[at], jnp.zeros((cols - 2 * wide, full), BF16)]
        beside = halo_part(jnp.concatenate(tile, axis=0), wall_ref[0], halo_ref.at[0])
        for odd in range(2):
            t = 2 * pair + odd
            psi = psi_in[t] + beside[odd]
            psi_ref[t] = psi
            place_cells(wide_ref[6] + wide_ref[0] * psi, t, cells_ref, 0)
        return carry

    lax.fori_loop(0, planes // 2, pair_step, 0, unroll=True)
    copy = pltpu.make_async_copy(psi_ref, psi_out, psi_sem.at[0])
    copy.start()
    scatter_cells(cells_ref, target_ref, sent_ref, out_ref, sems)
    copy.wait()


def rest_kernel(
    planes, psi_ref, factor_ref, target_ref, wall_ref, main_ref, halo_ref, *rest,
):
    *in_refs, out_ref, cells_ref, tile_ref, wide_ref, sent_ref, sems = rest
    early_refs, late_refs = in_refs[: len(in_refs) // 2], in_refs[len(in_refs) // 2 :]
    full, cols = psi_ref.shape[1:]
    some = wall_ref.shape[0]
    rows = full // len(early_refs)
    pairs = planes // 2
    height = pairs * HALO
    widen(factor_ref, wide_ref, range(1, 6))
    for c in range(some):
        starts = [planes * rows + (side * some + c) * height for side in range(2)]
        parts = [[ref[pl.ds(at, height)].astype(F32) for ref in late_refs] for at in starts]
        for pair, tile in enumerate(halo_tiles(parts, cols)):
            tile_ref[c * pairs + pair] = tile

    def pair_step(pair, carry):
        psi = []
        for c in range(some):
            pair_planes = []
            for odd in range(2):
                at = pl.ds(pl.multiple_of((2 * pair + odd) * rows, rows), rows)
                pair_planes.append(jnp.concatenate([ref[at] for ref in (early_refs, late_refs)[c]], axis=0))
            main = main_part(pair_planes, wall_ref[c], main_ref[c])
            beside = halo_part(tile_ref[c * pairs + pair], wall_ref[c], halo_ref.at[c])
            psi.append([m + b for m, b in zip(main, beside)])
        for odd in range(2):
            t = 2 * pair + odd
            p, q, r = psi_ref[t], psi[0][odd], psi[1][odd]
            place_cells(wide_ref[1] * p + wide_ref[2] * q, t, cells_ref, 0)
            place_cells(wide_ref[3] * p + wide_ref[4] * q + wide_ref[5] * r, t, cells_ref, 1)
        return carry

    lax.fori_loop(0, pairs, pair_step, 0, unroll=True)
    scatter_cells(cells_ref, target_ref, sent_ref, out_ref, sems)


def join_kernel(first, some, walls, in_ref, *rest):
    out_ref, sems = rest[-2:]
    devices, height, width = in_ref.shape
    values = width // some
    copies = []
    for c in range(some):
        for s in range(devices // walls):
            for w in range(walls):
                copies.append(
                    pltpu.make_async_copy(
                        in_ref.at[s * walls + w, :, pl.ds(c * values, values)],
                        out_ref.at[0, pl.ds(s * height, height), pl.ds(((c + first) * walls + w) * values, values)],
                        sems.at[c, s * walls + w],
                    )
                )
    run(copies)


def join_narrow_kernel(some, in_ref, *rest):
    out_ref = rest[-1]
    walls, _, width = in_ref.shape
    values = width // some
    for c in range(some):

        @pl.when(pl.program_id(1) == c)
        def _():
            for w in range(walls):
                out_ref[0, :, w * values : (w + 1) * values] = in_ref[w, :, c * values : (c + 1) * values]


def per_device(noise, wall_scale, span_scale, lund_factor, mean_velocity, owner_map):
    trio, all_planes, rows, cols = noise.shape
    n_span = lax.axis_size("span")
    n_wall = lax.axis_size("wall")
    devices = n_span * n_wall
    planes = all_planes // n_wall
    pairs = planes // 2
    full = rows * n_wall
    faces = full // (EDGE * EDGE)
    values = planes * EDGE * EDGE
    owners = owner_map.reshape(1, -1)
    elements = owners.shape[1]
    slots = max(8, 2 * elements // devices)
    count = elements // cols
    rest = trio - 1
    struct = jax.ShapeDtypeStruct
    hbm = pltpu.MemorySpace.HBM

    def call(kernel, ins, outs, name, limit, scratch=(), grid=(), out_specs=None):
        specs = out_specs or [VMEM] * len(outs)
        return pl.pallas_call(
            kernel,
            grid=grid,
            in_specs=ins,
            out_specs=specs if len(outs) > 1 else specs[0],
            out_shape=outs if len(outs) > 1 else outs[0],
            scratch_shapes=scratch,
            compiler_params=pltpu.CompilerParams(vmem_limit_bytes=limit * 1024 * 1024),
            cost_estimate=pl.CostEstimate(flops=1024, bytes_accessed=1024, transcendentals=0),
            name=name,
        )

    up = [(i, (i + 1) % n_span) for i in range(n_span)]
    down = [(b, a) for a, b in up]

    def swap(x):
        return lax.all_to_all(x, "wall", 0, 0, tiled=True)

    def send(x):
        return lax.all_to_all(x, ("span", "wall"), 0, 0, tiled=True).reshape(devices, n_wall * slots, -1)

    dma = pltpu.SemaphoreType.DMA
    noise = noise.reshape(trio, all_planes * rows, cols)
    packed = call(
        functools.partial(pack_kernel, devices),
        [pl.BlockSpec((1, all_planes * rows, cols), lambda i: (0, 0, 0)), VMEM, VMEM, VMEM],
        [hbm((n_wall, planes * rows + tail_rows(count), cols), BF16)],
        "pack",
        56,
        [pltpu.VMEM((tail_rows(count), cols), BF16), dma((n_wall,)), dma((n_wall,))],
        grid=(1,),
        out_specs=[ANYWHERE],
    )(noise, lund_factor, mean_velocity.reshape(1, rows), owners)
    noise, packed = lax.optimization_barrier((noise, packed))
    packed = swap(packed)

    height = pairs * HALO
    edge = hbm((n_wall, rest, height, cols), BF16)
    spec = pl.BlockSpec((n_wall, 1, height, cols), lambda c: (0, c, 0, 0))
    first, last = call(
        raw_edges_kernel,
        [pl.BlockSpec((1, all_planes * rows, cols), lambda c: (c + 1, 0, 0))],
        [edge, edge],
        "edges_rest",
        56,
        grid=(rest,),
        out_specs=[spec, spec],
    )(noise)
    rest_low, rest_high = lax.ppermute(last, "span", up), lax.ppermute(first, "span", down)
    early = call(
        pack_planes_kernel,
        [pl.BlockSpec((1, all_planes * rows, cols), lambda i: (1, 0, 0))],
        [hbm((planes * rows, cols), BF16)] * n_wall,
        "pack_early",
        56,
        [dma((n_wall,))],
        grid=(1,),
        out_specs=[ANYWHERE] * n_wall,
    )(noise)
    packed, _ = lax.optimization_barrier((packed, (first, last, early)))

    def spread(blocks):
        return [blocks[0]] + [
            lax.ppermute(x, "wall", [(i, (i + step) % n_wall) for i in range(n_wall)])
            for step, x in enumerate(blocks[1:], 1)
        ]

    def taps(first, some, make, name):
        return call(
            functools.partial(taps_kernel, first),
            [SMEM, SMEM],
            [
                make((some, full, 2 * full), BF16),
                make((some, 2 * cols, 2 * cols), BF16),
                make((some, 2, 2 * cols, 2 * cols), BF16),
            ],
            name,
            16,
        )(wall_scale, span_scale)

    wall_first, main_first, halo_first = taps(0, 1, struct, "taps_first")
    factor, target = call(
        functools.partial(small_kernel, slots),
        [VMEM],
        [struct((full, cols), F32), struct((n_wall, count, cols), jnp.int32)],
        "small",
        16,
    )(packed)

    edge = struct((planes * HALO, full), BF16)
    first, last = call(
        functools.partial(edges_kernel, planes), [VMEM], [edge, edge], "edges_first", 16
    )(packed)
    low, high = lax.ppermute(last, "span", up), lax.ppermute(first, "span", down)
    early = spread(early)
    low, early = lax.optimization_barrier((low, early))

    psi = struct((planes, full, cols), F32)
    psi_main = call(functools.partial(main_kernel, planes), [VMEM] * 3, [psi], "main_first", 16)(
        packed, wall_first, main_first
    )

    def scratch(some):
        return [
            pltpu.VMEM((some, faces * values, cols), F32),
            pltpu.VMEM((rest * pairs, cols, full), BF16),
            pltpu.VMEM((FACTORS, full, cols), F32),
            pltpu.VMEM((n_wall, devices, slots, some * values), BF16),
            dma((n_wall,)),
        ]

    def out(some):
        return hbm((devices, n_wall, slots, some * values), BF16)

    cells, _, *more = scratch(1)
    sent, psi = call(
        functools.partial(first_kernel, planes),
        [VMEM] * 7,
        [out(1), hbm(psi.shape, F32)],
        "filter_first",
        24,
        [pltpu.VMEM(psi.shape, F32), cells, *more, dma((1,))],
        out_specs=[ANYWHERE, ANYWHERE],
    )(psi_main, low, high, factor, target, wall_first, halo_first)
    (noise, rest_low, rest_high, wall_scale, span_scale), sent = lax.optimization_barrier(
        ((noise, rest_low, rest_high, wall_scale, span_scale), sent)
    )
    got_first = send(sent)
    late = call(
        pack_late_kernel,
        [pl.BlockSpec((1, all_planes * rows, cols), lambda i: (trio - 1, 0, 0)), VMEM, VMEM],
        [hbm((planes * rows + 2 * rest * height, cols), BF16)] * n_wall,
        "pack_late",
        56,
        [dma((n_wall, 1 + 2 * rest))],
        grid=(1,),
        out_specs=[ANYWHERE] * n_wall,
    )(noise, rest_low, rest_high)
    late = spread(late)
    wall_rest, main_rest, halo_rest = taps(1, rest, struct, "taps_rest")
    sent = call(
        functools.partial(rest_kernel, planes),
        [VMEM] * (6 + 2 * n_wall),
        [out(rest)],
        "filter_rest",
        32,
        scratch(rest),
        out_specs=[ANYWHERE],
    )(psi, factor, target, wall_rest, main_rest, halo_rest, *early, *late)
    got_rest = send(sent)

    whole = hbm((1, devices * slots, trio * values * n_wall), BF16)
    block = (1, n_wall * slots, values * n_wall)

    def join(received, some, before):
        keep = [] if before is None else [before]
        narrow = values % LANES != 0
        return pl.pallas_call(
            functools.partial(join_narrow_kernel, some)
            if narrow
            else functools.partial(join_kernel, len(keep), some, n_wall),
            grid=(n_span, some) if narrow else (),
            in_specs=[
                pl.BlockSpec((n_wall, n_wall * slots, some * values), lambda s, c: (s, 0, 0)) if narrow else ANYWHERE
            ]
            + [ANYWHERE] * len(keep),
            out_specs=pl.BlockSpec(block, lambda s, c: (0, s, c + len(keep))) if narrow else ANYWHERE,
            out_shape=whole,
            scratch_shapes=[] if narrow else [pltpu.SemaphoreType.DMA((some, devices))],
            input_output_aliases={1: 0} if keep else {},
            compiler_params=pltpu.CompilerParams(vmem_limit_bytes=16 * 1024 * 1024),
            name="join",
        )(received, *keep)

    return join(got_rest, rest, join(got_first, 1, None))


def solution(mesh):
    return jax.shard_map(
        per_device,
        mesh=mesh,
        in_specs=(
            P(None, None, "wall", "span"),
            P(),
            P(),
            P(None, "wall"),
            P("wall"),
            P("wall", "span", None, None),
        ),
        out_specs=P(("span", "wall"), None, None),
        check_vma=False,
    )
```

```python
import functools
import math

import jax
import jax.numpy as jnp
from jax import lax
from jax.experimental import pallas as pl
from jax.experimental.pallas import tpu as pltpu
from jax.sharding import PartitionSpec as P

HALO = 24
EDGE = 4
LANES = 128
FACTORS = 7
F32 = jnp.float32
BF16 = jnp.bfloat16
VMEM = pl.BlockSpec(memory_space=pltpu.VMEM)
ANYWHERE = pl.BlockSpec(memory_space=pl.ANY)
SMEM = pl.BlockSpec(memory_space=pltpu.SMEM)
ROWS_BY_ROWS = (((1,), (1,)), ((), ()))


def iota(shape, dim):
    return lax.broadcasted_iota(jnp.int32, shape, dim)


def split(x):
    high = x.astype(BF16)
    return high, (x - high.astype(F32)).astype(BF16)


def tap_values(scale, distance, valid):
    scale = jnp.full((1, 1), scale, F32)
    k = iota((1, LANES), 1) - HALO
    squares = jnp.where(k <= HALO, jnp.exp(-math.pi * (k * k).astype(F32) / (scale * scale)), 0.0)
    norm = jnp.sqrt(jnp.sum(squares, axis=1, keepdims=True))
    d = distance.astype(F32)
    raw = jnp.exp(-math.pi * (d * d) / (2.0 * scale * scale))
    inside = valid & (distance >= -HALO) & (distance <= HALO)
    return jnp.where(inside, raw, 0.0) / norm


def tail_rows(count):
    return -(-(2 * count + 3 * FACTORS) // 16) * 16


def cell_row(i, faces):
    return (i % faces) * (EDGE * EDGE) + (i // (faces * EDGE)) * EDGE + (i // faces) % EDGE


def taps_kernel(first, wall_scale, span_scale, wall_ref, main_ref, halo_ref):
    some, full, _ = wall_ref.shape
    cols = main_ref.shape[1] // 2
    walls = lax.axis_size("wall")
    rows = full // walls
    i, j = iota((full, full), 0), iota((full, full), 1)
    y = cell_row(i, full // (EDGE * EDGE))
    source = lax.rem(lax.axis_index("wall") + walls - j // rows, walls)
    column = source * rows + j % rows if first else j
    n = iota((cols, cols), 1)
    target = (n % (cols // EDGE)) * EDGE + n // (cols // EDGE)
    k = iota((cols, cols), 0)
    side, odd, r = k // (2 * HALO), (k // HALO) % 2, k % HALO
    z = jnp.where(side == 0, r - HALO, cols + r)

    def span_matrix(scale, distance, valid):
        high, low = split(tap_values(scale, distance, valid))
        top = jnp.concatenate([high, low], axis=1)
        return jnp.concatenate([top, jnp.concatenate([high, jnp.zeros_like(high)], axis=1)], axis=0)

    for c in range(some):
        high, low = split(tap_values(wall_scale[first + c], column - y, i >= 0))
        wall_ref[c, :, :full] = high
        wall_ref[c, :, full:] = low
        scale = span_scale[first + c]
        main_ref[c] = span_matrix(scale, k - target, k >= 0)
        for parity in range(2):
            valid = (k < 4 * HALO) & (odd == parity)
            halo_ref[c, parity] = span_matrix(scale, z - target, valid)


def run(copies):
    for copy in copies:
        copy.start()
    for copy in copies:
        copy.wait()


def pack_kernel(devices, noise_ref, lund_ref, mean_ref, owner_ref, out_ref, small_ref, noise_sems, small_sems):
    walls, height, cols = out_ref.shape
    tail = small_ref.shape[0]
    block = height - tail
    rows = mean_ref.shape[1]
    copies = [
        pltpu.make_async_copy(
            noise_ref.at[0, pl.ds(w * block, block)], out_ref.at[w, pl.ds(0, block)], noise_sems.at[w]
        )
        for w in range(walls)
    ]
    for copy in copies:
        copy.start()
    owner = owner_ref[...]
    elements = owner.shape[1]
    mine = jnp.where(iota((devices, elements), 0) == owner, 1.0, 0.0)
    before = jnp.where(iota((elements, elements), 0) < iota((elements, elements), 1), 1.0, 0.0)
    count = jnp.dot(mine.astype(BF16), before.astype(BF16), preferred_element_type=F32)
    rank = jnp.sum(mine * count, axis=0, keepdims=True)
    pieces = [owner.astype(F32), rank]
    pieces = [p[:, at : at + cols] for p in pieces for at in range(0, elements, cols)]
    factor = jnp.concatenate([lund_ref[...], mean_ref[...]], axis=0)
    factor = jnp.concatenate([factor, jnp.zeros((FACTORS, cols - rows), F32)], axis=1)
    for _ in range(3):
        part = factor.astype(BF16).astype(F32)
        pieces.append(part)
        factor = factor - part
    pieces.append(jnp.zeros((tail - sum(p.shape[0] for p in pieces), cols), F32))
    small_ref[...] = jnp.concatenate(pieces, axis=0).astype(BF16)
    run(
        [
            pltpu.make_async_copy(small_ref, out_ref.at[w, pl.ds(block, tail)], small_sems.at[w])
            for w in range(walls)
        ]
    )
    for copy in copies:
        copy.wait()


def pack_late_kernel(noise_ref, low_ref, high_ref, *rest):
    out_refs, sems = rest[:-1], rest[-1]
    walls, some, height, _ = low_ref.shape
    block = noise_ref.shape[1] // walls
    me = lax.axis_index("wall")
    copies = []
    for step, out_ref in enumerate(out_refs):
        to = lax.rem(me + step, walls)
        half = block // 2
        source = pl.multiple_of(to * block + half, half)
        parts = [(noise_ref.at[0, pl.ds(source, half)], 0, half)]
        for side, ref in enumerate((low_ref, high_ref)):
            for c in range(some):
                parts.append((ref.at[to, c], half + (side * some + c) * height, height))
        for part, (ref, start, size) in enumerate(parts):
            copies.append(
                pltpu.make_async_copy(ref, out_ref.at[pl.ds(start, size)], sems.at[step, part])
            )
    run(copies)


def small_kernel(slots, in_ref, factor_ref, target_ref):
    walls, height, cols = in_ref.shape
    full = factor_ref.shape[0]
    rows = full // walls
    count = target_ref.shape[1]
    tail = tail_rows(count)
    columns = jnp.zeros((full, tail), F32)
    y = cell_row(iota((full, cols), 0), full // (EDGE * EDGE))
    for w in range(walls):
        small = in_ref[w, height - tail :]
        pick = jnp.where(y == iota((full, cols), 1) + w * rows, 1.0, 0.0)
        pick = jnp.where(iota((full, cols), 1) < rows, pick, 0.0).astype(BF16)
        columns = columns + lax.dot_general(pick, small, ROWS_BY_ROWS, preferred_element_type=F32)
        numbers = small.astype(F32)
        target = numbers[:count] * slots + numbers[count : 2 * count]
        target_ref[w] = target.astype(jnp.int32)
    at = 2 * count
    factor = sum(columns[:, at + p * FACTORS : at + (p + 1) * FACTORS] for p in range(3))
    factor_ref[...] = jnp.concatenate([factor, jnp.zeros((full, cols - FACTORS), F32)], axis=1)


def edge_picker(cols):
    wide = 2 * HALO
    row, col = iota((wide, cols), 0), iota((wide, cols), 1)
    return jnp.where(col == jnp.where(row < HALO, row, cols - wide + row), 1.0, 0.0).astype(BF16)


def edges_kernel(planes, noise_ref, low_ref, high_ref):
    walls, _, cols = noise_ref.shape
    rows = low_ref.shape[1] // walls
    wide = 2 * HALO
    pick = edge_picker(cols)
    for pair in range(planes // 2):
        edges = []
        for t in (2 * pair, 2 * pair + 1):
            plane = [noise_ref[w, t * rows : (t + 1) * rows] for w in range(walls)]
            plane = jnp.concatenate(plane, axis=0)
            edges.append(lax.dot_general(pick, plane, ROWS_BY_ROWS, preferred_element_type=F32))
        at = pl.ds(pair * wide, wide)
        low_ref[at] = jnp.concatenate([e[:HALO] for e in edges], axis=0).astype(BF16)
        high_ref[at] = jnp.concatenate([e[HALO:] for e in edges], axis=0).astype(BF16)


def prepare_rest_kernel(noise_ref, low_ref, high_ref, *rest):
    out_refs, sems = rest[:-1], rest[-1]
    walls, _, height, cols = low_ref.shape
    block = noise_ref.shape[1] // walls
    me = lax.axis_index("wall")
    c = pl.program_id(0)
    last = pl.num_programs(0) - 1

    def copies(size):
        out = []
        for step, out_ref in enumerate(out_refs):
            source = pl.multiple_of(lax.rem(me + step, walls) * block, block)
            target = pl.multiple_of(c * block, block)
            out.append(
                pltpu.make_async_copy(
                    noise_ref.at[0, pl.ds(source, size)], out_ref.at[pl.ds(target, size)], sems.at[step]
                )
            )
        return out

    def each(do):
        @pl.when(c < last)
        def _():
            for copy in copies(block):
                do(copy)

        @pl.when(c == last)
        def _():
            for copy in copies(block // 2):
                do(copy)

    each(lambda copy: copy.start())
    pairs = height // HALO
    pick = edge_picker(cols)
    for w in range(walls):
        edges = []
        for pair in range(pairs):
            plane = noise_ref[0, (w * pairs + pair) * cols : (w * pairs + pair + 1) * cols]
            edges.append(lax.dot_general(pick, plane, ROWS_BY_ROWS, preferred_element_type=F32))
        low_ref[w, 0] = jnp.concatenate([e[:HALO] for e in edges], axis=0).astype(BF16)
        high_ref[w, 0] = jnp.concatenate([e[HALO:] for e in edges], axis=0).astype(BF16)

    each(lambda copy: copy.wait())


def swap_blocks(blocks, cols):
    part = cols // EDGE
    lane = iota(blocks[0].shape, 1)
    for step in (2, 1):
        first = (lane // (part * step)) % 2 == 0
        out = list(blocks)
        for a in range(EDGE):
            if a & step:
                continue
            one, two = blocks[a], blocks[a + step]
            out[a] = jnp.where(first, one, pltpu.roll(two, part * step, 1))
            out[a + step] = jnp.where(first, pltpu.roll(one, cols - part * step, 1), two)
        blocks = out
    return blocks


def halo_tiles(parts, cols):
    half = cols // 2
    sides = []
    for side in parts:
        planes = [[], []]
        for one, two in zip(side[::2], side[1::2]):
            lower = iota(one.shape, 1) < half
            planes[0].append(jnp.where(lower, one, pltpu.roll(two, half, 1)))
            planes[1].append(jnp.where(lower, pltpu.roll(one, half, 1), two))
        sides.append([jnp.concatenate(p, axis=1) for p in planes])
    pairs = sides[0][0].shape[0] // HALO
    zeros = jnp.zeros((cols - 4 * HALO, sides[0][0].shape[1]), F32)
    for pair in range(pairs):
        at = slice(pair * HALO, (pair + 1) * HALO)
        tile = [sides[s][odd][at] for s in range(2) for odd in range(2)]
        yield jnp.concatenate(tile + [zeros], axis=0).astype(BF16)


def span_product(x, matrix):
    cols = x.shape[1]
    both = jnp.dot(jnp.concatenate(split(x), axis=1), matrix, preferred_element_type=F32)
    return both[:, :cols] + both[:, cols:]


def main_part(planes, wall, matrix):
    both = jnp.concatenate(planes, axis=1)
    cols = planes[0].shape[1]
    smooth = jnp.dot(wall, jnp.concatenate([both, both], axis=0), preferred_element_type=F32)
    return [span_product(smooth[:, odd * cols : (odd + 1) * cols], matrix) for odd in range(2)]


def halo_part(tile, wall, halo_ref):
    smooth = lax.dot_general(
        wall, jnp.concatenate([tile, tile], axis=1), ROWS_BY_ROWS, preferred_element_type=F32
    )
    return [span_product(smooth, halo_ref[odd]) for odd in range(2)]


def planes_of(refs, t, rows):
    return [
        jnp.concatenate([ref[at * rows : (at + 1) * rows] for ref in refs], axis=0) for at in (t, t + 1)
    ]


def main_first_kernel(planes, wall_ref, main_ref, noise_ref, psi_ref):
    refs = [noise_ref.at[w] for w in range(noise_ref.shape[0])]
    rows = psi_ref.shape[1] // len(refs)
    for t in range(0, planes, 2):
        psi_ref[t], psi_ref[t + 1] = main_part(planes_of(refs, t, rows), wall_ref[0], main_ref[0])


def main_next_kernel(planes, wall_ref, main_ref, *rest):
    *refs, psi_ref = rest
    rows = psi_ref.shape[1] // len(refs)
    for t in range(0, psi_ref.shape[0], 2):
        c = t // planes
        psi_ref[t], psi_ref[t + 1] = main_part(planes_of(refs, t, rows), wall_ref[c], main_ref[c])


def widen(factor_ref, wide_ref, which):
    for f in which:
        wide_ref[f] = jnp.broadcast_to(factor_ref[:, f : f + 1], wide_ref.shape[1:])


def place_cells(velocity, t, cells_ref, at):
    full, cols = velocity.shape
    quarter, faces = full // EDGE, full // (EDGE * EDGE)
    values = cells_ref.shape[1] // faces
    blocks = [velocity[a * quarter : (a + 1) * quarter] for a in range(EDGE)]
    for dz, block in enumerate(swap_blocks(blocks, cols)):
        for dy in range(EDGE):
            j = t * EDGE * EDGE + dy * EDGE + dz
            cells_ref[at, pl.ds(j, faces, stride=values), :] = block[dy * faces : (dy + 1) * faces]


def scatter_cells(cells_ref, target_ref, sent_ref, out_ref, sems):
    walls, tile_faces, cols = target_ref.shape
    some = cells_ref.shape[0]
    values = cells_ref.shape[1] // (walls * tile_faces)
    _, devices, slots, width = sent_ref.shape
    copies = []
    for w in range(walls):
        payload = [
            [
                cells_ref[at, pl.ds((w * tile_faces + f) * values, values), :].astype(BF16)
                for f in range(tile_faces)
            ]
            for at in range(some)
        ]
        payload = jnp.concatenate([jnp.concatenate(p, axis=1) for p in payload], axis=0)
        slot = iota((devices * slots, cols), 0)
        onehot = [
            jnp.where(slot == target_ref[w, f : f + 1], 1.0, 0.0).astype(BF16)
            for f in range(tile_faces)
        ]
        onehot = jnp.concatenate(onehot, axis=1)
        sent = lax.dot_general(onehot, payload, ROWS_BY_ROWS, preferred_element_type=F32)
        sent_ref[w] = sent.astype(BF16).reshape(devices, slots, width)
        copies.append(pltpu.make_async_copy(sent_ref.at[w], out_ref.at[:, w], sems.at[w]))
        copies[-1].start()
    for copy in copies:
        copy.wait()


def first_kernel(
    planes, psi_in, low_ref, high_ref, factor_ref, target_ref, wall_ref, halo_ref,
    out_ref, psi_out, psi_ref, cells_ref, wide_ref, sent_ref, sems, psi_sem,
):
    full, cols = psi_ref.shape[1:]
    wide = 2 * HALO
    widen(factor_ref, wide_ref, (0, 6))

    def pair_step(pair, carry):
        at = pl.ds(pl.multiple_of(pair * wide, wide), wide)
        tile = [low_ref[at], high_ref[at], jnp.zeros((cols - 2 * wide, full), BF16)]
        beside = halo_part(jnp.concatenate(tile, axis=0), wall_ref[0], halo_ref.at[0])
        for odd in range(2):
            t = 2 * pair + odd
            psi = psi_in[t] + beside[odd]
            psi_ref[t] = psi
            place_cells(wide_ref[6] + wide_ref[0] * psi, t, cells_ref, 0)
        return carry

    lax.fori_loop(0, planes // 2, pair_step, 0, unroll=True)
    copy = pltpu.make_async_copy(psi_ref, psi_out, psi_sem.at[0])
    copy.start()
    scatter_cells(cells_ref, target_ref, sent_ref, out_ref, sems)
    copy.wait()


def rest_kernel(
    planes, psi_ref, next_ref, factor_ref, target_ref, wall_ref, main_ref, halo_ref, *rest,
):
    *late_refs, out_ref, cells_ref, tile_ref, wide_ref, sent_ref, sems = rest
    full, cols = psi_ref.shape[1:]
    some = wall_ref.shape[0]
    rows = full // len(late_refs)
    pairs = planes // 2
    height = pairs * HALO
    widen(factor_ref, wide_ref, range(1, 6))
    for c in range(some):
        starts = [planes * rows // 2 + (side * some + c) * height for side in range(2)]
        parts = [[ref[pl.ds(at, height)].astype(F32) for ref in late_refs] for at in starts]
        for pair, tile in enumerate(halo_tiles(parts, cols)):
            tile_ref[c * pairs + pair] = tile

    for pair in range(pairs):
        psi = []
        for c in range(some):
            at = c * planes + 2 * pair
            if at < next_ref.shape[0]:
                main = [next_ref[at], next_ref[at + 1]]
            else:
                at = at - next_ref.shape[0]
                main = main_part(planes_of(late_refs, at, rows), wall_ref[c], main_ref[c])
            beside = halo_part(tile_ref[c * pairs + pair], wall_ref[c], halo_ref.at[c])
            psi.append([m + b for m, b in zip(main, beside)])
        for odd in range(2):
            t = 2 * pair + odd
            p, q, r = psi_ref[t], psi[0][odd], psi[1][odd]
            place_cells(wide_ref[1] * p + wide_ref[2] * q, t, cells_ref, 0)
            place_cells(wide_ref[3] * p + wide_ref[4] * q + wide_ref[5] * r, t, cells_ref, 1)
    scatter_cells(cells_ref, target_ref, sent_ref, out_ref, sems)


def join_kernel(first, some, walls, in_ref, *rest):
    out_ref, sems = rest[-2:]
    devices, height, width = in_ref.shape
    values = width // some
    copies = []
    for c in range(some):
        for s in range(devices // walls):
            for w in range(walls):
                copies.append(
                    pltpu.make_async_copy(
                        in_ref.at[s * walls + w, :, pl.ds(c * values, values)],
                        out_ref.at[0, pl.ds(s * height, height), pl.ds(((c + first) * walls + w) * values, values)],
                        sems.at[c, s * walls + w],
                    )
                )
    run(copies)


def join_narrow_kernel(some, in_ref, *rest):
    out_ref = rest[-1]
    walls, _, width = in_ref.shape
    values = width // some
    for c in range(some):

        @pl.when(pl.program_id(1) == c)
        def _():
            for w in range(walls):
                out_ref[0, :, w * values : (w + 1) * values] = in_ref[w, :, c * values : (c + 1) * values]


def per_device(noise, wall_scale, span_scale, lund_factor, mean_velocity, owner_map):
    trio, all_planes, rows, cols = noise.shape
    n_span = lax.axis_size("span")
    n_wall = lax.axis_size("wall")
    devices = n_span * n_wall
    planes = all_planes // n_wall
    pairs = planes // 2
    full = rows * n_wall
    faces = full // (EDGE * EDGE)
    values = planes * EDGE * EDGE
    owners = owner_map.reshape(1, -1)
    elements = owners.shape[1]
    slots = max(8, 2 * elements // devices)
    count = elements // cols
    rest = trio - 1
    struct = jax.ShapeDtypeStruct
    hbm = pltpu.MemorySpace.HBM

    def call(kernel, ins, outs, name, limit, scratch=(), grid=(), out_specs=None):
        specs = out_specs or [VMEM] * len(outs)
        return pl.pallas_call(
            kernel,
            grid=grid,
            in_specs=ins,
            out_specs=specs if len(outs) > 1 else specs[0],
            out_shape=outs if len(outs) > 1 else outs[0],
            scratch_shapes=scratch,
            compiler_params=pltpu.CompilerParams(vmem_limit_bytes=limit * 1024 * 1024),
            cost_estimate=pl.CostEstimate(flops=1024, bytes_accessed=1024, transcendentals=0),
            name=name,
        )

    up = [(i, (i + 1) % n_span) for i in range(n_span)]
    down = [(b, a) for a, b in up]

    def swap(x):
        return lax.all_to_all(x, "wall", 0, 0, tiled=True)

    def send(x):
        return lax.all_to_all(x, ("span", "wall"), 0, 0, tiled=True).reshape(devices, n_wall * slots, -1)

    dma = pltpu.SemaphoreType.DMA
    noise = noise.reshape(trio, all_planes * rows, cols)
    packed = call(
        functools.partial(pack_kernel, devices),
        [pl.BlockSpec((1, all_planes * rows, cols), lambda i: (0, 0, 0)), VMEM, VMEM, VMEM],
        [hbm((n_wall, planes * rows + tail_rows(count), cols), BF16)],
        "pack",
        56,
        [pltpu.VMEM((tail_rows(count), cols), BF16), dma((n_wall,)), dma((n_wall,))],
        grid=(1,),
        out_specs=[ANYWHERE],
    )(noise, lund_factor, mean_velocity.reshape(1, rows), owners)
    noise, packed = lax.optimization_barrier((noise, packed))
    packed = swap(packed)

    height = pairs * HALO
    edge = hbm((n_wall, rest, height, cols), BF16)
    spec = pl.BlockSpec((n_wall, 1, height, cols), lambda c: (0, c, 0, 0))
    first, last, *early = call(
        prepare_rest_kernel,
        [pl.BlockSpec((1, all_planes * rows, cols), lambda c: (c + 1, 0, 0))],
        [edge, edge] + [hbm((rest * planes * rows - planes * rows // 2, cols), BF16)] * n_wall,
        "prepare_rest",
        16,
        [dma((n_wall,))],
        grid=(rest,),
        out_specs=[spec, spec] + [ANYWHERE] * n_wall,
    )(noise)
    rest_low, rest_high = lax.ppermute(last, "span", up), lax.ppermute(first, "span", down)
    packed, _ = lax.optimization_barrier((packed, (first, last, early)))

    def spread(blocks):
        return [blocks[0]] + [
            lax.ppermute(x, "wall", [(i, (i + step) % n_wall) for i in range(n_wall)])
            for step, x in enumerate(blocks[1:], 1)
        ]

    def taps(first, some, make, name):
        return call(
            functools.partial(taps_kernel, first),
            [SMEM, SMEM],
            [
                make((some, full, 2 * full), BF16),
                make((some, 2 * cols, 2 * cols), BF16),
                make((some, 2, 2 * cols, 2 * cols), BF16),
            ],
            name,
            16,
        )(wall_scale, span_scale)

    wall_first, main_first, halo_first = taps(0, 1, struct, "taps_first")
    factor, target = call(
        functools.partial(small_kernel, slots),
        [VMEM],
        [struct((full, cols), F32), struct((n_wall, count, cols), jnp.int32)],
        "small",
        16,
    )(packed)

    edge = struct((planes * HALO, full), BF16)
    first, last = call(
        functools.partial(edges_kernel, planes), [VMEM], [edge, edge], "edges_first", 16
    )(packed)
    low, high = lax.ppermute(last, "span", up), lax.ppermute(first, "span", down)
    early = spread(early)
    late = call(
        pack_late_kernel,
        [pl.BlockSpec((1, all_planes * rows, cols), lambda i: (trio - 1, 0, 0)), VMEM, VMEM],
        [hbm((planes * rows // 2 + 2 * rest * height, cols), BF16)] * n_wall,
        "pack_late",
        16,
        [dma((n_wall, 1 + 2 * rest))],
        grid=(1,),
        out_specs=[ANYWHERE] * n_wall,
    )(noise, rest_low, rest_high)
    low, early, late = lax.optimization_barrier((low, early, late))

    psi = struct((planes, full, cols), F32)
    psi_main = call(
        functools.partial(main_first_kernel, planes), [VMEM] * 3, [psi], "main_first", 16
    )(wall_first, main_first, packed)

    def scratch(some):
        return [
            pltpu.VMEM((some, faces * values, cols), F32),
            pltpu.VMEM((rest * pairs, cols, full), BF16),
            pltpu.VMEM((FACTORS, full, cols), F32),
            pltpu.VMEM((n_wall, devices, slots, some * values), BF16),
            dma((n_wall,)),
        ]

    def out(some):
        return hbm((devices, n_wall, slots, some * values), BF16)

    cells, _, *more = scratch(1)
    sent, psi = call(
        functools.partial(first_kernel, planes),
        [VMEM] * 7,
        [out(1), hbm(psi.shape, F32)],
        "filter_first",
        24,
        [pltpu.VMEM(psi.shape, F32), cells, *more, dma((1,))],
        out_specs=[ANYWHERE, ANYWHERE],
    )(psi_main, low, high, factor, target, wall_first, halo_first)
    (wall_scale, span_scale), sent = lax.optimization_barrier(((wall_scale, span_scale), sent))
    got_first = send(sent)
    late = spread(late)
    wall_rest, main_rest, halo_rest = taps(1, rest, struct, "taps_rest")
    psi_next = call(
        functools.partial(main_next_kernel, planes),
        [VMEM] * (2 + n_wall),
        [struct((rest * planes - planes // 2, full, cols), F32)],
        "main_next",
        16,
    )(wall_rest, main_rest, *early)
    sent = call(
        functools.partial(rest_kernel, planes),
        [VMEM] * (7 + n_wall),
        [out(rest)],
        "filter_rest",
        32,
        scratch(rest),
        out_specs=[ANYWHERE],
    )(psi, psi_next, factor, target, wall_rest, main_rest, halo_rest, *late)
    got_rest = send(sent)

    whole = hbm((1, devices * slots, trio * values * n_wall), BF16)
    block = (1, n_wall * slots, values * n_wall)

    def join(received, some, before):
        keep = [] if before is None else [before]
        narrow = values % LANES != 0
        return pl.pallas_call(
            functools.partial(join_narrow_kernel, some)
            if narrow
            else functools.partial(join_kernel, len(keep), some, n_wall),
            grid=(n_span, some) if narrow else (),
            in_specs=[
                pl.BlockSpec((n_wall, n_wall * slots, some * values), lambda s, c: (s, 0, 0)) if narrow else ANYWHERE
            ]
            + [ANYWHERE] * len(keep),
            out_specs=pl.BlockSpec(block, lambda s, c: (0, s, c + len(keep))) if narrow else ANYWHERE,
            out_shape=whole,
            scratch_shapes=[] if narrow else [pltpu.SemaphoreType.DMA((some, devices))],
            input_output_aliases={1: 0} if keep else {},
            compiler_params=pltpu.CompilerParams(vmem_limit_bytes=16 * 1024 * 1024),
            name="join",
        )(received, *keep)

    return join(got_rest, rest, join(got_first, 1, None))


def solution(mesh):
    return jax.shard_map(
        per_device,
        mesh=mesh,
        in_specs=(
            P(None, None, "wall", "span"),
            P(),
            P(),
            P(None, "wall"),
            P("wall"),
            P("wall", "span", None, None),
        ),
        out_specs=P(("span", "wall"), None, None),
        check_vma=False,
    )
```

```python
import functools
import math

import jax
import jax.numpy as jnp
from jax import lax
from jax.experimental import pallas as pl
from jax.experimental.pallas import tpu as pltpu
from jax.sharding import PartitionSpec as P

HALO = 24
EDGE = 4
LANES = 128
FACTORS = 7
CORES = 2
F32 = jnp.float32
BF16 = jnp.bfloat16
VMEM = pl.BlockSpec(memory_space=pltpu.VMEM)
ANYWHERE = pl.BlockSpec(memory_space=pl.ANY)
SMEM = pl.BlockSpec(memory_space=pltpu.SMEM)
ROWS_BY_ROWS = (((1,), (1,)), ((), ()))


def iota(shape, dim):
    return lax.broadcasted_iota(jnp.int32, shape, dim)


def split(x):
    high = x.astype(BF16)
    return high, (x - high.astype(F32)).astype(BF16)


def tap_values(scale, distance, valid):
    scale = jnp.full((1, 1), scale, F32)
    k = iota((1, LANES), 1) - HALO
    squares = jnp.where(k <= HALO, jnp.exp(-math.pi * (k * k).astype(F32) / (scale * scale)), 0.0)
    norm = jnp.sqrt(jnp.sum(squares, axis=1, keepdims=True))
    d = distance.astype(F32)
    raw = jnp.exp(-math.pi * (d * d) / (2.0 * scale * scale))
    inside = valid & (distance >= -HALO) & (distance <= HALO)
    return jnp.where(inside, raw, 0.0) / norm


def tail_rows(count):
    return -(-(2 * count + 3 * FACTORS) // 16) * 16


def cell_row(i, faces):
    return (i % faces) * (EDGE * EDGE) + (i // (faces * EDGE)) * EDGE + (i // faces) % EDGE


def taps_kernel(first, wall_scale, span_scale, wall_ref, main_ref, halo_ref):
    some, full, _ = wall_ref.shape
    cols = main_ref.shape[1] // 2
    walls = lax.axis_size("wall")
    rows = full // walls
    i, j = iota((full, full), 0), iota((full, full), 1)
    y = cell_row(i, full // (EDGE * EDGE))
    source = lax.rem(lax.axis_index("wall") + walls - j // rows, walls)
    column = source * rows + j % rows if first else j
    n = iota((cols, cols), 1)
    target = (n % (cols // EDGE)) * EDGE + n // (cols // EDGE)
    k = iota((cols, cols), 0)
    side, odd, r = k // (2 * HALO), (k // HALO) % 2, k % HALO
    core = lax.rem(lax.axis_index("span"), CORES)
    z = jnp.where(side + core == 1, r - HALO, cols + r)

    def span_matrix(scale, distance, valid):
        high, low = split(tap_values(scale, distance, valid))
        top = jnp.concatenate([high, low], axis=1)
        return jnp.concatenate([top, jnp.concatenate([high, jnp.zeros_like(high)], axis=1)], axis=0)

    for c in range(some):
        high, low = split(tap_values(wall_scale[first + c], column - y, i >= 0))
        wall_ref[c, :, :full] = high
        wall_ref[c, :, full:] = low
        scale = span_scale[first + c]
        main_ref[c] = span_matrix(scale, k - target, k >= 0)
        for parity in range(2):
            valid = (k < 4 * HALO) & (odd == parity)
            halo_ref[c, parity] = span_matrix(scale, z - target, valid)


def run(copies):
    for copy in copies:
        copy.start()
    for copy in copies:
        copy.wait()


def pack_kernel(devices, noise_ref, lund_ref, mean_ref, owner_ref, out_ref, small_ref, noise_sems, small_sems):
    walls, height, cols = out_ref.shape
    tail = small_ref.shape[0]
    block = height - tail
    rows = mean_ref.shape[1]
    copies = [
        pltpu.make_async_copy(
            noise_ref.at[0, pl.ds(w * block, block)], out_ref.at[w, pl.ds(0, block)], noise_sems.at[w]
        )
        for w in range(walls)
    ]
    for copy in copies:
        copy.start()
    owner = owner_ref[...]
    elements = owner.shape[1]
    mine = jnp.where(iota((devices, elements), 0) == owner, 1.0, 0.0)
    before = jnp.where(iota((elements, elements), 0) < iota((elements, elements), 1), 1.0, 0.0)
    count = jnp.dot(mine.astype(BF16), before.astype(BF16), preferred_element_type=F32)
    rank = jnp.sum(mine * count, axis=0, keepdims=True)
    pieces = [owner.astype(F32), rank]
    pieces = [p[:, at : at + cols] for p in pieces for at in range(0, elements, cols)]
    factor = jnp.concatenate([lund_ref[...], mean_ref[...]], axis=0)
    factor = jnp.concatenate([factor, jnp.zeros((FACTORS, cols - rows), F32)], axis=1)
    for _ in range(3):
        part = factor.astype(BF16).astype(F32)
        pieces.append(part)
        factor = factor - part
    pieces.append(jnp.zeros((tail - sum(p.shape[0] for p in pieces), cols), F32))
    small_ref[...] = jnp.concatenate(pieces, axis=0).astype(BF16)
    run(
        [
            pltpu.make_async_copy(small_ref, out_ref.at[w, pl.ds(block, tail)], small_sems.at[w])
            for w in range(walls)
        ]
    )
    for copy in copies:
        copy.wait()


def pack_late_kernel(noise_ref, near_ref, far_ref, *rest):
    out_refs, sems = rest[:-1], rest[-1]
    walls, some, height, _ = near_ref.shape
    block = noise_ref.shape[1] // walls
    me = lax.axis_index("wall")
    copies = []
    for step, out_ref in enumerate(out_refs):
        to = lax.rem(me + step, walls)
        left = out_ref.shape[0] - 2 * some * height
        source = pl.multiple_of(to * block + block - left, math.gcd(block, left))
        parts = [(noise_ref.at[0, pl.ds(source, left)], 0, left)]
        for side, ref in enumerate((near_ref, far_ref)):
            for c in range(some):
                parts.append((ref.at[to, c], left + (side * some + c) * height, height))
        for part, (ref, start, size) in enumerate(parts):
            copies.append(
                pltpu.make_async_copy(ref, out_ref.at[pl.ds(start, size)], sems.at[step, part])
            )
    run(copies)


def small_kernel(slots, in_ref, factor_ref, target_ref):
    walls, height, cols = in_ref.shape
    full = factor_ref.shape[0]
    rows = full // walls
    count = target_ref.shape[1]
    tail = tail_rows(count)
    columns = jnp.zeros((full, tail), F32)
    y = cell_row(iota((full, cols), 0), full // (EDGE * EDGE))
    for w in range(walls):
        small = in_ref[w, height - tail :]
        pick = jnp.where(y == iota((full, cols), 1) + w * rows, 1.0, 0.0)
        pick = jnp.where(iota((full, cols), 1) < rows, pick, 0.0).astype(BF16)
        columns = columns + lax.dot_general(pick, small, ROWS_BY_ROWS, preferred_element_type=F32)
        numbers = small.astype(F32)
        target = numbers[:count] * slots + numbers[count : 2 * count]
        target_ref[w] = target.astype(jnp.int32)
    at = 2 * count
    factor = sum(columns[:, at + p * FACTORS : at + (p + 1) * FACTORS] for p in range(3))
    factor_ref[...] = jnp.concatenate([factor, jnp.zeros((full, cols - FACTORS), F32)], axis=1)


def edge_picker(cols):
    core = lax.rem(lax.axis_index("span"), CORES)
    row, col = iota((2 * HALO, cols), 0), iota((2 * HALO, cols), 1)
    start = jnp.where(row // HALO == core, cols - HALO, 0)
    return jnp.where(col == start + row % HALO, 1.0, 0.0).astype(BF16)


def edges_kernel(planes, noise_ref, near_ref, far_ref):
    walls, _, cols = noise_ref.shape
    rows = near_ref.shape[1] // walls
    wide = 2 * HALO
    pick = edge_picker(cols)
    for pair in range(planes // 2):
        edges = []
        for t in (2 * pair, 2 * pair + 1):
            plane = [noise_ref[w, t * rows : (t + 1) * rows] for w in range(walls)]
            plane = jnp.concatenate(plane, axis=0)
            edges.append(lax.dot_general(pick, plane, ROWS_BY_ROWS, preferred_element_type=F32))
        at = pl.ds(pair * wide, wide)
        near_ref[at] = jnp.concatenate([e[:HALO] for e in edges], axis=0).astype(BF16)
        far_ref[at] = jnp.concatenate([e[HALO:] for e in edges], axis=0).astype(BF16)


def prepare_rest_kernel(noise_ref, near_ref, far_ref, *rest):
    out_refs, sems = rest[:-1], rest[-1]
    walls, _, height, cols = near_ref.shape
    block = noise_ref.shape[1] // walls
    me = lax.axis_index("wall")
    c = pl.program_id(0)
    last = pl.num_programs(0) - 1

    def copies(size):
        out = []
        for step, out_ref in enumerate(out_refs):
            source = pl.multiple_of(lax.rem(me + step, walls) * block, block)
            target = pl.multiple_of(c * block, block)
            out.append(
                pltpu.make_async_copy(
                    noise_ref.at[0, pl.ds(source, size)], out_ref.at[pl.ds(target, size)], sems.at[step]
                )
            )
        return out

    def each(do):
        @pl.when(c < last)
        def _():
            for copy in copies(block):
                do(copy)

        @pl.when(c == last)
        def _():
            for copy in copies(out_refs[0].shape[0] - last * block):
                do(copy)

    each(lambda copy: copy.start())
    pairs = height // HALO
    pick = edge_picker(cols)
    for w in range(walls):
        edges = []
        for pair in range(pairs):
            plane = noise_ref[0, (w * pairs + pair) * cols : (w * pairs + pair + 1) * cols]
            edges.append(lax.dot_general(pick, plane, ROWS_BY_ROWS, preferred_element_type=F32))
        near_ref[w, 0] = jnp.concatenate([e[:HALO] for e in edges], axis=0).astype(BF16)
        far_ref[w, 0] = jnp.concatenate([e[HALO:] for e in edges], axis=0).astype(BF16)

    each(lambda copy: copy.wait())


def swap_blocks(blocks, cols):
    part = cols // EDGE
    lane = iota(blocks[0].shape, 1)
    for step in (2, 1):
        first = (lane // (part * step)) % 2 == 0
        out = list(blocks)
        for a in range(EDGE):
            if a & step:
                continue
            one, two = blocks[a], blocks[a + step]
            out[a] = jnp.where(first, one, pltpu.roll(two, part * step, 1))
            out[a + step] = jnp.where(first, pltpu.roll(one, cols - part * step, 1), two)
        blocks = out
    return blocks


def halo_tiles(parts, cols):
    half = cols // 2
    sides = []
    for side in parts:
        planes = [[], []]
        for one, two in zip(side[::2], side[1::2]):
            lower = iota(one.shape, 1) < half
            planes[0].append(jnp.where(lower, one, pltpu.roll(two, half, 1)))
            planes[1].append(jnp.where(lower, pltpu.roll(one, half, 1), two))
        sides.append([jnp.concatenate(p, axis=1) for p in planes])
    pairs = sides[0][0].shape[0] // HALO
    zeros = jnp.zeros((cols - 4 * HALO, sides[0][0].shape[1]), F32)
    for pair in range(pairs):
        at = slice(pair * HALO, (pair + 1) * HALO)
        tile = [sides[s][odd][at] for s in range(2) for odd in range(2)]
        yield jnp.concatenate(tile + [zeros], axis=0).astype(BF16)


def span_product(x, matrix):
    cols = x.shape[1]
    both = jnp.dot(jnp.concatenate(split(x), axis=1), matrix, preferred_element_type=F32)
    return both[:, :cols] + both[:, cols:]


def main_part(planes, wall, matrix):
    both = jnp.concatenate(planes, axis=1)
    cols = planes[0].shape[1]
    smooth = jnp.dot(wall, jnp.concatenate([both, both], axis=0), preferred_element_type=F32)
    return [span_product(smooth[:, odd * cols : (odd + 1) * cols], matrix) for odd in range(2)]


def halo_part(tile, wall, halo_ref):
    smooth = lax.dot_general(
        wall, jnp.concatenate([tile, tile], axis=1), ROWS_BY_ROWS, preferred_element_type=F32
    )
    return [span_product(smooth, halo_ref[odd]) for odd in range(2)]


def planes_of(refs, t, rows):
    return [
        jnp.concatenate([ref[at * rows : (at + 1) * rows] for ref in refs], axis=0) for at in (t, t + 1)
    ]


def main_first_kernel(planes, wall_ref, main_ref, noise_ref, psi_ref):
    refs = [noise_ref.at[w] for w in range(noise_ref.shape[0])]
    rows = psi_ref.shape[1] // len(refs)
    for t in range(0, planes, 2):
        psi_ref[t], psi_ref[t + 1] = main_part(planes_of(refs, t, rows), wall_ref[0], main_ref[0])


def main_next_kernel(planes, wall_ref, main_ref, *rest):
    *refs, psi_ref = rest
    rows = psi_ref.shape[1] // len(refs)
    for t in range(0, psi_ref.shape[0], 2):
        c = t // planes
        psi_ref[t], psi_ref[t + 1] = main_part(planes_of(refs, t, rows), wall_ref[c], main_ref[c])


def widen(factor_ref, wide_ref, which):
    for f in which:
        wide_ref[f] = jnp.broadcast_to(factor_ref[:, f : f + 1], wide_ref.shape[1:])


def place_cells(velocity, t, cells_ref, at):
    full, cols = velocity.shape
    quarter, faces = full // EDGE, full // (EDGE * EDGE)
    values = cells_ref.shape[1] // faces
    blocks = [velocity[a * quarter : (a + 1) * quarter] for a in range(EDGE)]
    for dz, block in enumerate(swap_blocks(blocks, cols)):
        for dy in range(EDGE):
            j = t * EDGE * EDGE + dy * EDGE + dz
            cells_ref[at, pl.ds(j, faces, stride=values), :] = block[dy * faces : (dy + 1) * faces]


def scatter_cells(cells_ref, target_ref, sent_ref, out_ref, sems):
    walls, tile_faces, cols = target_ref.shape
    some = cells_ref.shape[0]
    values = cells_ref.shape[1] // (walls * tile_faces)
    _, devices, slots, width = sent_ref.shape
    copies = []
    for w in range(walls):
        payload = [
            [
                cells_ref[at, pl.ds((w * tile_faces + f) * values, values), :].astype(BF16)
                for f in range(tile_faces)
            ]
            for at in range(some)
        ]
        payload = jnp.concatenate([jnp.concatenate(p, axis=1) for p in payload], axis=0)
        slot = iota((devices * slots, cols), 0)
        onehot = [
            jnp.where(slot == target_ref[w, f : f + 1], 1.0, 0.0).astype(BF16)
            for f in range(tile_faces)
        ]
        onehot = jnp.concatenate(onehot, axis=1)
        sent = lax.dot_general(onehot, payload, ROWS_BY_ROWS, preferred_element_type=F32)
        sent_ref[w] = sent.astype(BF16).reshape(devices, slots, width)
        copies.append(pltpu.make_async_copy(sent_ref.at[w], out_ref.at[:, w], sems.at[w]))
        copies[-1].start()
    for copy in copies:
        copy.wait()


def first_kernel(
    planes, psi_in, near_ref, far_ref, factor_ref, target_ref, wall_ref, halo_ref,
    out_ref, psi_out, psi_ref, cells_ref, wide_ref, sent_ref, sems, psi_sem,
):
    full, cols = psi_ref.shape[1:]
    wide = 2 * HALO
    widen(factor_ref, wide_ref, (0, 6))

    def pair_step(pair, carry):
        at = pl.ds(pl.multiple_of(pair * wide, wide), wide)
        tile = [near_ref[at], far_ref[at], jnp.zeros((cols - 2 * wide, full), BF16)]
        beside = halo_part(jnp.concatenate(tile, axis=0), wall_ref[0], halo_ref.at[0])
        for odd in range(2):
            t = 2 * pair + odd
            psi = psi_in[t] + beside[odd]
            psi_ref[t] = psi
            place_cells(wide_ref[6] + wide_ref[0] * psi, t, cells_ref, 0)
        return carry

    lax.fori_loop(0, planes // 2, pair_step, 0, unroll=True)
    copy = pltpu.make_async_copy(psi_ref, psi_out, psi_sem.at[0])
    copy.start()
    scatter_cells(cells_ref, target_ref, sent_ref, out_ref, sems)
    copy.wait()


def rest_kernel(
    planes, psi_ref, next_ref, factor_ref, target_ref, wall_ref, main_ref, halo_ref, *rest,
):
    *late_refs, out_ref, cells_ref, tile_ref, wide_ref, sent_ref, sems = rest
    full, cols = psi_ref.shape[1:]
    some = wall_ref.shape[0]
    rows = full // len(late_refs)
    pairs = planes // 2
    height = pairs * HALO
    widen(factor_ref, wide_ref, range(1, 6))
    for c in range(some):
        left = (some * planes - next_ref.shape[0]) * rows
        starts = [left + (side * some + c) * height for side in range(2)]
        parts = [[ref[pl.ds(at, height)].astype(F32) for ref in late_refs] for at in starts]
        for pair, tile in enumerate(halo_tiles(parts, cols)):
            tile_ref[c * pairs + pair] = tile

    for pair in range(pairs):
        psi = []
        for c in range(some):
            at = c * planes + 2 * pair
            if at < next_ref.shape[0]:
                main = [next_ref[at], next_ref[at + 1]]
            else:
                at = at - next_ref.shape[0]
                main = main_part(planes_of(late_refs, at, rows), wall_ref[c], main_ref[c])
            beside = halo_part(tile_ref[c * pairs + pair], wall_ref[c], halo_ref.at[c])
            psi.append([m + b for m, b in zip(main, beside)])
        for odd in range(2):
            t = 2 * pair + odd
            p, q, r = psi_ref[t], psi[0][odd], psi[1][odd]
            place_cells(wide_ref[1] * p + wide_ref[2] * q, t, cells_ref, 0)
            place_cells(wide_ref[3] * p + wide_ref[4] * q + wide_ref[5] * r, t, cells_ref, 1)
    scatter_cells(cells_ref, target_ref, sent_ref, out_ref, sems)


def join_kernel(first, some, in_ref, *rest):
    out_ref, sems = rest[-2:]
    _, walls, _, width = in_ref.shape
    values = width // some
    run(
        [
            pltpu.make_async_copy(
                in_ref.at[:, w, :, pl.ds(c * values, values)],
                out_ref.at[:, :, pl.ds(((c + first) * walls + w) * values, values)],
                sems.at[c, w],
            )
            for c in range(some)
            for w in range(walls)
        ]
    )


def join_narrow_kernel(some, in_ref, *rest):
    out_ref = rest[-1]
    _, walls, _, width = in_ref.shape
    values = width // some
    for c in range(some):

        @pl.when(pl.program_id(1) == c)
        def _():
            for w in range(walls):
                out_ref[0, :, w * values : (w + 1) * values] = in_ref[0, w, :, c * values : (c + 1) * values]


def per_device(noise, wall_scale, span_scale, lund_factor, mean_velocity, owner_map):
    trio, all_planes, rows, cols = noise.shape
    n_span = lax.axis_size("span")
    n_wall = lax.axis_size("wall")
    devices = n_span * n_wall
    planes = all_planes // n_wall
    pairs = planes // 2
    full = rows * n_wall
    faces = full // (EDGE * EDGE)
    values = planes * EDGE * EDGE
    owners = owner_map.reshape(1, -1)
    elements = owners.shape[1]
    slots = max(8, 2 * elements // devices)
    count = elements // cols
    rest = trio - 1
    ahead = rest * planes - planes // 2
    struct = jax.ShapeDtypeStruct
    hbm = pltpu.MemorySpace.HBM

    def call(kernel, ins, outs, name, limit, scratch=(), grid=(), out_specs=None):
        specs = out_specs or [VMEM] * len(outs)
        return pl.pallas_call(
            kernel,
            grid=grid,
            in_specs=ins,
            out_specs=specs if len(outs) > 1 else specs[0],
            out_shape=outs if len(outs) > 1 else outs[0],
            scratch_shapes=scratch,
            compiler_params=pltpu.CompilerParams(vmem_limit_bytes=limit * 1024 * 1024),
            cost_estimate=pl.CostEstimate(flops=1024, bytes_accessed=1024, transcendentals=0),
            name=name,
        )

    core_pairs = [(i, i ^ 1) for i in range(n_span)]
    chip_pairs = [(i, (i + 2 * (i % CORES) - 1) % n_span) for i in range(n_span)]

    def exchange(near, far):
        return lax.ppermute(near, "span", core_pairs), lax.ppermute(far, "span", chip_pairs)

    def swap(x):
        return lax.all_to_all(x, "wall", 0, 0, tiled=True)

    def send(x):
        return lax.all_to_all(x, ("span", "wall"), 0, 0, tiled=True).reshape(devices, n_wall * slots, -1)

    dma = pltpu.SemaphoreType.DMA
    noise = noise.reshape(trio, all_planes * rows, cols)
    packed = call(
        functools.partial(pack_kernel, devices),
        [pl.BlockSpec((1, all_planes * rows, cols), lambda i: (0, 0, 0)), VMEM, VMEM, VMEM],
        [hbm((n_wall, planes * rows + tail_rows(count), cols), BF16)],
        "pack",
        56,
        [pltpu.VMEM((tail_rows(count), cols), BF16), dma((n_wall,)), dma((n_wall,))],
        grid=(1,),
        out_specs=[ANYWHERE],
    )(noise, lund_factor, mean_velocity.reshape(1, rows), owners)
    noise, packed = lax.optimization_barrier((noise, packed))
    packed = swap(packed)

    height = pairs * HALO
    edge = hbm((n_wall, rest, height, cols), BF16)
    spec = pl.BlockSpec((n_wall, 1, height, cols), lambda c: (0, c, 0, 0))
    near, far, *early = call(
        prepare_rest_kernel,
        [pl.BlockSpec((1, all_planes * rows, cols), lambda c: (c + 1, 0, 0))],
        [edge, edge] + [hbm((ahead * rows, cols), BF16)] * n_wall,
        "prepare_rest",
        16,
        [dma((n_wall,))],
        grid=(rest,),
        out_specs=[spec, spec] + [ANYWHERE] * n_wall,
    )(noise)
    rest_near, rest_far = exchange(near, far)
    packed, _ = lax.optimization_barrier((packed, (near, far, early)))

    def spread(blocks):
        return [blocks[0]] + [
            lax.ppermute(x, "wall", [(i, (i + step) % n_wall) for i in range(n_wall)])
            for step, x in enumerate(blocks[1:], 1)
        ]

    def taps(first, some, make, name):
        return call(
            functools.partial(taps_kernel, first),
            [SMEM, SMEM],
            [
                make((some, full, 2 * full), BF16),
                make((some, 2 * cols, 2 * cols), BF16),
                make((some, 2, 2 * cols, 2 * cols), BF16),
            ],
            name,
            16,
        )(wall_scale, span_scale)

    wall_first, main_first, halo_first = taps(0, 1, struct, "taps_first")
    factor, target = call(
        functools.partial(small_kernel, slots),
        [VMEM],
        [struct((full, cols), F32), struct((n_wall, count, cols), jnp.int32)],
        "small",
        16,
    )(packed)

    edge = struct((planes * HALO, full), BF16)
    near, far = call(
        functools.partial(edges_kernel, planes), [VMEM], [edge, edge], "edges_first", 16
    )(packed)
    near, far = exchange(near, far)
    early = spread(early)
    late = call(
        pack_late_kernel,
        [pl.BlockSpec((1, all_planes * rows, cols), lambda i: (trio - 1, 0, 0)), VMEM, VMEM],
        [hbm(((rest * planes - ahead) * rows + 2 * rest * height, cols), BF16)] * n_wall,
        "pack_late",
        16,
        [dma((n_wall, 1 + 2 * rest))],
        grid=(1,),
        out_specs=[ANYWHERE] * n_wall,
    )(noise, rest_near, rest_far)
    near, early, late = lax.optimization_barrier((near, early, late))

    psi = struct((planes, full, cols), F32)
    psi_main = call(
        functools.partial(main_first_kernel, planes), [VMEM] * 3, [psi], "main_first", 16
    )(wall_first, main_first, packed)

    def scratch(some):
        return [
            pltpu.VMEM((some, faces * values, cols), F32),
            pltpu.VMEM((rest * pairs, cols, full), BF16),
            pltpu.VMEM((FACTORS, full, cols), F32),
            pltpu.VMEM((n_wall, devices, slots, some * values), BF16),
            dma((n_wall,)),
        ]

    def out(some):
        return hbm((devices, n_wall, slots, some * values), BF16)

    cells, _, *more = scratch(1)
    sent, psi = call(
        functools.partial(first_kernel, planes),
        [VMEM] * 7,
        [out(1), hbm(psi.shape, F32)],
        "filter_first",
        24,
        [pltpu.VMEM(psi.shape, F32), cells, *more, dma((1,))],
        out_specs=[ANYWHERE, ANYWHERE],
    )(psi_main, near, far, factor, target, wall_first, halo_first)
    (wall_scale, span_scale), sent = lax.optimization_barrier(((wall_scale, span_scale), sent))
    got_first = send(sent)
    late = spread(late)
    wall_rest, main_rest, halo_rest = taps(1, rest, struct, "taps_rest")
    psi_next = call(
        functools.partial(main_next_kernel, planes),
        [VMEM] * (2 + n_wall),
        [struct((ahead, full, cols), F32)],
        "main_next",
        16,
    )(wall_rest, main_rest, *early)
    sent = call(
        functools.partial(rest_kernel, planes),
        [VMEM] * (7 + n_wall),
        [out(rest)],
        "filter_rest",
        32,
        scratch(rest),
        out_specs=[ANYWHERE],
    )(psi, psi_next, factor, target, wall_rest, main_rest, halo_rest, *late)
    got_rest = send(sent)

    whole = hbm((n_span, n_wall * slots, trio * values * n_wall), BF16)
    narrow = values % LANES != 0

    def join(received, some, before):
        keep = [] if before is None else [before]
        shape = (n_span, n_wall, n_wall * slots, some * values)
        return pl.pallas_call(
            functools.partial(join_narrow_kernel, some)
            if narrow
            else functools.partial(join_kernel, len(keep), some),
            grid=(n_span, some) if narrow else (),
            in_specs=[pl.BlockSpec((1, *shape[1:]), lambda s, c: (s, 0, 0, 0)) if narrow else VMEM]
            + [ANYWHERE] * len(keep),
            out_specs=pl.BlockSpec((1, n_wall * slots, values * n_wall), lambda s, c: (s, 0, c + len(keep)))
            if narrow
            else ANYWHERE,
            out_shape=whole,
            scratch_shapes=[] if narrow else [dma((some, n_wall))],
            input_output_aliases={1: 0} if keep else {},
            compiler_params=pltpu.CompilerParams(vmem_limit_bytes=16 * 1024 * 1024),
            name="join",
        )(received.reshape(shape), *keep)

    return join(got_rest, rest, join(got_first, 1, None)).reshape(1, devices * slots, -1)


def solution(mesh):
    return jax.shard_map(
        per_device,
        mesh=mesh,
        in_specs=(
            P(None, None, "wall", "span"),
            P(),
            P(),
            P(None, "wall"),
            P("wall"),
            P("wall", "span", None, None),
        ),
        out_specs=P(("span", "wall"), None, None),
        check_vma=False,
    )
```

```python
import functools
import math

import jax
import jax.numpy as jnp
from jax import lax
from jax.experimental import pallas as pl
from jax.experimental.pallas import tpu as pltpu
from jax.sharding import PartitionSpec as P

HALO = 24
EDGE = 4
LANES = 128
FACTORS = 7
CORES = 2
F32 = jnp.float32
BF16 = jnp.bfloat16
VMEM = pl.BlockSpec(memory_space=pltpu.VMEM)
ANYWHERE = pl.BlockSpec(memory_space=pl.ANY)
SMEM = pl.BlockSpec(memory_space=pltpu.SMEM)
ROWS_BY_ROWS = (((1,), (1,)), ((), ()))


def iota(shape, dim):
    return lax.broadcasted_iota(jnp.int32, shape, dim)


def split(x):
    high = x.astype(BF16)
    return high, (x - high.astype(F32)).astype(BF16)


def tap_values(scale, distance, valid):
    scale = jnp.full((1, 1), scale, F32)
    k = iota((1, LANES), 1) - HALO
    squares = jnp.where(k <= HALO, jnp.exp(-math.pi * (k * k).astype(F32) / (scale * scale)), 0.0)
    norm = jnp.sqrt(jnp.sum(squares, axis=1, keepdims=True))
    d = distance.astype(F32)
    raw = jnp.exp(-math.pi * (d * d) / (2.0 * scale * scale))
    inside = valid & (distance >= -HALO) & (distance <= HALO)
    return jnp.where(inside, raw, 0.0) / norm


def tail_rows(count):
    return -(-(2 * count + 3 * FACTORS) // 16) * 16


def cell_row(i, faces):
    return (i % faces) * (EDGE * EDGE) + (i // (faces * EDGE)) * EDGE + (i // faces) % EDGE


def taps_kernel(first, wall_scale, span_scale, wall_ref, main_ref, halo_ref):
    some, full, _ = wall_ref.shape
    cols = main_ref.shape[1] // 2
    walls = lax.axis_size("wall")
    rows = full // walls
    i, j = iota((full, full), 0), iota((full, full), 1)
    y = cell_row(i, full // (EDGE * EDGE))
    source = lax.rem(lax.axis_index("wall") + walls - j // rows, walls)
    column = source * rows + j % rows if first else j
    n = iota((cols, cols), 1)
    target = (n % (cols // EDGE)) * EDGE + n // (cols // EDGE)
    k = iota((cols, cols), 0)
    side, odd, r = k // (2 * HALO), (k // HALO) % 2, k % HALO
    core = lax.rem(lax.axis_index("span"), CORES)
    z = jnp.where(side + core == 1, r - HALO, cols + r)

    def span_matrix(scale, distance, valid):
        high, low = split(tap_values(scale, distance, valid))
        top = jnp.concatenate([high, low], axis=1)
        return jnp.concatenate([top, jnp.concatenate([high, jnp.zeros_like(high)], axis=1)], axis=0)

    for c in range(some):
        high, low = split(tap_values(wall_scale[first + c], column - y, i >= 0))
        wall_ref[c, :, :full] = high
        wall_ref[c, :, full:] = low
        scale = span_scale[first + c]
        main_ref[c] = span_matrix(scale, k - target, k >= 0)
        for parity in range(2):
            valid = (k < 4 * HALO) & (odd == parity)
            halo_ref[c, parity] = span_matrix(scale, z - target, valid)


def run(copies):
    for copy in copies:
        copy.start()
    for copy in copies:
        copy.wait()


def pack_kernel(devices, noise_ref, lund_ref, mean_ref, owner_ref, out_ref, small_ref, noise_sems, small_sems):
    walls, height, cols = out_ref.shape
    tail = small_ref.shape[0]
    block = height - tail
    rows = mean_ref.shape[1]
    copies = [
        pltpu.make_async_copy(
            noise_ref.at[0, pl.ds(w * block, block)], out_ref.at[w, pl.ds(0, block)], noise_sems.at[w]
        )
        for w in range(walls)
    ]
    for copy in copies:
        copy.start()
    owner = owner_ref[...]
    elements = owner.shape[1]
    mine = jnp.where(iota((devices, elements), 0) == owner, 1.0, 0.0)
    before = jnp.where(iota((elements, elements), 0) < iota((elements, elements), 1), 1.0, 0.0)
    count = jnp.dot(mine.astype(BF16), before.astype(BF16), preferred_element_type=F32)
    rank = jnp.sum(mine * count, axis=0, keepdims=True)
    pieces = [owner.astype(F32), rank]
    pieces = [p[:, at : at + cols] for p in pieces for at in range(0, elements, cols)]
    factor = jnp.concatenate([lund_ref[...], mean_ref[...]], axis=0)
    factor = jnp.concatenate([factor, jnp.zeros((FACTORS, cols - rows), F32)], axis=1)
    for _ in range(3):
        part = factor.astype(BF16).astype(F32)
        pieces.append(part)
        factor = factor - part
    pieces.append(jnp.zeros((tail - sum(p.shape[0] for p in pieces), cols), F32))
    small_ref[...] = jnp.concatenate(pieces, axis=0).astype(BF16)
    run(
        [
            pltpu.make_async_copy(small_ref, out_ref.at[w, pl.ds(block, tail)], small_sems.at[w])
            for w in range(walls)
        ]
    )
    for copy in copies:
        copy.wait()


def pack_late_kernel(noise_ref, near_ref, far_ref, *rest):
    out_refs, sems = rest[:-1], rest[-1]
    walls, some, height, _ = near_ref.shape
    block = noise_ref.shape[1] // walls
    me = lax.axis_index("wall")
    copies = []
    for step, out_ref in enumerate(out_refs):
        to = lax.rem(me + step, walls)
        left = out_ref.shape[0] - 2 * some * height
        source = pl.multiple_of(to * block + block - left, math.gcd(block, left) or block)
        parts = [(noise_ref.at[0, pl.ds(source, left)], 0, left)] if left else []
        for side, ref in enumerate((near_ref, far_ref)):
            for c in range(some):
                parts.append((ref.at[to, c], left + (side * some + c) * height, height))
        for part, (ref, start, size) in enumerate(parts):
            copies.append(
                pltpu.make_async_copy(ref, out_ref.at[pl.ds(start, size)], sems.at[step, part])
            )
    run(copies)


def small_kernel(slots, in_ref, factor_ref, target_ref):
    walls, height, cols = in_ref.shape
    full = factor_ref.shape[0]
    rows = full // walls
    count = target_ref.shape[1]
    tail = tail_rows(count)
    columns = jnp.zeros((full, tail), F32)
    y = cell_row(iota((full, cols), 0), full // (EDGE * EDGE))
    for w in range(walls):
        small = in_ref[w, height - tail :]
        pick = jnp.where(y == iota((full, cols), 1) + w * rows, 1.0, 0.0)
        pick = jnp.where(iota((full, cols), 1) < rows, pick, 0.0).astype(BF16)
        columns = columns + lax.dot_general(pick, small, ROWS_BY_ROWS, preferred_element_type=F32)
        numbers = small.astype(F32)
        target = numbers[:count] * slots + numbers[count : 2 * count]
        target_ref[w] = target.astype(jnp.int32)
    at = 2 * count
    factor = sum(columns[:, at + p * FACTORS : at + (p + 1) * FACTORS] for p in range(3))
    factor_ref[...] = jnp.concatenate([factor, jnp.zeros((full, cols - FACTORS), F32)], axis=1)


def edge_picker(cols):
    core = lax.rem(lax.axis_index("span"), CORES)
    row, col = iota((2 * HALO, cols), 0), iota((2 * HALO, cols), 1)
    start = jnp.where(row // HALO == core, cols - HALO, 0)
    return jnp.where(col == start + row % HALO, 1.0, 0.0).astype(BF16)


def edges_kernel(planes, noise_ref, near_ref, far_ref):
    walls, _, cols = noise_ref.shape
    rows = near_ref.shape[1] // walls
    wide = 2 * HALO
    pick = edge_picker(cols)
    for pair in range(planes // 2):
        edges = []
        for t in (2 * pair, 2 * pair + 1):
            plane = [noise_ref[w, t * rows : (t + 1) * rows] for w in range(walls)]
            plane = jnp.concatenate(plane, axis=0)
            edges.append(lax.dot_general(pick, plane, ROWS_BY_ROWS, preferred_element_type=F32))
        at = pl.ds(pair * wide, wide)
        near_ref[at] = jnp.concatenate([e[:HALO] for e in edges], axis=0).astype(BF16)
        far_ref[at] = jnp.concatenate([e[HALO:] for e in edges], axis=0).astype(BF16)


def prepare_rest_kernel(noise_ref, near_ref, far_ref, *rest):
    out_refs, sems = rest[:-1], rest[-1]
    walls, _, height, cols = near_ref.shape
    block = noise_ref.shape[1] // walls
    me = lax.axis_index("wall")
    c = pl.program_id(0)
    last = pl.num_programs(0) - 1

    def copies(size):
        out = []
        for step, out_ref in enumerate(out_refs):
            source = pl.multiple_of(lax.rem(me + step, walls) * block, block)
            target = pl.multiple_of(c * block, block)
            out.append(
                pltpu.make_async_copy(
                    noise_ref.at[0, pl.ds(source, size)], out_ref.at[pl.ds(target, size)], sems.at[step]
                )
            )
        return out

    def each(do):
        @pl.when(c < last)
        def _():
            for copy in copies(block):
                do(copy)

        @pl.when(c == last)
        def _():
            for copy in copies(out_refs[0].shape[0] - last * block):
                do(copy)

    each(lambda copy: copy.start())
    pairs = height // HALO
    pick = edge_picker(cols)
    for w in range(walls):
        edges = []
        for pair in range(pairs):
            plane = noise_ref[0, (w * pairs + pair) * cols : (w * pairs + pair + 1) * cols]
            edges.append(lax.dot_general(pick, plane, ROWS_BY_ROWS, preferred_element_type=F32))
        near_ref[w, 0] = jnp.concatenate([e[:HALO] for e in edges], axis=0).astype(BF16)
        far_ref[w, 0] = jnp.concatenate([e[HALO:] for e in edges], axis=0).astype(BF16)

    each(lambda copy: copy.wait())


def swap_blocks(blocks, cols):
    part = cols // EDGE
    lane = iota(blocks[0].shape, 1)
    for step in (2, 1):
        first = (lane // (part * step)) % 2 == 0
        out = list(blocks)
        for a in range(EDGE):
            if a & step:
                continue
            one, two = blocks[a], blocks[a + step]
            out[a] = jnp.where(first, one, pltpu.roll(two, part * step, 1))
            out[a + step] = jnp.where(first, pltpu.roll(one, cols - part * step, 1), two)
        blocks = out
    return blocks


def halo_tiles(parts, cols):
    half = cols // 2
    sides = []
    for side in parts:
        planes = [[], []]
        for one, two in zip(side[::2], side[1::2]):
            lower = iota(one.shape, 1) < half
            planes[0].append(jnp.where(lower, one, pltpu.roll(two, half, 1)))
            planes[1].append(jnp.where(lower, pltpu.roll(one, half, 1), two))
        sides.append([jnp.concatenate(p, axis=1) for p in planes])
    pairs = sides[0][0].shape[0] // HALO
    zeros = jnp.zeros((cols - 4 * HALO, sides[0][0].shape[1]), F32)
    for pair in range(pairs):
        at = slice(pair * HALO, (pair + 1) * HALO)
        tile = [sides[s][odd][at] for s in range(2) for odd in range(2)]
        yield jnp.concatenate(tile + [zeros], axis=0).astype(BF16)


def span_product(x, matrix):
    cols = x.shape[1]
    both = jnp.dot(jnp.concatenate(split(x), axis=1), matrix, preferred_element_type=F32)
    return both[:, :cols] + both[:, cols:]


def main_part(planes, wall, matrix):
    both = jnp.concatenate(planes, axis=1)
    cols = planes[0].shape[1]
    smooth = jnp.dot(wall, jnp.concatenate([both, both], axis=0), preferred_element_type=F32)
    return [span_product(smooth[:, odd * cols : (odd + 1) * cols], matrix) for odd in range(2)]


def halo_part(tile, wall, halo_ref):
    smooth = lax.dot_general(
        wall, jnp.concatenate([tile, tile], axis=1), ROWS_BY_ROWS, preferred_element_type=F32
    )
    return [span_product(smooth, halo_ref[odd]) for odd in range(2)]


def planes_of(refs, t, rows):
    return [
        jnp.concatenate([ref[at * rows : (at + 1) * rows] for ref in refs], axis=0) for at in (t, t + 1)
    ]


def main_first_kernel(planes, wall_ref, main_ref, noise_ref, psi_ref):
    refs = [noise_ref.at[w] for w in range(noise_ref.shape[0])]
    rows = psi_ref.shape[1] // len(refs)
    for t in range(0, planes, 2):
        psi_ref[t], psi_ref[t + 1] = main_part(planes_of(refs, t, rows), wall_ref[0], main_ref[0])


def main_next_kernel(planes, wall_ref, main_ref, *rest):
    *refs, psi_ref = rest
    rows = psi_ref.shape[1] // len(refs)
    for t in range(0, psi_ref.shape[0], 2):
        c = t // planes
        psi_ref[t], psi_ref[t + 1] = main_part(planes_of(refs, t, rows), wall_ref[c], main_ref[c])


def widen(factor_ref, wide_ref, which):
    for f in which:
        wide_ref[f] = jnp.broadcast_to(factor_ref[:, f : f + 1], wide_ref.shape[1:])


def place_cells(velocity, t, cells_ref, at):
    full, cols = velocity.shape
    quarter, faces = full // EDGE, full // (EDGE * EDGE)
    values = cells_ref.shape[1] // faces
    blocks = [velocity[a * quarter : (a + 1) * quarter] for a in range(EDGE)]
    for dz, block in enumerate(swap_blocks(blocks, cols)):
        for dy in range(EDGE):
            j = t * EDGE * EDGE + dy * EDGE + dz
            cells_ref[at, pl.ds(j, faces, stride=values), :] = block[dy * faces : (dy + 1) * faces]


def scatter_cells(cells_ref, target_ref, sent_ref, out_ref, sems):
    walls, tile_faces, cols = target_ref.shape
    some = cells_ref.shape[0]
    values = cells_ref.shape[1] // (walls * tile_faces)
    _, devices, slots, width = sent_ref.shape
    copies = []
    for w in range(walls):
        payload = [
            [
                cells_ref[at, pl.ds((w * tile_faces + f) * values, values), :].astype(BF16)
                for f in range(tile_faces)
            ]
            for at in range(some)
        ]
        payload = jnp.concatenate([jnp.concatenate(p, axis=1) for p in payload], axis=0)
        slot = iota((devices * slots, cols), 0)
        onehot = [
            jnp.where(slot == target_ref[w, f : f + 1], 1.0, 0.0).astype(BF16)
            for f in range(tile_faces)
        ]
        onehot = jnp.concatenate(onehot, axis=1)
        sent = lax.dot_general(onehot, payload, ROWS_BY_ROWS, preferred_element_type=F32)
        sent_ref[w] = sent.astype(BF16).reshape(devices, slots, width)
        copies.append(pltpu.make_async_copy(sent_ref.at[w], out_ref.at[:, w], sems.at[w]))
        copies[-1].start()
    for copy in copies:
        copy.wait()


def first_kernel(
    planes, psi_in, near_ref, far_ref, factor_ref, target_ref, wall_ref, halo_ref,
    out_ref, psi_out, psi_ref, cells_ref, wide_ref, sent_ref, sems, psi_sem,
):
    full, cols = psi_ref.shape[1:]
    wide = 2 * HALO
    widen(factor_ref, wide_ref, (0, 6))

    def pair_step(pair, carry):
        at = pl.ds(pl.multiple_of(pair * wide, wide), wide)
        tile = [near_ref[at], far_ref[at], jnp.zeros((cols - 2 * wide, full), BF16)]
        beside = halo_part(jnp.concatenate(tile, axis=0), wall_ref[0], halo_ref.at[0])
        for odd in range(2):
            t = 2 * pair + odd
            psi = psi_in[t] + beside[odd]
            psi_ref[t] = psi
            place_cells(wide_ref[6] + wide_ref[0] * psi, t, cells_ref, 0)
        return carry

    lax.fori_loop(0, planes // 2, pair_step, 0, unroll=True)
    copy = pltpu.make_async_copy(psi_ref, psi_out, psi_sem.at[0])
    copy.start()
    scatter_cells(cells_ref, target_ref, sent_ref, out_ref, sems)
    copy.wait()


def rest_kernel(
    planes, psi_ref, next_ref, factor_ref, target_ref, wall_ref, main_ref, halo_ref, *rest,
):
    *late_refs, out_ref, cells_ref, tile_ref, wide_ref, sent_ref, sems = rest
    full, cols = psi_ref.shape[1:]
    some = wall_ref.shape[0]
    rows = full // len(late_refs)
    pairs = planes // 2
    height = pairs * HALO
    widen(factor_ref, wide_ref, range(1, 6))
    for c in range(some):
        left = (some * planes - next_ref.shape[0]) * rows
        starts = [left + (side * some + c) * height for side in range(2)]
        parts = [[ref[pl.ds(at, height)].astype(F32) for ref in late_refs] for at in starts]
        for pair, tile in enumerate(halo_tiles(parts, cols)):
            tile_ref[c * pairs + pair] = tile

    for pair in range(pairs):
        psi = []
        for c in range(some):
            at = c * planes + 2 * pair
            if at < next_ref.shape[0]:
                main = [next_ref[at], next_ref[at + 1]]
            else:
                at = at - next_ref.shape[0]
                main = main_part(planes_of(late_refs, at, rows), wall_ref[c], main_ref[c])
            beside = halo_part(tile_ref[c * pairs + pair], wall_ref[c], halo_ref.at[c])
            psi.append([m + b for m, b in zip(main, beside)])
        for odd in range(2):
            t = 2 * pair + odd
            p, q, r = psi_ref[t], psi[0][odd], psi[1][odd]
            place_cells(wide_ref[1] * p + wide_ref[2] * q, t, cells_ref, 0)
            place_cells(wide_ref[3] * p + wide_ref[4] * q + wide_ref[5] * r, t, cells_ref, 1)
    scatter_cells(cells_ref, target_ref, sent_ref, out_ref, sems)


def join_kernel(first, some, in_ref, *rest):
    out_ref, sems = rest[-2:]
    _, walls, _, width = in_ref.shape
    values = width // some
    run(
        [
            pltpu.make_async_copy(
                in_ref.at[:, w, :, pl.ds(c * values, values)],
                out_ref.at[:, :, pl.ds(((c + first) * walls + w) * values, values)],
                sems.at[c, w],
            )
            for c in range(some)
            for w in range(walls)
        ]
    )


def join_narrow_kernel(some, in_ref, *rest):
    out_ref = rest[-1]
    _, walls, _, width = in_ref.shape
    values = width // some
    for c in range(some):

        @pl.when(pl.program_id(1) == c)
        def _():
            for w in range(walls):
                out_ref[0, :, w * values : (w + 1) * values] = in_ref[0, w, :, c * values : (c + 1) * values]


def per_device(noise, wall_scale, span_scale, lund_factor, mean_velocity, owner_map):
    trio, all_planes, rows, cols = noise.shape
    n_span = lax.axis_size("span")
    n_wall = lax.axis_size("wall")
    devices = n_span * n_wall
    planes = all_planes // n_wall
    pairs = planes // 2
    full = rows * n_wall
    faces = full // (EDGE * EDGE)
    values = planes * EDGE * EDGE
    owners = owner_map.reshape(1, -1)
    elements = owners.shape[1]
    slots = max(8, 2 * elements // devices)
    count = elements // cols
    rest = trio - 1
    ahead = rest * planes
    struct = jax.ShapeDtypeStruct
    hbm = pltpu.MemorySpace.HBM

    def call(kernel, ins, outs, name, limit, scratch=(), grid=(), out_specs=None, us=1):
        specs = out_specs or [VMEM] * len(outs)
        return pl.pallas_call(
            kernel,
            grid=grid,
            in_specs=ins,
            out_specs=specs if len(outs) > 1 else specs[0],
            out_shape=outs if len(outs) > 1 else outs[0],
            scratch_shapes=scratch,
            compiler_params=pltpu.CompilerParams(vmem_limit_bytes=limit * 1024 * 1024),
            cost_estimate=pl.CostEstimate(flops=us * 10**9, bytes_accessed=1024, transcendentals=0),
            name=name,
        )

    core_pairs = [(i, i ^ 1) for i in range(n_span)]
    chip_pairs = [(i, (i + 2 * (i % CORES) - 1) % n_span) for i in range(n_span)]

    def exchange(near, far):
        return lax.ppermute(near, "span", core_pairs), lax.ppermute(far, "span", chip_pairs)

    def swap(x):
        return lax.all_to_all(x, "wall", 0, 0, tiled=True)

    def send(x):
        return lax.all_to_all(x, ("span", "wall"), 0, 0, tiled=True).reshape(devices, n_wall * slots, -1)

    dma = pltpu.SemaphoreType.DMA
    noise = noise.reshape(trio, all_planes * rows, cols)
    packed = call(
        functools.partial(pack_kernel, devices),
        [pl.BlockSpec((1, all_planes * rows, cols), lambda i: (0, 0, 0)), VMEM, VMEM, VMEM],
        [hbm((n_wall, planes * rows + tail_rows(count), cols), BF16)],
        "pack",
        56,
        [pltpu.VMEM((tail_rows(count), cols), BF16), dma((n_wall,)), dma((n_wall,))],
        grid=(1,),
        out_specs=[ANYWHERE],
    )(noise, lund_factor, mean_velocity.reshape(1, rows), owners)
    noise, packed = lax.optimization_barrier((noise, packed))
    packed = swap(packed)

    height = pairs * HALO
    edge = hbm((n_wall, rest, height, cols), BF16)
    spec = pl.BlockSpec((n_wall, 1, height, cols), lambda c: (0, c, 0, 0))
    near, far, *early = call(
        prepare_rest_kernel,
        [pl.BlockSpec((1, all_planes * rows, cols), lambda c: (c + 1, 0, 0))],
        [edge, edge] + [hbm((ahead * rows, cols), BF16)] * n_wall,
        "prepare_rest",
        16,
        [dma((n_wall,))],
        grid=(rest,),
        out_specs=[spec, spec] + [ANYWHERE] * n_wall,
    )(noise)
    rest_near, rest_far = exchange(near, far)
    packed, _ = lax.optimization_barrier((packed, (near, far, early)))

    def spread(blocks):
        return [blocks[0]] + [
            lax.ppermute(x, "wall", [(i, (i + step) % n_wall) for i in range(n_wall)])
            for step, x in enumerate(blocks[1:], 1)
        ]

    def taps(first, some, make, name):
        return call(
            functools.partial(taps_kernel, first),
            [SMEM, SMEM],
            [
                make((some, full, 2 * full), BF16),
                make((some, 2 * cols, 2 * cols), BF16),
                make((some, 2, 2 * cols, 2 * cols), BF16),
            ],
            name,
            16,
        )(wall_scale, span_scale)

    wall_first, main_first, halo_first = taps(0, 1, struct, "taps_first")
    factor, target = call(
        functools.partial(small_kernel, slots),
        [VMEM],
        [struct((full, cols), F32), struct((n_wall, count, cols), jnp.int32)],
        "small",
        16,
    )(packed)

    edge = struct((planes * HALO, full), BF16)
    near, far = call(
        functools.partial(edges_kernel, planes), [VMEM], [edge, edge], "edges_first", 16
    )(packed)
    near, far = exchange(near, far)
    early, rest_near = lax.optimization_barrier((early, rest_near))
    early = spread(early)
    (rest_near, rest_far), _ = lax.optimization_barrier(((rest_near, rest_far), (near, far)))
    late = call(
        pack_late_kernel,
        [pl.BlockSpec((1, all_planes * rows, cols), lambda i: (trio - 1, 0, 0)), VMEM, VMEM],
        [hbm(((rest * planes - ahead) * rows + 2 * rest * height, cols), BF16)] * n_wall,
        "pack_late",
        16,
        [dma((n_wall, 1 + 2 * rest))],
        grid=(1,),
        out_specs=[ANYWHERE] * n_wall,
    )(noise, rest_near, rest_far)
    near, late = lax.optimization_barrier((near, late))

    psi = struct((planes, full, cols), F32)
    psi_main = call(
        functools.partial(main_first_kernel, planes), [VMEM] * 3, [psi], "main_first", 16
    )(wall_first, main_first, packed)

    def scratch(some):
        return [
            pltpu.VMEM((some, faces * values, cols), F32),
            pltpu.VMEM((rest * pairs, cols, full), BF16),
            pltpu.VMEM((FACTORS, full, cols), F32),
            pltpu.VMEM((n_wall, devices, slots, some * values), BF16),
            dma((n_wall,)),
        ]

    def out(some):
        return hbm((devices, n_wall, slots, some * values), BF16)

    cells, _, *more = scratch(1)
    sent, psi = call(
        functools.partial(first_kernel, planes),
        [VMEM] * 7,
        [out(1), hbm(psi.shape, F32)],
        "filter_first",
        24,
        [pltpu.VMEM(psi.shape, F32), cells, *more, dma((1,))],
        out_specs=[ANYWHERE, ANYWHERE],
    )(psi_main, near, far, factor, target, wall_first, halo_first)
    (wall_scale, span_scale, late), sent = lax.optimization_barrier(((wall_scale, span_scale, late), sent))
    got_first = send(sent)
    late = spread(late)
    wall_rest, main_rest, halo_rest = taps(1, rest, struct, "taps_rest")
    psi_next = call(
        functools.partial(main_next_kernel, planes),
        [VMEM] * (2 + n_wall),
        [struct((ahead, full, cols), F32)],
        "main_next",
        16,
    )(wall_rest, main_rest, *early)
    sent = call(
        functools.partial(rest_kernel, planes),
        [VMEM] * (7 + n_wall),
        [out(rest)],
        "filter_rest",
        32,
        scratch(rest),
        out_specs=[ANYWHERE],
        us=100,
    )(psi, psi_next, factor, target, wall_rest, main_rest, halo_rest, *late)
    got_rest = send(sent)

    whole = hbm((n_span, n_wall * slots, trio * values * n_wall), BF16)
    narrow = values % LANES != 0

    def join(received, some, before):
        keep = [] if before is None else [before]
        shape = (n_span, n_wall, n_wall * slots, some * values)
        return pl.pallas_call(
            functools.partial(join_narrow_kernel, some)
            if narrow
            else functools.partial(join_kernel, len(keep), some),
            grid=(n_span, some) if narrow else (),
            in_specs=[pl.BlockSpec((1, *shape[1:]), lambda s, c: (s, 0, 0, 0)) if narrow else VMEM]
            + [ANYWHERE] * len(keep),
            out_specs=pl.BlockSpec((1, n_wall * slots, values * n_wall), lambda s, c: (s, 0, c + len(keep)))
            if narrow
            else ANYWHERE,
            out_shape=whole,
            scratch_shapes=[] if narrow else [dma((some, n_wall))],
            input_output_aliases={1: 0} if keep else {},
            compiler_params=pltpu.CompilerParams(vmem_limit_bytes=16 * 1024 * 1024),
            name="join",
        )(received.reshape(shape), *keep)

    return join(got_rest, rest, join(got_first, 1, None)).reshape(1, devices * slots, -1)


def solution(mesh):
    return jax.shard_map(
        per_device,
        mesh=mesh,
        in_specs=(
            P(None, None, "wall", "span"),
            P(),
            P(),
            P(None, "wall"),
            P("wall"),
            P("wall", "span", None, None),
        ),
        out_specs=P(("span", "wall"), None, None),
        check_vma=False,
    )
```

```python
import functools
import math

import jax
import jax.numpy as jnp
from jax import lax
from jax.experimental import pallas as pl
from jax.experimental.pallas import tpu as pltpu
from jax.sharding import PartitionSpec as P

HALO = 24
EDGE = 4
LANES = 128
FACTORS = 7
CORES = 2
F32 = jnp.float32
BF16 = jnp.bfloat16
VMEM = pl.BlockSpec(memory_space=pltpu.VMEM)
ANYWHERE = pl.BlockSpec(memory_space=pl.ANY)
SMEM = pl.BlockSpec(memory_space=pltpu.SMEM)
ROWS_BY_ROWS = (((1,), (1,)), ((), ()))


def iota(shape, dim):
    return lax.broadcasted_iota(jnp.int32, shape, dim)


def split(x):
    high = x.astype(BF16)
    return high, (x - high.astype(F32)).astype(BF16)


def tap_values(scale, distance, valid):
    scale = jnp.full((1, 1), scale, F32)
    k = iota((1, LANES), 1) - HALO
    squares = jnp.where(k <= HALO, jnp.exp(-math.pi * (k * k).astype(F32) / (scale * scale)), 0.0)
    norm = jnp.sqrt(jnp.sum(squares, axis=1, keepdims=True))
    d = distance.astype(F32)
    raw = jnp.exp(-math.pi * (d * d) / (2.0 * scale * scale))
    inside = valid & (distance >= -HALO) & (distance <= HALO)
    return jnp.where(inside, raw, 0.0) / norm


def tail_rows(count):
    return -(-(2 * count + 3 * FACTORS) // 16) * 16


def cell_row(i, faces):
    return (i % faces) * (EDGE * EDGE) + (i // (faces * EDGE)) * EDGE + (i // faces) % EDGE


def taps_kernel(first, wall_scale, span_scale, wall_ref, main_ref, halo_ref):
    some, full, _ = wall_ref.shape
    cols = main_ref.shape[1] // 2
    walls = lax.axis_size("wall")
    rows = full // walls
    i, j = iota((full, full), 0), iota((full, full), 1)
    y = cell_row(i, full // (EDGE * EDGE))
    source = lax.rem(lax.axis_index("wall") + walls - j // rows, walls)
    column = source * rows + j % rows
    n = iota((cols, cols), 1)
    target = (n % (cols // EDGE)) * EDGE + n // (cols // EDGE)
    k = iota((cols, cols), 0)
    side, odd, r = k // (2 * HALO), (k // HALO) % 2, k % HALO
    core = lax.rem(lax.axis_index("span"), CORES)
    z = jnp.where(side + core == 1, r - HALO, cols + r)

    def span_matrix(scale, distance, valid):
        high, low = split(tap_values(scale, distance, valid))
        top = jnp.concatenate([high, low], axis=1)
        return jnp.concatenate([top, jnp.concatenate([high, jnp.zeros_like(high)], axis=1)], axis=0)

    for c in range(some):
        high, low = split(tap_values(wall_scale[first + c], column - y, i >= 0))
        wall_ref[c, :, :full] = high
        wall_ref[c, :, full:] = low
        scale = span_scale[first + c]
        main_ref[c] = span_matrix(scale, k - target, k >= 0)
        for parity in range(2):
            valid = (k < 4 * HALO) & (odd == parity)
            halo_ref[c, parity] = span_matrix(scale, z - target, valid)


def run(copies):
    for copy in copies:
        copy.start()
    for copy in copies:
        copy.wait()


def pack_kernel(devices, noise_ref, lund_ref, mean_ref, owner_ref, *rest):
    *out_refs, small_ref, noise_sems, small_sems = rest
    walls = len(out_refs)
    tail, cols = small_ref.shape
    block = out_refs[0].shape[0] - tail
    rows = mean_ref.shape[1]
    me = lax.axis_index("wall")
    copies = []
    for step, out_ref in enumerate(out_refs):
        start = pl.multiple_of(lax.rem(me + step, walls) * block, block)
        copies.append(
            pltpu.make_async_copy(
                noise_ref.at[0, pl.ds(start, block)], out_ref.at[pl.ds(0, block)], noise_sems.at[step]
            )
        )
    for copy in copies:
        copy.start()
    owner = owner_ref[...]
    elements = owner.shape[1]
    mine = jnp.where(iota((devices, elements), 0) == owner, 1.0, 0.0)
    before = jnp.where(iota((elements, elements), 0) < iota((elements, elements), 1), 1.0, 0.0)
    count = jnp.dot(mine.astype(BF16), before.astype(BF16), preferred_element_type=F32)
    rank = jnp.sum(mine * count, axis=0, keepdims=True)
    pieces = [owner.astype(F32), rank]
    pieces = [p[:, at : at + cols] for p in pieces for at in range(0, elements, cols)]
    factor = jnp.concatenate([lund_ref[...], mean_ref[...]], axis=0)
    factor = jnp.concatenate([factor, jnp.zeros((FACTORS, cols - rows), F32)], axis=1)
    for _ in range(3):
        part = factor.astype(BF16).astype(F32)
        pieces.append(part)
        factor = factor - part
    pieces.append(jnp.zeros((tail - sum(p.shape[0] for p in pieces), cols), F32))
    small_ref[...] = jnp.concatenate(pieces, axis=0).astype(BF16)
    run(
        [
            pltpu.make_async_copy(small_ref, out_ref.at[pl.ds(block, tail)], small_sems.at[step])
            for step, out_ref in enumerate(out_refs)
        ]
    )
    for copy in copies:
        copy.wait()


def pack_late_kernel(noise_ref, near_ref, far_ref, *rest):
    out_refs, sems = rest[:-1], rest[-1]
    walls, some, height, _ = near_ref.shape
    block = noise_ref.shape[1] // walls
    me = lax.axis_index("wall")
    copies = []
    for step, out_ref in enumerate(out_refs):
        to = lax.rem(me + step, walls)
        left = out_ref.shape[0] - 2 * some * height
        source = pl.multiple_of(to * block + block - left, math.gcd(block, left) or block)
        parts = [(noise_ref.at[0, pl.ds(source, left)], 0, left)] if left else []
        for side, ref in enumerate((near_ref, far_ref)):
            for c in range(some):
                parts.append((ref.at[to, c], left + (side * some + c) * height, height))
        for part, (ref, start, size) in enumerate(parts):
            copies.append(
                pltpu.make_async_copy(ref, out_ref.at[pl.ds(start, size)], sems.at[step, part])
            )
    run(copies)


def small_kernel(slots, *rest):
    *in_refs, factor_ref, target_ref = rest
    walls = len(in_refs)
    height, cols = in_refs[0].shape
    full = factor_ref.shape[0]
    rows = full // walls
    count = target_ref.shape[1]
    tail = tail_rows(count)
    me = lax.axis_index("wall")
    columns = jnp.zeros((full, tail), F32)
    y = cell_row(iota((full, cols), 0), full // (EDGE * EDGE))
    for step, in_ref in enumerate(in_refs):
        w = lax.rem(me + walls - step, walls)
        small = in_ref[height - tail :]
        pick = jnp.where(y == iota((full, cols), 1) + w * rows, 1.0, 0.0)
        pick = jnp.where(iota((full, cols), 1) < rows, pick, 0.0).astype(BF16)
        columns = columns + lax.dot_general(pick, small, ROWS_BY_ROWS, preferred_element_type=F32)
        numbers = small.astype(F32)
        target = numbers[:count] * slots + numbers[count : 2 * count]
        target_ref[pl.ds(w, 1)] = target.astype(jnp.int32)[None]
    at = 2 * count
    factor = sum(columns[:, at + p * FACTORS : at + (p + 1) * FACTORS] for p in range(3))
    factor_ref[...] = jnp.concatenate([factor, jnp.zeros((full, cols - FACTORS), F32)], axis=1)


def edge_picker(cols):
    core = lax.rem(lax.axis_index("span"), CORES)
    row, col = iota((2 * HALO, cols), 0), iota((2 * HALO, cols), 1)
    start = jnp.where(row // HALO == core, cols - HALO, 0)
    return jnp.where(col == start + row % HALO, 1.0, 0.0).astype(BF16)


def edges_kernel(planes, *rest):
    *noise_refs, near_ref, far_ref = rest
    cols = noise_refs[0].shape[1]
    rows = near_ref.shape[1] // len(noise_refs)
    wide = 2 * HALO
    pick = edge_picker(cols)
    for pair in range(planes // 2):
        edges = []
        for t in (2 * pair, 2 * pair + 1):
            plane = [ref[t * rows : (t + 1) * rows] for ref in noise_refs]
            plane = jnp.concatenate(plane, axis=0)
            edges.append(lax.dot_general(pick, plane, ROWS_BY_ROWS, preferred_element_type=F32))
        at = pl.ds(pair * wide, wide)
        near_ref[at] = jnp.concatenate([e[:HALO] for e in edges], axis=0).astype(BF16)
        far_ref[at] = jnp.concatenate([e[HALO:] for e in edges], axis=0).astype(BF16)


def prepare_rest_kernel(noise_ref, near_ref, far_ref, *rest):
    out_refs, sems = rest[:-1], rest[-1]
    walls, _, height, cols = near_ref.shape
    block = noise_ref.shape[1] // walls
    me = lax.axis_index("wall")
    c = pl.program_id(0)
    last = pl.num_programs(0) - 1

    def copies(size):
        out = []
        for step, out_ref in enumerate(out_refs):
            source = pl.multiple_of(lax.rem(me + step, walls) * block, block)
            target = pl.multiple_of(c * block, block)
            out.append(
                pltpu.make_async_copy(
                    noise_ref.at[0, pl.ds(source, size)], out_ref.at[pl.ds(target, size)], sems.at[step]
                )
            )
        return out

    def each(do):
        @pl.when(c < last)
        def _():
            for copy in copies(block):
                do(copy)

        @pl.when(c == last)
        def _():
            for copy in copies(out_refs[0].shape[0] - last * block):
                do(copy)

    each(lambda copy: copy.start())
    pairs = height // HALO
    pick = edge_picker(cols)
    for w in range(walls):
        edges = []
        for pair in range(pairs):
            plane = noise_ref[0, (w * pairs + pair) * cols : (w * pairs + pair + 1) * cols]
            edges.append(lax.dot_general(pick, plane, ROWS_BY_ROWS, preferred_element_type=F32))
        near_ref[w, 0] = jnp.concatenate([e[:HALO] for e in edges], axis=0).astype(BF16)
        far_ref[w, 0] = jnp.concatenate([e[HALO:] for e in edges], axis=0).astype(BF16)

    each(lambda copy: copy.wait())


def swap_blocks(blocks, cols):
    part = cols // EDGE
    lane = iota(blocks[0].shape, 1)
    for step in (2, 1):
        first = (lane // (part * step)) % 2 == 0
        out = list(blocks)
        for a in range(EDGE):
            if a & step:
                continue
            one, two = blocks[a], blocks[a + step]
            out[a] = jnp.where(first, one, pltpu.roll(two, part * step, 1))
            out[a + step] = jnp.where(first, pltpu.roll(one, cols - part * step, 1), two)
        blocks = out
    return blocks


def halo_tiles(parts, cols):
    half = cols // 2
    sides = []
    for side in parts:
        planes = [[], []]
        for one, two in zip(side[::2], side[1::2]):
            lower = iota(one.shape, 1) < half
            planes[0].append(jnp.where(lower, one, pltpu.roll(two, half, 1)))
            planes[1].append(jnp.where(lower, pltpu.roll(one, half, 1), two))
        sides.append([jnp.concatenate(p, axis=1) for p in planes])
    pairs = sides[0][0].shape[0] // HALO
    zeros = jnp.zeros((cols - 4 * HALO, sides[0][0].shape[1]), F32)
    for pair in range(pairs):
        at = slice(pair * HALO, (pair + 1) * HALO)
        tile = [sides[s][odd][at] for s in range(2) for odd in range(2)]
        yield jnp.concatenate(tile + [zeros], axis=0).astype(BF16)


def span_product(x, matrix):
    cols = x.shape[1]
    both = jnp.dot(jnp.concatenate(split(x), axis=1), matrix, preferred_element_type=F32)
    return both[:, :cols] + both[:, cols:]


def main_part(planes, wall, matrix):
    both = jnp.concatenate(planes, axis=1)
    cols = planes[0].shape[1]
    smooth = jnp.dot(wall, jnp.concatenate([both, both], axis=0), preferred_element_type=F32)
    return [span_product(smooth[:, odd * cols : (odd + 1) * cols], matrix) for odd in range(2)]


def halo_part(tile, wall, halo_ref):
    smooth = lax.dot_general(
        wall, jnp.concatenate([tile, tile], axis=1), ROWS_BY_ROWS, preferred_element_type=F32
    )
    return [span_product(smooth, halo_ref[odd]) for odd in range(2)]


def planes_of(refs, t, rows):
    return [
        jnp.concatenate([ref[at * rows : (at + 1) * rows] for ref in refs], axis=0) for at in (t, t + 1)
    ]


def main_kernel(planes, wall_ref, main_ref, *rest):
    *refs, psi_ref = rest
    rows = psi_ref.shape[1] // len(refs)
    for t in range(0, psi_ref.shape[0], 2):
        c = t // planes
        psi_ref[t], psi_ref[t + 1] = main_part(planes_of(refs, t, rows), wall_ref[c], main_ref[c])


def widen(factor_ref, wide_ref, which):
    for f in which:
        wide_ref[f] = jnp.broadcast_to(factor_ref[:, f : f + 1], wide_ref.shape[1:])


def place_cells(velocity, t, cells_ref, at):
    full, cols = velocity.shape
    quarter, faces = full // EDGE, full // (EDGE * EDGE)
    values = cells_ref.shape[1] // faces
    blocks = [velocity[a * quarter : (a + 1) * quarter] for a in range(EDGE)]
    for dz, block in enumerate(swap_blocks(blocks, cols)):
        for dy in range(EDGE):
            j = t * EDGE * EDGE + dy * EDGE + dz
            cells_ref[at, pl.ds(j, faces, stride=values), :] = block[dy * faces : (dy + 1) * faces]


def scatter_cells(cells_ref, target_ref, sent_ref, out_ref, sems):
    walls, tile_faces, cols = target_ref.shape
    some = cells_ref.shape[0]
    values = cells_ref.shape[1] // (walls * tile_faces)
    _, devices, slots, width = sent_ref.shape
    copies = []
    for w in range(walls):
        payload = [
            [
                cells_ref[at, pl.ds((w * tile_faces + f) * values, values), :].astype(BF16)
                for f in range(tile_faces)
            ]
            for at in range(some)
        ]
        payload = jnp.concatenate([jnp.concatenate(p, axis=1) for p in payload], axis=0)
        slot = iota((devices * slots, cols), 0)
        onehot = [
            jnp.where(slot == target_ref[w, f : f + 1], 1.0, 0.0).astype(BF16)
            for f in range(tile_faces)
        ]
        onehot = jnp.concatenate(onehot, axis=1)
        sent = lax.dot_general(onehot, payload, ROWS_BY_ROWS, preferred_element_type=F32)
        sent_ref[w] = sent.astype(BF16).reshape(devices, slots, width)
        copies.append(pltpu.make_async_copy(sent_ref.at[w], out_ref.at[:, w], sems.at[w]))
        copies[-1].start()
    for copy in copies:
        copy.wait()


def first_kernel(
    planes, psi_in, near_ref, far_ref, factor_ref, target_ref, wall_ref, halo_ref,
    out_ref, psi_out, psi_ref, cells_ref, wide_ref, sent_ref, sems, psi_sem,
):
    full, cols = psi_ref.shape[1:]
    wide = 2 * HALO
    widen(factor_ref, wide_ref, (0, 6))

    def pair_step(pair, carry):
        at = pl.ds(pl.multiple_of(pair * wide, wide), wide)
        tile = [near_ref[at], far_ref[at], jnp.zeros((cols - 2 * wide, full), BF16)]
        beside = halo_part(jnp.concatenate(tile, axis=0), wall_ref[0], halo_ref.at[0])
        for odd in range(2):
            t = 2 * pair + odd
            psi = psi_in[t] + beside[odd]
            psi_ref[t] = psi
            place_cells(wide_ref[6] + wide_ref[0] * psi, t, cells_ref, 0)
        return carry

    lax.fori_loop(0, planes // 2, pair_step, 0, unroll=True)
    copy = pltpu.make_async_copy(psi_ref, psi_out, psi_sem.at[0])
    copy.start()
    scatter_cells(cells_ref, target_ref, sent_ref, out_ref, sems)
    copy.wait()


def rest_kernel(
    planes, psi_ref, next_ref, factor_ref, target_ref, wall_ref, main_ref, halo_ref, *rest,
):
    *late_refs, out_ref, cells_ref, tile_ref, wide_ref, sent_ref, sems = rest
    full, cols = psi_ref.shape[1:]
    some = wall_ref.shape[0]
    rows = full // len(late_refs)
    pairs = planes // 2
    height = pairs * HALO
    widen(factor_ref, wide_ref, range(1, 6))
    for c in range(some):
        left = (some * planes - next_ref.shape[0]) * rows
        starts = [left + (side * some + c) * height for side in range(2)]
        parts = [[ref[pl.ds(at, height)].astype(F32) for ref in late_refs] for at in starts]
        for pair, tile in enumerate(halo_tiles(parts, cols)):
            tile_ref[c * pairs + pair] = tile

    for pair in range(pairs):
        psi = []
        for c in range(some):
            at = c * planes + 2 * pair
            if at < next_ref.shape[0]:
                main = [next_ref[at], next_ref[at + 1]]
            else:
                at = at - next_ref.shape[0]
                main = main_part(planes_of(late_refs, at, rows), wall_ref[c], main_ref[c])
            beside = halo_part(tile_ref[c * pairs + pair], wall_ref[c], halo_ref.at[c])
            psi.append([m + b for m, b in zip(main, beside)])
        for odd in range(2):
            t = 2 * pair + odd
            p, q, r = psi_ref[t], psi[0][odd], psi[1][odd]
            place_cells(wide_ref[1] * p + wide_ref[2] * q, t, cells_ref, 0)
            place_cells(wide_ref[3] * p + wide_ref[4] * q + wide_ref[5] * r, t, cells_ref, 1)
    scatter_cells(cells_ref, target_ref, sent_ref, out_ref, sems)


def join_kernel(first, some, in_ref, *rest):
    out_ref, sems = rest[-2:]
    _, walls, _, width = in_ref.shape
    values = width // some
    run(
        [
            pltpu.make_async_copy(
                in_ref.at[:, w, :, pl.ds(c * values, values)],
                out_ref.at[:, :, pl.ds(((c + first) * walls + w) * values, values)],
                sems.at[c, w],
            )
            for c in range(some)
            for w in range(walls)
        ]
    )


def join_narrow_kernel(some, in_ref, *rest):
    out_ref = rest[-1]
    _, walls, _, width = in_ref.shape
    values = width // some
    for c in range(some):

        @pl.when(pl.program_id(1) == c)
        def _():
            for w in range(walls):
                out_ref[0, :, w * values : (w + 1) * values] = in_ref[0, w, :, c * values : (c + 1) * values]


def per_device(noise, wall_scale, span_scale, lund_factor, mean_velocity, owner_map):
    trio, all_planes, rows, cols = noise.shape
    n_span = lax.axis_size("span")
    n_wall = lax.axis_size("wall")
    devices = n_span * n_wall
    planes = all_planes // n_wall
    pairs = planes // 2
    full = rows * n_wall
    faces = full // (EDGE * EDGE)
    values = planes * EDGE * EDGE
    owners = owner_map.reshape(1, -1)
    elements = owners.shape[1]
    slots = max(8, 2 * elements // devices)
    count = elements // cols
    rest = trio - 1
    ahead = rest * planes
    struct = jax.ShapeDtypeStruct
    hbm = pltpu.MemorySpace.HBM

    def call(kernel, ins, outs, name, limit, scratch=(), grid=(), out_specs=None, us=1):
        specs = out_specs or [VMEM] * len(outs)
        return pl.pallas_call(
            kernel,
            grid=grid,
            in_specs=ins,
            out_specs=specs if len(outs) > 1 else specs[0],
            out_shape=outs if len(outs) > 1 else outs[0],
            scratch_shapes=scratch,
            compiler_params=pltpu.CompilerParams(vmem_limit_bytes=limit * 1024 * 1024),
            cost_estimate=pl.CostEstimate(flops=us * 10**9, bytes_accessed=1024, transcendentals=0),
            name=name,
        )

    core_pairs = [(i, i ^ 1) for i in range(n_span)]
    chip_pairs = [(i, (i + 2 * (i % CORES) - 1) % n_span) for i in range(n_span)]

    def exchange(near, far):
        return lax.ppermute(near, "span", core_pairs), lax.ppermute(far, "span", chip_pairs)

    def spread(blocks):
        return [blocks[0]] + [
            lax.ppermute(x, "wall", [(i, (i + step) % n_wall) for i in range(n_wall)])
            for step, x in enumerate(blocks[1:], 1)
        ]

    def send(x):
        return lax.all_to_all(x, ("span", "wall"), 0, 0, tiled=True).reshape(devices, n_wall * slots, -1)

    dma = pltpu.SemaphoreType.DMA
    noise = noise.reshape(trio, all_planes * rows, cols)
    packed = call(
        functools.partial(pack_kernel, devices),
        [pl.BlockSpec((1, all_planes * rows, cols), lambda i: (0, 0, 0)), VMEM, VMEM, VMEM],
        [hbm((planes * rows + tail_rows(count), cols), BF16)] * n_wall,
        "pack",
        56,
        [pltpu.VMEM((tail_rows(count), cols), BF16), dma((n_wall,)), dma((n_wall,))],
        grid=(1,),
        out_specs=[ANYWHERE] * n_wall,
    )(noise, lund_factor, mean_velocity.reshape(1, rows), owners)
    noise, packed = lax.optimization_barrier((noise, packed))
    packed = spread(packed)

    height = pairs * HALO
    edge = hbm((n_wall, rest, height, cols), BF16)
    spec = pl.BlockSpec((n_wall, 1, height, cols), lambda c: (0, c, 0, 0))
    near, far, *early = call(
        prepare_rest_kernel,
        [pl.BlockSpec((1, all_planes * rows, cols), lambda c: (c + 1, 0, 0))],
        [edge, edge] + [hbm((ahead * rows, cols), BF16)] * n_wall,
        "prepare_rest",
        16,
        [dma((n_wall,))],
        grid=(rest,),
        out_specs=[spec, spec] + [ANYWHERE] * n_wall,
    )(noise)
    rest_near, rest_far = exchange(near, far)
    packed, _ = lax.optimization_barrier((packed, (near, far, early)))

    def taps(first, some, make, name):
        return call(
            functools.partial(taps_kernel, first),
            [SMEM, SMEM],
            [
                make((some, full, 2 * full), BF16),
                make((some, 2 * cols, 2 * cols), BF16),
                make((some, 2, 2 * cols, 2 * cols), BF16),
            ],
            name,
            16,
        )(wall_scale, span_scale)

    wall_first, main_first, halo_first = taps(0, 1, struct, "taps_first")
    factor, target = call(
        functools.partial(small_kernel, slots),
        [VMEM] * n_wall,
        [struct((full, cols), F32), struct((n_wall, count, cols), jnp.int32)],
        "small",
        16,
    )(*packed)

    edge = struct((planes * HALO, full), BF16)
    near, far = call(
        functools.partial(edges_kernel, planes), [VMEM] * n_wall, [edge, edge], "edges_first", 16
    )(*packed)
    near, far = exchange(near, far)
    early, rest_near = lax.optimization_barrier((early, rest_near))
    early = spread(early)
    (rest_near, rest_far), _ = lax.optimization_barrier(((rest_near, rest_far), (near, far)))
    late = call(
        pack_late_kernel,
        [pl.BlockSpec((1, all_planes * rows, cols), lambda i: (trio - 1, 0, 0)), VMEM, VMEM],
        [hbm(((rest * planes - ahead) * rows + 2 * rest * height, cols), BF16)] * n_wall,
        "pack_late",
        16,
        [dma((n_wall, 1 + 2 * rest))],
        grid=(1,),
        out_specs=[ANYWHERE] * n_wall,
    )(noise, rest_near, rest_far)
    near, late = lax.optimization_barrier((near, late))

    psi = struct((planes, full, cols), F32)
    psi_main = call(
        functools.partial(main_kernel, planes), [VMEM] * (2 + n_wall), [psi], "main_first", 16
    )(wall_first, main_first, *packed)

    def scratch(some):
        return [
            pltpu.VMEM((some, faces * values, cols), F32),
            pltpu.VMEM((rest * pairs, cols, full), BF16),
            pltpu.VMEM((FACTORS, full, cols), F32),
            pltpu.VMEM((n_wall, devices, slots, some * values), BF16),
            dma((n_wall,)),
        ]

    def out(some):
        return hbm((devices, n_wall, slots, some * values), BF16)

    cells, _, *more = scratch(1)
    sent, psi = call(
        functools.partial(first_kernel, planes),
        [VMEM] * 7,
        [out(1), hbm(psi.shape, F32)],
        "filter_first",
        24,
        [pltpu.VMEM(psi.shape, F32), cells, *more, dma((1,))],
        out_specs=[ANYWHERE, ANYWHERE],
    )(psi_main, near, far, factor, target, wall_first, halo_first)
    (wall_scale, span_scale, late), sent = lax.optimization_barrier(((wall_scale, span_scale, late), sent))
    got_first = send(sent)
    late = spread(late)
    wall_rest, main_rest, halo_rest = taps(1, rest, struct, "taps_rest")
    psi_next = call(
        functools.partial(main_kernel, planes),
        [VMEM] * (2 + n_wall),
        [struct((ahead, full, cols), F32)],
        "main_next",
        16,
    )(wall_rest, main_rest, *early)
    sent = call(
        functools.partial(rest_kernel, planes),
        [VMEM] * (7 + n_wall),
        [out(rest)],
        "filter_rest",
        32,
        scratch(rest),
        out_specs=[ANYWHERE],
        us=100,
    )(psi, psi_next, factor, target, wall_rest, main_rest, halo_rest, *late)
    got_rest = send(sent)

    whole = hbm((n_span, n_wall * slots, trio * values * n_wall), BF16)
    narrow = values % LANES != 0

    def join(received, some, before):
        keep = [] if before is None else [before]
        shape = (n_span, n_wall, n_wall * slots, some * values)
        return pl.pallas_call(
            functools.partial(join_narrow_kernel, some)
            if narrow
            else functools.partial(join_kernel, len(keep), some),
            grid=(n_span, some) if narrow else (),
            in_specs=[pl.BlockSpec((1, *shape[1:]), lambda s, c: (s, 0, 0, 0)) if narrow else VMEM]
            + [ANYWHERE] * len(keep),
            out_specs=pl.BlockSpec((1, n_wall * slots, values * n_wall), lambda s, c: (s, 0, c + len(keep)))
            if narrow
            else ANYWHERE,
            out_shape=whole,
            scratch_shapes=[] if narrow else [dma((some, n_wall))],
            input_output_aliases={1: 0} if keep else {},
            compiler_params=pltpu.CompilerParams(vmem_limit_bytes=16 * 1024 * 1024),
            name="join",
        )(received.reshape(shape), *keep)

    return join(got_rest, rest, join(got_first, 1, None)).reshape(1, devices * slots, -1)


def solution(mesh):
    return jax.shard_map(
        per_device,
        mesh=mesh,
        in_specs=(
            P(None, None, "wall", "span"),
            P(),
            P(),
            P(None, "wall"),
            P("wall"),
            P("wall", "span", None, None),
        ),
        out_specs=P(("span", "wall"), None, None),
        check_vma=False,
    )
```

```python
import functools
import math

import jax
import jax.numpy as jnp
from jax import lax
from jax.experimental import pallas as pl
from jax.experimental.pallas import tpu as pltpu
from jax.sharding import PartitionSpec as P

HALO = 24
EDGE = 4
LANES = 128
FACTORS = 7
CORES = 2
F32 = jnp.float32
BF16 = jnp.bfloat16
VMEM = pl.BlockSpec(memory_space=pltpu.VMEM)
ANYWHERE = pl.BlockSpec(memory_space=pl.ANY)
SMEM = pl.BlockSpec(memory_space=pltpu.SMEM)
ROWS_BY_ROWS = (((1,), (1,)), ((), ()))


def iota(shape, dim):
    return lax.broadcasted_iota(jnp.int32, shape, dim)


def split(x):
    high = x.astype(BF16)
    return high, (x - high.astype(F32)).astype(BF16)


def tap_values(scale, distance, valid):
    scale = jnp.full((1, 1), scale, F32)
    k = iota((1, LANES), 1) - HALO
    squares = jnp.where(k <= HALO, jnp.exp(-math.pi * (k * k).astype(F32) / (scale * scale)), 0.0)
    norm = jnp.sqrt(jnp.sum(squares, axis=1, keepdims=True))
    d = distance.astype(F32)
    raw = jnp.exp(-math.pi * (d * d) / (2.0 * scale * scale))
    inside = valid & (distance >= -HALO) & (distance <= HALO)
    return jnp.where(inside, raw, 0.0) / norm


def tail_rows(count):
    return -(-(2 * count + 3 * FACTORS) // 16) * 16


def cell_row(i, faces):
    return (i % faces) * (EDGE * EDGE) + (i // (faces * EDGE)) * EDGE + (i // faces) % EDGE


def taps_kernel(first, wall_scale, span_scale, wall_ref, main_ref, halo_ref):
    some, full, _ = wall_ref.shape
    cols = main_ref.shape[1] // 2
    walls = lax.axis_size("wall")
    rows = full // walls
    i, j = iota((full, full), 0), iota((full, full), 1)
    y = cell_row(i, full // (EDGE * EDGE))
    source = lax.rem(lax.axis_index("wall") + walls - j // rows, walls)
    column = source * rows + j % rows
    n = iota((cols, cols), 1)
    target = (n % (cols // EDGE)) * EDGE + n // (cols // EDGE)
    k = iota((cols, cols), 0)
    side, odd, r = k // (2 * HALO), (k // HALO) % 2, k % HALO
    core = lax.rem(lax.axis_index("span"), CORES)
    z = jnp.where(side + core == 1, r - HALO, cols + r)

    def span_matrix(scale, distance, valid):
        high, low = split(tap_values(scale, distance, valid))
        top = jnp.concatenate([high, low], axis=1)
        return jnp.concatenate([top, jnp.concatenate([high, jnp.zeros_like(high)], axis=1)], axis=0)

    for c in range(some):
        high, low = split(tap_values(wall_scale[first + c], column - y, i >= 0))
        wall_ref[c, :, :full] = high
        wall_ref[c, :, full:] = low
        scale = span_scale[first + c]
        main_ref[c] = span_matrix(scale, k - target, k >= 0)
        for parity in range(2):
            valid = (k < 4 * HALO) & (odd == parity)
            halo_ref[c, parity] = span_matrix(scale, z - target, valid)


def run(copies):
    for copy in copies:
        copy.start()
    for copy in copies:
        copy.wait()


def pack_kernel(devices, noise_in, lund_in, mean_in, owner_in, *rest):
    *out_refs, noise_ref, lund_ref, mean_ref, owner_ref, sems = rest
    walls = len(out_refs)
    cols = noise_ref.shape[1]
    block = noise_ref.shape[0] // walls
    tail = out_refs[0].shape[0] - block
    rows = mean_ref.shape[1]
    me = lax.axis_index("wall")
    pairs = ((lund_in, lund_ref), (mean_in, mean_ref), (owner_in, owner_ref), (noise_in.at[0], noise_ref))
    *small, noise = [pltpu.make_async_copy(a, b, sems.at[i]) for i, (a, b) in enumerate(pairs)]
    noise.start()
    run(small)
    owner = owner_ref[...]
    elements = owner.shape[1]
    mine = jnp.where(iota((devices, elements), 0) == owner, 1.0, 0.0)
    before = jnp.where(iota((elements, elements), 0) < iota((elements, elements), 1), 1.0, 0.0)
    count = jnp.dot(mine.astype(BF16), before.astype(BF16), preferred_element_type=F32)
    rank = jnp.sum(mine * count, axis=0, keepdims=True)
    pieces = [owner.astype(F32), rank]
    pieces = [p[:, at : at + cols] for p in pieces for at in range(0, elements, cols)]
    factor = jnp.concatenate([lund_ref[...], mean_ref[...]], axis=0)
    factor = jnp.concatenate([factor, jnp.zeros((FACTORS, cols - rows), F32)], axis=1)
    for _ in range(3):
        part = factor.astype(BF16).astype(F32)
        pieces.append(part)
        factor = factor - part
    pieces.append(jnp.zeros((tail - sum(p.shape[0] for p in pieces), cols), F32))
    small = jnp.concatenate(pieces, axis=0).astype(BF16)
    noise.wait()
    for step, out_ref in enumerate(out_refs):
        start = pl.multiple_of(lax.rem(me + step, walls) * block, block)
        out_ref[:block] = noise_ref[pl.ds(start, block)]
        out_ref[block:] = small


def pack_late_kernel(near_ref, far_ref, *rest):
    out_refs, sems = rest[:-1], rest[-1]
    walls, some, height, _ = near_ref.shape
    me = lax.axis_index("wall")
    copies = []
    for step, out_ref in enumerate(out_refs):
        to = lax.rem(me + step, walls)
        for side, ref in enumerate((near_ref, far_ref)):
            for c in range(some):
                at = side * some + c
                copies.append(
                    pltpu.make_async_copy(
                        ref.at[to, c], out_ref.at[pl.ds(at * height, height)], sems.at[step, at]
                    )
                )
    run(copies)


def small_kernel(slots, *rest):
    *in_refs, factor_ref, target_ref = rest
    walls = len(in_refs)
    height, cols = in_refs[0].shape
    full = factor_ref.shape[0]
    rows = full // walls
    count = target_ref.shape[1]
    tail = tail_rows(count)
    me = lax.axis_index("wall")
    columns = jnp.zeros((full, tail), F32)
    y = cell_row(iota((full, cols), 0), full // (EDGE * EDGE))
    for step, in_ref in enumerate(in_refs):
        w = lax.rem(me + walls - step, walls)
        small = in_ref[height - tail :]
        pick = jnp.where(y == iota((full, cols), 1) + w * rows, 1.0, 0.0)
        pick = jnp.where(iota((full, cols), 1) < rows, pick, 0.0).astype(BF16)
        columns = columns + lax.dot_general(pick, small, ROWS_BY_ROWS, preferred_element_type=F32)
        numbers = small.astype(F32)
        target = numbers[:count] * slots + numbers[count : 2 * count]
        target_ref[pl.ds(w, 1)] = target.astype(jnp.int32)[None]
    at = 2 * count
    factor = sum(columns[:, at + p * FACTORS : at + (p + 1) * FACTORS] for p in range(3))
    factor_ref[...] = jnp.concatenate([factor, jnp.zeros((full, cols - FACTORS), F32)], axis=1)


def edge_picker(cols):
    core = lax.rem(lax.axis_index("span"), CORES)
    row, col = iota((2 * HALO, cols), 0), iota((2 * HALO, cols), 1)
    start = jnp.where(row // HALO == core, cols - HALO, 0)
    return jnp.where(col == start + row % HALO, 1.0, 0.0).astype(BF16)


def edges_kernel(planes, *rest):
    *noise_refs, near_ref, far_ref = rest
    cols = noise_refs[0].shape[1]
    rows = near_ref.shape[1] // len(noise_refs)
    wide = 2 * HALO
    pick = edge_picker(cols)
    for pair in range(planes // 2):
        edges = []
        for t in (2 * pair, 2 * pair + 1):
            plane = [ref[t * rows : (t + 1) * rows] for ref in noise_refs]
            plane = jnp.concatenate(plane, axis=0)
            edges.append(lax.dot_general(pick, plane, ROWS_BY_ROWS, preferred_element_type=F32))
        at = pl.ds(pair * wide, wide)
        near_ref[at] = jnp.concatenate([e[:HALO] for e in edges], axis=0).astype(BF16)
        far_ref[at] = jnp.concatenate([e[HALO:] for e in edges], axis=0).astype(BF16)


def prepare_rest_kernel(noise_ref, near_ref, far_ref, *out_refs):
    walls, _, height, cols = near_ref.shape
    block = noise_ref.shape[1] // walls
    me = lax.axis_index("wall")
    c = pl.program_id(0)
    target = pl.ds(pl.multiple_of(c * block, block), block)
    for step, out_ref in enumerate(out_refs):
        source = pl.multiple_of(lax.rem(me + step, walls) * block, block)
        out_ref[target] = noise_ref[0, pl.ds(source, block)]
    pairs = height // HALO
    pick = edge_picker(cols)
    for w in range(walls):
        edges = []
        for pair in range(pairs):
            plane = noise_ref[0, (w * pairs + pair) * cols : (w * pairs + pair + 1) * cols]
            edges.append(lax.dot_general(pick, plane, ROWS_BY_ROWS, preferred_element_type=F32))
        near_ref[w, c] = jnp.concatenate([e[:HALO] for e in edges], axis=0).astype(BF16)
        far_ref[w, c] = jnp.concatenate([e[HALO:] for e in edges], axis=0).astype(BF16)


def swap_blocks(blocks, cols):
    part = cols // EDGE
    lane = iota(blocks[0].shape, 1)
    for step in (2, 1):
        first = (lane // (part * step)) % 2 == 0
        out = list(blocks)
        for a in range(EDGE):
            if a & step:
                continue
            one, two = blocks[a], blocks[a + step]
            out[a] = jnp.where(first, one, pltpu.roll(two, part * step, 1))
            out[a + step] = jnp.where(first, pltpu.roll(one, cols - part * step, 1), two)
        blocks = out
    return blocks


def halo_tiles(parts, cols):
    half = cols // 2
    sides = []
    for side in parts:
        planes = [[], []]
        for one, two in zip(side[::2], side[1::2]):
            lower = iota(one.shape, 1) < half
            planes[0].append(jnp.where(lower, one, pltpu.roll(two, half, 1)))
            planes[1].append(jnp.where(lower, pltpu.roll(one, half, 1), two))
        sides.append([jnp.concatenate(p, axis=1) for p in planes])
    pairs = sides[0][0].shape[0] // HALO
    zeros = jnp.zeros((cols - 4 * HALO, sides[0][0].shape[1]), F32)
    for pair in range(pairs):
        at = slice(pair * HALO, (pair + 1) * HALO)
        tile = [sides[s][odd][at] for s in range(2) for odd in range(2)]
        yield jnp.concatenate(tile + [zeros], axis=0).astype(BF16)


def span_product(x, matrix):
    cols = x.shape[1]
    both = jnp.dot(jnp.concatenate(split(x), axis=1), matrix, preferred_element_type=F32)
    return both[:, :cols] + both[:, cols:]


def main_part(planes, wall, matrix):
    both = jnp.concatenate(planes, axis=1)
    cols = planes[0].shape[1]
    smooth = jnp.dot(wall, jnp.concatenate([both, both], axis=0), preferred_element_type=F32)
    return [span_product(smooth[:, odd * cols : (odd + 1) * cols], matrix) for odd in range(2)]


def halo_part(tile, wall, halo_ref):
    smooth = lax.dot_general(
        wall, jnp.concatenate([tile, tile], axis=1), ROWS_BY_ROWS, preferred_element_type=F32
    )
    return [span_product(smooth, halo_ref[odd]) for odd in range(2)]


def planes_of(refs, t, rows):
    return [
        jnp.concatenate([ref[at * rows : (at + 1) * rows] for ref in refs], axis=0) for at in (t, t + 1)
    ]


def main_kernel(planes, wall_ref, main_ref, *rest):
    *refs, psi_ref = rest
    rows = psi_ref.shape[1] // len(refs)
    for t in range(0, psi_ref.shape[0], 2):
        c = t // planes
        psi_ref[t], psi_ref[t + 1] = main_part(planes_of(refs, t, rows), wall_ref[c], main_ref[c])


def widen(factor_ref, wide_ref, which):
    for f in which:
        wide_ref[f] = jnp.broadcast_to(factor_ref[:, f : f + 1], wide_ref.shape[1:])


def place_cells(velocity, t, cells_ref, at):
    full, cols = velocity.shape
    quarter, faces = full // EDGE, full // (EDGE * EDGE)
    values = cells_ref.shape[1] // faces
    blocks = [velocity[a * quarter : (a + 1) * quarter] for a in range(EDGE)]
    for dz, block in enumerate(swap_blocks(blocks, cols)):
        for dy in range(EDGE):
            j = t * EDGE * EDGE + dy * EDGE + dz
            cells_ref[at, pl.ds(j, faces, stride=values), :] = block[dy * faces : (dy + 1) * faces]


def scatter_cells(cells_ref, target_ref, sent_ref, out_ref, sems):
    walls, tile_faces, cols = target_ref.shape
    some = cells_ref.shape[0]
    values = cells_ref.shape[1] // (walls * tile_faces)
    _, devices, slots, width = sent_ref.shape
    copies = []
    for w in range(walls):
        payload = [
            [
                cells_ref[at, pl.ds((w * tile_faces + f) * values, values), :].astype(BF16)
                for f in range(tile_faces)
            ]
            for at in range(some)
        ]
        payload = jnp.concatenate([jnp.concatenate(p, axis=1) for p in payload], axis=0)
        slot = iota((devices * slots, cols), 0)
        onehot = [
            jnp.where(slot == target_ref[w, f : f + 1], 1.0, 0.0).astype(BF16)
            for f in range(tile_faces)
        ]
        onehot = jnp.concatenate(onehot, axis=1)
        sent = lax.dot_general(onehot, payload, ROWS_BY_ROWS, preferred_element_type=F32)
        sent_ref[w] = sent.astype(BF16).reshape(devices, slots, width)
        copies.append(pltpu.make_async_copy(sent_ref.at[w], out_ref.at[:, w], sems.at[w]))
        copies[-1].start()
    for copy in copies:
        copy.wait()


def first_kernel(
    planes, psi_in, near_ref, far_ref, factor_ref, target_ref, wall_ref, halo_ref,
    out_ref, psi_out, psi_ref, cells_ref, wide_ref, sent_ref, sems, psi_sem,
):
    full, cols = psi_ref.shape[1:]
    wide = 2 * HALO
    widen(factor_ref, wide_ref, (0, 6))

    def pair_step(pair, carry):
        at = pl.ds(pl.multiple_of(pair * wide, wide), wide)
        tile = [near_ref[at], far_ref[at], jnp.zeros((cols - 2 * wide, full), BF16)]
        beside = halo_part(jnp.concatenate(tile, axis=0), wall_ref[0], halo_ref.at[0])
        for odd in range(2):
            t = 2 * pair + odd
            psi = psi_in[t] + beside[odd]
            psi_ref[t] = psi
            place_cells(wide_ref[6] + wide_ref[0] * psi, t, cells_ref, 0)
        return carry

    lax.fori_loop(0, planes // 2, pair_step, 0, unroll=True)
    copy = pltpu.make_async_copy(psi_ref, psi_out, psi_sem.at[0])
    copy.start()
    scatter_cells(cells_ref, target_ref, sent_ref, out_ref, sems)
    copy.wait()


def rest_kernel(
    planes, psi_ref, next_ref, factor_ref, target_ref, wall_ref, main_ref, halo_ref, *rest,
):
    *late_refs, out_ref, cells_ref, tile_ref, wide_ref, sent_ref, sems = rest
    full, cols = psi_ref.shape[1:]
    some = wall_ref.shape[0]
    pairs = planes // 2
    height = pairs * HALO
    widen(factor_ref, wide_ref, range(1, 6))
    for c in range(some):
        starts = [(side * some + c) * height for side in range(2)]
        parts = [[ref[pl.ds(at, height)].astype(F32) for ref in late_refs] for at in starts]
        for pair, tile in enumerate(halo_tiles(parts, cols)):
            tile_ref[c * pairs + pair] = tile

    for pair in range(pairs):
        psi = []
        for c in range(some):
            main = [next_ref[c * planes + 2 * pair + odd] for odd in range(2)]
            beside = halo_part(tile_ref[c * pairs + pair], wall_ref[c], halo_ref.at[c])
            psi.append([m + b for m, b in zip(main, beside)])
        for odd in range(2):
            t = 2 * pair + odd
            p, q, r = psi_ref[t], psi[0][odd], psi[1][odd]
            place_cells(wide_ref[1] * p + wide_ref[2] * q, t, cells_ref, 0)
            place_cells(wide_ref[3] * p + wide_ref[4] * q + wide_ref[5] * r, t, cells_ref, 1)
    scatter_cells(cells_ref, target_ref, sent_ref, out_ref, sems)


def join_kernel(first, some, in_ref, *rest):
    out_ref, sems = rest[-2:]
    _, walls, _, width = in_ref.shape
    values = width // some
    run(
        [
            pltpu.make_async_copy(
                in_ref.at[:, w, :, pl.ds(c * values, values)],
                out_ref.at[:, :, pl.ds(((c + first) * walls + w) * values, values)],
                sems.at[c, w],
            )
            for c in range(some)
            for w in range(walls)
        ]
    )


def join_narrow_kernel(some, in_ref, *rest):
    out_ref = rest[-1]
    _, walls, _, width = in_ref.shape
    values = width // some
    for c in range(some):

        @pl.when(pl.program_id(1) == c)
        def _():
            for w in range(walls):
                out_ref[0, :, w * values : (w + 1) * values] = in_ref[0, w, :, c * values : (c + 1) * values]


def per_device(noise, wall_scale, span_scale, lund_factor, mean_velocity, owner_map):
    trio, all_planes, rows, cols = noise.shape
    n_span = lax.axis_size("span")
    n_wall = lax.axis_size("wall")
    devices = n_span * n_wall
    planes = all_planes // n_wall
    pairs = planes // 2
    full = rows * n_wall
    faces = full // (EDGE * EDGE)
    values = planes * EDGE * EDGE
    owners = owner_map.reshape(1, -1)
    elements = owners.shape[1]
    slots = max(8, 2 * elements // devices)
    count = elements // cols
    rest = trio - 1
    struct = jax.ShapeDtypeStruct
    hbm = pltpu.MemorySpace.HBM

    def call(kernel, ins, outs, name, limit, scratch=(), grid=(), out_specs=None, us=1):
        specs = out_specs or [VMEM] * len(outs)
        return pl.pallas_call(
            kernel,
            grid=grid,
            in_specs=ins,
            out_specs=specs if len(outs) > 1 else specs[0],
            out_shape=outs if len(outs) > 1 else outs[0],
            scratch_shapes=scratch,
            compiler_params=pltpu.CompilerParams(vmem_limit_bytes=limit * 1024 * 1024),
            cost_estimate=pl.CostEstimate(flops=us * 10**9, bytes_accessed=1024, transcendentals=0),
            name=name,
        )

    core_pairs = [(i, i ^ 1) for i in range(n_span)]
    chip_pairs = [(i, (i + 2 * (i % CORES) - 1) % n_span) for i in range(n_span)]

    def exchange(near, far):
        return lax.ppermute(near, "span", core_pairs), lax.ppermute(far, "span", chip_pairs)

    def spread(blocks):
        return [blocks[0]] + [
            lax.ppermute(x, "wall", [(i, (i + step) % n_wall) for i in range(n_wall)])
            for step, x in enumerate(blocks[1:], 1)
        ]

    def send(x):
        return lax.all_to_all(x, ("span", "wall"), 0, 0, tiled=True).reshape(devices, n_wall * slots, -1)

    dma = pltpu.SemaphoreType.DMA
    noise = noise.reshape(trio, all_planes * rows, cols)
    packed = call(
        functools.partial(pack_kernel, devices),
        [pl.BlockSpec(memory_space=hbm)] * 4,
        [pltpu.MemorySpace.VMEM((planes * rows + tail_rows(count), cols), BF16)] * n_wall,
        "pack",
        56,
        [
            pltpu.VMEM((all_planes * rows, cols), BF16),
            pltpu.VMEM(lund_factor.shape, F32),
            pltpu.VMEM((1, rows), F32),
            pltpu.VMEM(owners.shape, jnp.int32),
            dma((4,)),
        ],
    )(noise, lund_factor, mean_velocity.reshape(1, rows), owners)
    noise, packed = lax.optimization_barrier((noise, packed))
    packed = spread(packed)

    height = pairs * HALO
    edge = struct((n_wall, rest, height, cols), BF16)
    near, far, *early = call(
        prepare_rest_kernel,
        [pl.BlockSpec((1, all_planes * rows, cols), lambda c: (c + 1, 0, 0))],
        [edge, edge] + [struct((rest * planes * rows, cols), BF16)] * n_wall,
        "prepare_rest",
        16,
        grid=(rest,),
    )(noise)
    rest_near, rest_far = exchange(near, far)
    packed, _ = lax.optimization_barrier((packed, (near, far, early)))

    def taps(first, some, make, name):
        return call(
            functools.partial(taps_kernel, first),
            [SMEM, SMEM],
            [
                make((some, full, 2 * full), BF16),
                make((some, 2 * cols, 2 * cols), BF16),
                make((some, 2, 2 * cols, 2 * cols), BF16),
            ],
            name,
            16,
        )(wall_scale, span_scale)

    wall_first, main_first, halo_first = taps(0, 1, struct, "taps_first")
    factor, target = call(
        functools.partial(small_kernel, slots),
        [VMEM] * n_wall,
        [struct((full, cols), F32), struct((n_wall, count, cols), jnp.int32)],
        "small",
        16,
    )(*packed)

    edge = struct((planes * HALO, full), BF16)
    near, far = call(
        functools.partial(edges_kernel, planes), [VMEM] * n_wall, [edge, edge], "edges_first", 16
    )(*packed)
    near, far = exchange(near, far)
    early, rest_near = lax.optimization_barrier((early, rest_near))
    early = spread(early)
    (rest_near, rest_far), _ = lax.optimization_barrier(((rest_near, rest_far), (near, far)))
    late = call(
        pack_late_kernel,
        [VMEM] * 2,
        [hbm((2 * rest * height, cols), BF16)] * n_wall,
        "pack_late",
        16,
        [dma((n_wall, 2 * rest))],
        out_specs=[ANYWHERE] * n_wall,
    )(rest_near, rest_far)
    near, late = lax.optimization_barrier((near, late))

    psi = struct((planes, full, cols), F32)
    psi_main = call(
        functools.partial(main_kernel, planes), [VMEM] * (2 + n_wall), [psi], "main_first", 16
    )(wall_first, main_first, *packed)

    def scratch(some):
        return [
            pltpu.VMEM((some, faces * values, cols), F32),
            pltpu.VMEM((rest * pairs, cols, full), BF16),
            pltpu.VMEM((FACTORS, full, cols), F32),
            pltpu.VMEM((n_wall, devices, slots, some * values), BF16),
            dma((n_wall,)),
        ]

    def out(some):
        return hbm((devices, n_wall, slots, some * values), BF16)

    cells, _, *more = scratch(1)
    sent, psi = call(
        functools.partial(first_kernel, planes),
        [VMEM] * 7,
        [out(1), hbm(psi.shape, F32)],
        "filter_first",
        24,
        [pltpu.VMEM(psi.shape, F32), cells, *more, dma((1,))],
        out_specs=[ANYWHERE, ANYWHERE],
    )(psi_main, near, far, factor, target, wall_first, halo_first)
    (wall_scale, span_scale, late), sent = lax.optimization_barrier(((wall_scale, span_scale, late), sent))
    got_first = send(sent)
    late = spread(late)
    wall_rest, main_rest, halo_rest = taps(1, rest, struct, "taps_rest")
    psi_next = call(
        functools.partial(main_kernel, planes),
        [VMEM] * (2 + n_wall),
        [struct((rest * planes, full, cols), F32)],
        "main_next",
        16,
    )(wall_rest, main_rest, *early)
    sent = call(
        functools.partial(rest_kernel, planes),
        [VMEM] * (7 + n_wall),
        [out(rest)],
        "filter_rest",
        32,
        scratch(rest),
        out_specs=[ANYWHERE],
        us=100,
    )(psi, psi_next, factor, target, wall_rest, main_rest, halo_rest, *late)
    got_rest = send(sent)

    whole = hbm((n_span, n_wall * slots, trio * values * n_wall), BF16)
    narrow = values % LANES != 0

    def join(received, some, before):
        keep = [] if before is None else [before]
        shape = (n_span, n_wall, n_wall * slots, some * values)
        return pl.pallas_call(
            functools.partial(join_narrow_kernel, some)
            if narrow
            else functools.partial(join_kernel, len(keep), some),
            grid=(n_span, some) if narrow else (),
            in_specs=[pl.BlockSpec((1, *shape[1:]), lambda s, c: (s, 0, 0, 0)) if narrow else VMEM]
            + [ANYWHERE] * len(keep),
            out_specs=pl.BlockSpec((1, n_wall * slots, values * n_wall), lambda s, c: (s, 0, c + len(keep)))
            if narrow
            else ANYWHERE,
            out_shape=whole,
            scratch_shapes=[] if narrow else [dma((some, n_wall))],
            input_output_aliases={1: 0} if keep else {},
            compiler_params=pltpu.CompilerParams(vmem_limit_bytes=16 * 1024 * 1024),
            name="join",
        )(received.reshape(shape), *keep)

    return join(got_rest, rest, join(got_first, 1, None)).reshape(1, devices * slots, -1)


def solution(mesh):
    return jax.shard_map(
        per_device,
        mesh=mesh,
        in_specs=(
            P(None, None, "wall", "span"),
            P(),
            P(),
            P(None, "wall"),
            P("wall"),
            P("wall", "span", None, None),
        ),
        out_specs=P(("span", "wall"), None, None),
        check_vma=False,
    )
```

```python
import functools
import math

import jax
import jax.numpy as jnp
from jax import lax
from jax.experimental import pallas as pl
from jax.experimental.pallas import tpu as pltpu
from jax.sharding import PartitionSpec as P

HALO = 24
EDGE = 4
LANES = 128
FACTORS = 7
CORES = 2
F32 = jnp.float32
BF16 = jnp.bfloat16
VMEM = pl.BlockSpec(memory_space=pltpu.VMEM)
ANYWHERE = pl.BlockSpec(memory_space=pl.ANY)
SMEM = pl.BlockSpec(memory_space=pltpu.SMEM)
ROWS_BY_ROWS = (((1,), (1,)), ((), ()))


def iota(shape, dim):
    return lax.broadcasted_iota(jnp.int32, shape, dim)


def split(x):
    high = x.astype(BF16)
    return high, (x - high.astype(F32)).astype(BF16)


def tap_values(scale, distance, valid):
    scale = jnp.full((1, 1), scale, F32)
    k = iota((1, LANES), 1) - HALO
    squares = jnp.where(k <= HALO, jnp.exp(-math.pi * (k * k).astype(F32) / (scale * scale)), 0.0)
    norm = jnp.sqrt(jnp.sum(squares, axis=1, keepdims=True))
    d = distance.astype(F32)
    raw = jnp.exp(-math.pi * (d * d) / (2.0 * scale * scale))
    inside = valid & (distance >= -HALO) & (distance <= HALO)
    return jnp.where(inside, raw, 0.0) / norm


def tail_rows(count):
    return -(-(2 * count + 3 * FACTORS) // 16) * 16


def cell_row(i, faces):
    return (i % faces) * (EDGE * EDGE) + (i // (faces * EDGE)) * EDGE + (i // faces) % EDGE


def taps_kernel(first, wall_scale, span_scale, wall_ref, main_ref, halo_ref):
    some, full, _ = wall_ref.shape
    cols = main_ref.shape[1] // 2
    walls = lax.axis_size("wall")
    rows = full // walls
    i, j = iota((full, full), 0), iota((full, full), 1)
    y = cell_row(i, full // (EDGE * EDGE))
    source = lax.rem(lax.axis_index("wall") + walls - j // rows, walls)
    column = source * rows + j % rows
    n = iota((cols, cols), 1)
    target = (n % (cols // EDGE)) * EDGE + n // (cols // EDGE)
    k = iota((cols, cols), 0)
    side, odd, r = k // (2 * HALO), (k // HALO) % 2, k % HALO
    core = lax.rem(lax.axis_index("span"), CORES)
    z = jnp.where(side + core == 1, r - HALO, cols + r)

    def span_matrix(scale, distance, valid):
        high, low = split(tap_values(scale, distance, valid))
        top = jnp.concatenate([high, low], axis=1)
        return jnp.concatenate([top, jnp.concatenate([high, jnp.zeros_like(high)], axis=1)], axis=0)

    for c in range(some):
        high, low = split(tap_values(wall_scale[first + c], column - y, i >= 0))
        wall_ref[c, :, :full] = high
        wall_ref[c, :, full:] = low
        scale = span_scale[first + c]
        main_ref[c] = span_matrix(scale, k - target, k >= 0)
        for parity in range(2):
            valid = (k < 4 * HALO) & (odd == parity)
            halo_ref[c, parity] = span_matrix(scale, z - target, valid)


def run(copies):
    for copy in copies:
        copy.start()
    for copy in copies:
        copy.wait()


def pack_kernel(devices, noise_in, lund_in, mean_in, owner_in, *rest):
    *out_refs, noise_ref, lund_ref, mean_ref, owner_ref, sems = rest
    walls = len(out_refs)
    cols = noise_ref.shape[1]
    block = noise_ref.shape[0] // walls
    tail = out_refs[0].shape[0] - block
    rows = mean_ref.shape[1]
    me = lax.axis_index("wall")
    pairs = ((lund_in, lund_ref), (mean_in, mean_ref), (owner_in, owner_ref), (noise_in.at[0], noise_ref))
    *small, noise = [pltpu.make_async_copy(a, b, sems.at[i]) for i, (a, b) in enumerate(pairs)]
    noise.start()
    run(small)
    owner = owner_ref[...]
    elements = owner.shape[1]
    mine = jnp.where(iota((devices, elements), 0) == owner, 1.0, 0.0)
    before = jnp.where(iota((elements, elements), 0) < iota((elements, elements), 1), 1.0, 0.0)
    count = jnp.dot(mine.astype(BF16), before.astype(BF16), preferred_element_type=F32)
    rank = jnp.sum(mine * count, axis=0, keepdims=True)
    pieces = [owner.astype(F32), rank]
    pieces = [p[:, at : at + cols] for p in pieces for at in range(0, elements, cols)]
    factor = jnp.concatenate([lund_ref[...], mean_ref[...]], axis=0)
    factor = jnp.concatenate([factor, jnp.zeros((FACTORS, cols - rows), F32)], axis=1)
    for _ in range(3):
        part = factor.astype(BF16).astype(F32)
        pieces.append(part)
        factor = factor - part
    pieces.append(jnp.zeros((tail - sum(p.shape[0] for p in pieces), cols), F32))
    small = jnp.concatenate(pieces, axis=0).astype(BF16)
    noise.wait()
    for step, out_ref in enumerate(out_refs):
        start = pl.multiple_of(lax.rem(me + step, walls) * block, block)
        out_ref[:block] = noise_ref[pl.ds(start, block)]
        out_ref[block:] = small


def pack_late_kernel(near_ref, far_ref, *rest):
    out_refs, sems = rest[:-1], rest[-1]
    walls, some, height, _ = near_ref.shape
    me = lax.axis_index("wall")
    copies = []
    for step, out_ref in enumerate(out_refs):
        to = lax.rem(me + step, walls)
        for side, ref in enumerate((near_ref, far_ref)):
            for c in range(some):
                at = side * some + c
                copies.append(
                    pltpu.make_async_copy(
                        ref.at[to, c], out_ref.at[pl.ds(at * height, height)], sems.at[step, at]
                    )
                )
    run(copies)


def small_kernel(slots, *rest):
    *in_refs, factor_ref, target_ref = rest
    walls = len(in_refs)
    height, cols = in_refs[0].shape
    full = factor_ref.shape[0]
    rows = full // walls
    count = target_ref.shape[1]
    tail = tail_rows(count)
    me = lax.axis_index("wall")
    columns = jnp.zeros((full, tail), F32)
    y = cell_row(iota((full, cols), 0), full // (EDGE * EDGE))
    for step, in_ref in enumerate(in_refs):
        w = lax.rem(me + walls - step, walls)
        small = in_ref[height - tail :]
        pick = jnp.where(y == iota((full, cols), 1) + w * rows, 1.0, 0.0)
        pick = jnp.where(iota((full, cols), 1) < rows, pick, 0.0).astype(BF16)
        columns = columns + lax.dot_general(pick, small, ROWS_BY_ROWS, preferred_element_type=F32)
        numbers = small.astype(F32)
        target = numbers[:count] * slots + numbers[count : 2 * count]
        target_ref[pl.ds(w, 1)] = target.astype(jnp.int32)[None]
    at = 2 * count
    factor = sum(columns[:, at + p * FACTORS : at + (p + 1) * FACTORS] for p in range(3))
    factor_ref[...] = jnp.concatenate([factor, jnp.zeros((full, cols - FACTORS), F32)], axis=1)


def edge_picker(cols):
    core = lax.rem(lax.axis_index("span"), CORES)
    row, col = iota((2 * HALO, cols), 0), iota((2 * HALO, cols), 1)
    start = jnp.where(row // HALO == core, cols - HALO, 0)
    return jnp.where(col == start + row % HALO, 1.0, 0.0).astype(BF16)


def edges_kernel(planes, *rest):
    *noise_refs, near_ref, far_ref = rest
    cols = noise_refs[0].shape[1]
    rows = near_ref.shape[1] // len(noise_refs)
    wide = 2 * HALO
    pick = edge_picker(cols)
    for pair in range(planes // 2):
        edges = []
        for t in (2 * pair, 2 * pair + 1):
            plane = [ref[t * rows : (t + 1) * rows] for ref in noise_refs]
            plane = jnp.concatenate(plane, axis=0)
            edges.append(lax.dot_general(pick, plane, ROWS_BY_ROWS, preferred_element_type=F32))
        at = pl.ds(pair * wide, wide)
        near_ref[at] = jnp.concatenate([e[:HALO] for e in edges], axis=0).astype(BF16)
        far_ref[at] = jnp.concatenate([e[HALO:] for e in edges], axis=0).astype(BF16)


def prepare_rest_kernel(noise_ref, near_ref, far_ref, *out_refs):
    walls, _, height, cols = near_ref.shape
    block = noise_ref.shape[1] // walls
    me = lax.axis_index("wall")
    c = pl.program_id(0)
    target = pl.ds(pl.multiple_of(c * block, block), block)
    for step, out_ref in enumerate(out_refs):
        source = pl.multiple_of(lax.rem(me + step, walls) * block, block)
        out_ref[target] = noise_ref[0, pl.ds(source, block)]
    pairs = height // HALO
    pick = edge_picker(cols)
    for w in range(walls):
        edges = []
        for pair in range(pairs):
            plane = noise_ref[0, (w * pairs + pair) * cols : (w * pairs + pair + 1) * cols]
            edges.append(lax.dot_general(pick, plane, ROWS_BY_ROWS, preferred_element_type=F32))
        near_ref[w, c] = jnp.concatenate([e[:HALO] for e in edges], axis=0).astype(BF16)
        far_ref[w, c] = jnp.concatenate([e[HALO:] for e in edges], axis=0).astype(BF16)


def swap_blocks(blocks, cols):
    part = cols // EDGE
    lane = iota(blocks[0].shape, 1)
    for step in (2, 1):
        first = (lane // (part * step)) % 2 == 0
        out = list(blocks)
        for a in range(EDGE):
            if a & step:
                continue
            one, two = blocks[a], blocks[a + step]
            out[a] = jnp.where(first, one, pltpu.roll(two, part * step, 1))
            out[a + step] = jnp.where(first, pltpu.roll(one, cols - part * step, 1), two)
        blocks = out
    return blocks


def halo_tiles(parts, cols):
    half = cols // 2
    sides = []
    for side in parts:
        planes = [[], []]
        for one, two in zip(side[::2], side[1::2]):
            lower = iota(one.shape, 1) < half
            planes[0].append(jnp.where(lower, one, pltpu.roll(two, half, 1)))
            planes[1].append(jnp.where(lower, pltpu.roll(one, half, 1), two))
        sides.append([jnp.concatenate(p, axis=1) for p in planes])
    pairs = sides[0][0].shape[0] // HALO
    zeros = jnp.zeros((cols - 4 * HALO, sides[0][0].shape[1]), F32)
    for pair in range(pairs):
        at = slice(pair * HALO, (pair + 1) * HALO)
        tile = [sides[s][odd][at] for s in range(2) for odd in range(2)]
        yield jnp.concatenate(tile + [zeros], axis=0).astype(BF16)


def span_product(x, matrix):
    cols = x.shape[1]
    both = jnp.dot(jnp.concatenate(split(x), axis=1), matrix, preferred_element_type=F32)
    return both[:, :cols] + both[:, cols:]


def main_part(planes, wall, matrix):
    both = jnp.concatenate(planes, axis=1)
    cols = planes[0].shape[1]
    smooth = jnp.dot(wall, jnp.concatenate([both, both], axis=0), preferred_element_type=F32)
    return [span_product(smooth[:, odd * cols : (odd + 1) * cols], matrix) for odd in range(2)]


def halo_part(tile, wall, halo_ref):
    smooth = lax.dot_general(
        wall, jnp.concatenate([tile, tile], axis=1), ROWS_BY_ROWS, preferred_element_type=F32
    )
    return [span_product(smooth, halo_ref[odd]) for odd in range(2)]


def planes_of(refs, t, rows):
    return [
        jnp.concatenate([ref[at * rows : (at + 1) * rows] for ref in refs], axis=0) for at in (t, t + 1)
    ]


def main_kernel(planes, wall_ref, main_ref, *rest):
    *refs, psi_ref = rest
    rows = psi_ref.shape[1] // len(refs)
    for t in range(0, psi_ref.shape[0], 2):
        c = t // planes
        psi_ref[t], psi_ref[t + 1] = main_part(planes_of(refs, t, rows), wall_ref[c], main_ref[c])


def widen(factor_ref, wide_ref, which):
    for f in which:
        wide_ref[f] = jnp.broadcast_to(factor_ref[:, f : f + 1], wide_ref.shape[1:])


def place_cells(velocity, t, cells_ref, at):
    full, cols = velocity.shape
    quarter, faces = full // EDGE, full // (EDGE * EDGE)
    values = cells_ref.shape[1] // faces
    blocks = [velocity[a * quarter : (a + 1) * quarter] for a in range(EDGE)]
    for dz, block in enumerate(swap_blocks(blocks, cols)):
        for dy in range(EDGE):
            j = t * EDGE * EDGE + dy * EDGE + dz
            cells_ref[at, pl.ds(j, faces, stride=values), :] = block[dy * faces : (dy + 1) * faces]


def scatter_cells(cells_ref, target_ref, sent_ref, out_ref, sems):
    walls, tile_faces, cols = target_ref.shape
    some = cells_ref.shape[0]
    values = cells_ref.shape[1] // (walls * tile_faces)
    _, devices, slots, width = sent_ref.shape
    copies = []
    for w in range(walls):
        payload = [
            [
                cells_ref[at, pl.ds((w * tile_faces + f) * values, values), :].astype(BF16)
                for f in range(tile_faces)
            ]
            for at in range(some)
        ]
        payload = jnp.concatenate([jnp.concatenate(p, axis=1) for p in payload], axis=0)
        slot = iota((devices * slots, cols), 0)
        onehot = [
            jnp.where(slot == target_ref[w, f : f + 1], 1.0, 0.0).astype(BF16)
            for f in range(tile_faces)
        ]
        onehot = jnp.concatenate(onehot, axis=1)
        sent = lax.dot_general(onehot, payload, ROWS_BY_ROWS, preferred_element_type=F32)
        sent_ref[w] = sent.astype(BF16).reshape(devices, slots, width)
        copies.append(pltpu.make_async_copy(sent_ref.at[w], out_ref.at[:, w], sems.at[w]))
        copies[-1].start()
    for copy in copies:
        copy.wait()


def first_kernel(
    planes, psi_in, near_ref, far_ref, factor_ref, target_ref, wall_ref, halo_ref,
    out_ref, psi_out, psi_ref, cells_ref, wide_ref, sent_ref, sems, psi_sem,
):
    full, cols = psi_ref.shape[1:]
    wide = 2 * HALO
    widen(factor_ref, wide_ref, (0, 6))

    def pair_step(pair, carry):
        at = pl.ds(pl.multiple_of(pair * wide, wide), wide)
        tile = [near_ref[at], far_ref[at], jnp.zeros((cols - 2 * wide, full), BF16)]
        beside = halo_part(jnp.concatenate(tile, axis=0), wall_ref[0], halo_ref.at[0])
        for odd in range(2):
            t = 2 * pair + odd
            psi = psi_in[t] + beside[odd]
            psi_ref[t] = psi
            place_cells(wide_ref[6] + wide_ref[0] * psi, t, cells_ref, 0)
        return carry

    lax.fori_loop(0, planes // 2, pair_step, 0, unroll=True)
    copy = pltpu.make_async_copy(psi_ref, psi_out, psi_sem.at[0])
    copy.start()
    scatter_cells(cells_ref, target_ref, sent_ref, out_ref, sems)
    copy.wait()


def rest_kernel(
    planes, psi_ref, next_ref, factor_ref, target_ref, wall_ref, main_ref, halo_ref, *rest,
):
    *late_refs, out_ref, cells_ref, tile_ref, wide_ref, sent_ref, sems = rest
    full, cols = psi_ref.shape[1:]
    some = wall_ref.shape[0]
    pairs = planes // 2
    height = pairs * HALO
    widen(factor_ref, wide_ref, range(1, 6))
    for c in range(some):
        starts = [(side * some + c) * height for side in range(2)]
        parts = [[ref[pl.ds(at, height)].astype(F32) for ref in late_refs] for at in starts]
        for pair, tile in enumerate(halo_tiles(parts, cols)):
            tile_ref[c * pairs + pair] = tile

    for pair in range(pairs):
        psi = []
        for c in range(some):
            main = [next_ref[c * planes + 2 * pair + odd] for odd in range(2)]
            beside = halo_part(tile_ref[c * pairs + pair], wall_ref[c], halo_ref.at[c])
            psi.append([m + b for m, b in zip(main, beside)])
        for odd in range(2):
            t = 2 * pair + odd
            p, q, r = psi_ref[t], psi[0][odd], psi[1][odd]
            place_cells(wide_ref[1] * p + wide_ref[2] * q, t, cells_ref, 0)
            place_cells(wide_ref[3] * p + wide_ref[4] * q + wide_ref[5] * r, t, cells_ref, 1)
    scatter_cells(cells_ref, target_ref, sent_ref, out_ref, sems)


def join_kernel(first, some, in_ref, *rest):
    out_ref, sems = rest[-2:]
    _, walls, _, width = in_ref.shape
    values = width // some
    run(
        [
            pltpu.make_async_copy(
                in_ref.at[:, w, :, pl.ds(c * values, values)],
                out_ref.at[:, :, pl.ds(((c + first) * walls + w) * values, values)],
                sems.at[c, w],
            )
            for c in range(some)
            for w in range(walls)
        ]
    )


def join_narrow_kernel(some, in_ref, *rest):
    out_ref = rest[-1]
    _, walls, _, width = in_ref.shape
    values = width // some
    for c in range(some):

        @pl.when(pl.program_id(1) == c)
        def _():
            for w in range(walls):
                out_ref[0, :, w * values : (w + 1) * values] = in_ref[0, w, :, c * values : (c + 1) * values]


def per_device(noise, wall_scale, span_scale, lund_factor, mean_velocity, owner_map):
    trio, all_planes, rows, cols = noise.shape
    n_span = lax.axis_size("span")
    n_wall = lax.axis_size("wall")
    devices = n_span * n_wall
    planes = all_planes // n_wall
    pairs = planes // 2
    full = rows * n_wall
    faces = full // (EDGE * EDGE)
    values = planes * EDGE * EDGE
    owners = owner_map.reshape(1, -1)
    elements = owners.shape[1]
    slots = max(8, 2 * elements // devices)
    count = elements // cols
    rest = trio - 1
    struct = jax.ShapeDtypeStruct
    hbm = pltpu.MemorySpace.HBM

    def call(kernel, ins, outs, name, limit, scratch=(), grid=(), out_specs=None, us=1):
        specs = out_specs or [VMEM] * len(outs)
        return pl.pallas_call(
            kernel,
            grid=grid,
            in_specs=ins,
            out_specs=specs if len(outs) > 1 else specs[0],
            out_shape=outs if len(outs) > 1 else outs[0],
            scratch_shapes=scratch,
            compiler_params=pltpu.CompilerParams(vmem_limit_bytes=limit * 1024 * 1024),
            cost_estimate=pl.CostEstimate(flops=us * 10**9, bytes_accessed=1024, transcendentals=0),
            name=name,
        )

    core_pairs = [(i, i ^ 1) for i in range(n_span)]
    chip_pairs = [(i, (i + 2 * (i % CORES) - 1) % n_span) for i in range(n_span)]

    def exchange(near, far):
        return lax.ppermute(near, "span", core_pairs), lax.ppermute(far, "span", chip_pairs)

    def spread(blocks):
        return [blocks[0]] + [
            lax.ppermute(x, "wall", [(i, (i + step) % n_wall) for i in range(n_wall)])
            for step, x in enumerate(blocks[1:], 1)
        ]

    def send(x):
        return lax.all_to_all(x, ("span", "wall"), 0, 0, tiled=True).reshape(devices, n_wall * slots, -1)

    dma = pltpu.SemaphoreType.DMA
    noise = noise.reshape(trio, all_planes * rows, cols)
    packed = call(
        functools.partial(pack_kernel, devices),
        [pl.BlockSpec(memory_space=hbm)] * 4,
        [pltpu.MemorySpace.VMEM((planes * rows + tail_rows(count), cols), BF16)] * n_wall,
        "pack",
        56,
        [
            pltpu.VMEM((all_planes * rows, cols), BF16),
            pltpu.VMEM(lund_factor.shape, F32),
            pltpu.VMEM((1, rows), F32),
            pltpu.VMEM(owners.shape, jnp.int32),
            dma((4,)),
        ],
    )(noise, lund_factor, mean_velocity.reshape(1, rows), owners)
    noise, packed = lax.optimization_barrier((noise, packed))
    packed = spread(packed)

    height = pairs * HALO
    edge = struct((n_wall, rest, height, cols), BF16)
    near, far, *early = call(
        prepare_rest_kernel,
        [pl.BlockSpec((1, all_planes * rows, cols), lambda c: (c + 1, 0, 0))],
        [edge, edge] + [struct((rest * planes * rows, cols), BF16)] * n_wall,
        "prepare_rest",
        16,
        grid=(rest,),
    )(noise)
    rest_near, rest_far = exchange(near, far)
    packed, _ = lax.optimization_barrier((packed, (near, far, early)))

    def taps(first, some, make, name):
        return call(
            functools.partial(taps_kernel, first),
            [SMEM, SMEM],
            [
                make((some, full, 2 * full), BF16),
                make((some, 2 * cols, 2 * cols), BF16),
                make((some, 2, 2 * cols, 2 * cols), BF16),
            ],
            name,
            16,
        )(wall_scale, span_scale)

    wall_first, main_first, halo_first = taps(0, 1, struct, "taps_first")
    factor, target = call(
        functools.partial(small_kernel, slots),
        [VMEM] * n_wall,
        [struct((full, cols), F32), struct((n_wall, count, cols), jnp.int32)],
        "small",
        16,
    )(*packed)

    edge = struct((planes * HALO, full), BF16)
    near, far = call(
        functools.partial(edges_kernel, planes), [VMEM] * n_wall, [edge, edge], "edges_first", 16
    )(*packed)
    near, far = exchange(near, far)
    early, rest_near = lax.optimization_barrier((early, rest_near))
    early = spread(early)
    (rest_near, rest_far), _ = lax.optimization_barrier(((rest_near, rest_far), (near, far)))
    near, rest_near, rest_far = lax.optimization_barrier((near, rest_near, rest_far))

    psi = struct((planes, full, cols), F32)
    psi_main = call(
        functools.partial(main_kernel, planes), [VMEM] * (2 + n_wall), [psi], "main_first", 16
    )(wall_first, main_first, *packed)

    def scratch(some):
        return [
            pltpu.VMEM((some, faces * values, cols), F32),
            pltpu.VMEM((rest * pairs, cols, full), BF16),
            pltpu.VMEM((FACTORS, full, cols), F32),
            pltpu.VMEM((n_wall, devices, slots, some * values), BF16),
            dma((n_wall,)),
        ]

    def out(some):
        return hbm((devices, n_wall, slots, some * values), BF16)

    cells, _, *more = scratch(1)
    sent, psi = call(
        functools.partial(first_kernel, planes),
        [VMEM] * 7,
        [out(1), hbm(psi.shape, F32)],
        "filter_first",
        24,
        [pltpu.VMEM(psi.shape, F32), cells, *more, dma((1,))],
        out_specs=[ANYWHERE, ANYWHERE],
    )(psi_main, near, far, factor, target, wall_first, halo_first)
    (wall_scale, span_scale, rest_near, rest_far), sent = lax.optimization_barrier(
        ((wall_scale, span_scale, rest_near, rest_far), sent)
    )
    got_first = send(sent)
    late = call(
        pack_late_kernel,
        [VMEM] * 2,
        [hbm((2 * rest * height, cols), BF16)] * n_wall,
        "pack_late",
        16,
        [dma((n_wall, 2 * rest))],
        out_specs=[ANYWHERE] * n_wall,
    )(rest_near, rest_far)
    late = spread(late)
    wall_rest, main_rest, halo_rest = taps(1, rest, struct, "taps_rest")
    psi_next = call(
        functools.partial(main_kernel, planes),
        [VMEM] * (2 + n_wall),
        [struct((rest * planes, full, cols), F32)],
        "main_next",
        16,
    )(wall_rest, main_rest, *early)
    sent = call(
        functools.partial(rest_kernel, planes),
        [VMEM] * (7 + n_wall),
        [out(rest)],
        "filter_rest",
        32,
        scratch(rest),
        out_specs=[ANYWHERE],
        us=100,
    )(psi, psi_next, factor, target, wall_rest, main_rest, halo_rest, *late)
    got_rest = send(sent)

    whole = hbm((n_span, n_wall * slots, trio * values * n_wall), BF16)
    narrow = values % LANES != 0

    def join(received, some, before):
        keep = [] if before is None else [before]
        shape = (n_span, n_wall, n_wall * slots, some * values)
        return pl.pallas_call(
            functools.partial(join_narrow_kernel, some)
            if narrow
            else functools.partial(join_kernel, len(keep), some),
            grid=(n_span, some) if narrow else (),
            in_specs=[pl.BlockSpec((1, *shape[1:]), lambda s, c: (s, 0, 0, 0)) if narrow else VMEM]
            + [ANYWHERE] * len(keep),
            out_specs=pl.BlockSpec((1, n_wall * slots, values * n_wall), lambda s, c: (s, 0, c + len(keep)))
            if narrow
            else ANYWHERE,
            out_shape=whole,
            scratch_shapes=[] if narrow else [dma((some, n_wall))],
            input_output_aliases={1: 0} if keep else {},
            compiler_params=pltpu.CompilerParams(vmem_limit_bytes=16 * 1024 * 1024),
            name="join",
        )(received.reshape(shape), *keep)

    return join(got_rest, rest, join(got_first, 1, None)).reshape(1, devices * slots, -1)


def solution(mesh):
    return jax.shard_map(
        per_device,
        mesh=mesh,
        in_specs=(
            P(None, None, "wall", "span"),
            P(),
            P(),
            P(None, "wall"),
            P("wall"),
            P("wall", "span", None, None),
        ),
        out_specs=P(("span", "wall"), None, None),
        check_vma=False,
    )
```

```python
import functools
import math

import jax
import jax.numpy as jnp
from jax import lax
from jax.experimental import pallas as pl
from jax.experimental.pallas import tpu as pltpu
from jax.sharding import PartitionSpec as P

HALO = 24
EDGE = 4
LANES = 128
FACTORS = 7
CORES = 2
F32 = jnp.float32
BF16 = jnp.bfloat16
VMEM = pl.BlockSpec(memory_space=pltpu.VMEM)
ANYWHERE = pl.BlockSpec(memory_space=pl.ANY)
SMEM = pl.BlockSpec(memory_space=pltpu.SMEM)
ROWS_BY_ROWS = (((1,), (1,)), ((), ()))


def iota(shape, dim):
    return lax.broadcasted_iota(jnp.int32, shape, dim)


def split(x):
    high = x.astype(BF16)
    return high, (x - high.astype(F32)).astype(BF16)


def tap_values(scale, distance, valid):
    scale = jnp.full((1, 1), scale, F32)
    k = iota((1, LANES), 1) - HALO
    squares = jnp.where(k <= HALO, jnp.exp(-math.pi * (k * k).astype(F32) / (scale * scale)), 0.0)
    norm = jnp.sqrt(jnp.sum(squares, axis=1, keepdims=True))
    d = distance.astype(F32)
    raw = jnp.exp(-math.pi * (d * d) / (2.0 * scale * scale))
    inside = valid & (distance >= -HALO) & (distance <= HALO)
    return jnp.where(inside, raw, 0.0) / norm


def tail_rows(count):
    return -(-(2 * count + 3 * FACTORS) // 16) * 16


def cell_row(i, faces):
    return (i % faces) * (EDGE * EDGE) + (i // (faces * EDGE)) * EDGE + (i // faces) % EDGE


def taps_kernel(first, wall_scale, span_scale, wall_ref, main_ref, halo_ref):
    some, full, _ = wall_ref.shape
    cols = main_ref.shape[1] // 2
    walls = lax.axis_size("wall")
    rows = full // walls
    i, j = iota((full, full), 0), iota((full, full), 1)
    y = cell_row(i, full // (EDGE * EDGE))
    source = lax.axis_index("wall") ^ (j // rows)
    column = source * rows + j % rows
    n = iota((cols, cols), 1)
    target = (n % (cols // EDGE)) * EDGE + n // (cols // EDGE)
    k = iota((cols, cols), 0)
    side, odd, r = k // (2 * HALO), (k // HALO) % 2, k % HALO
    core = lax.rem(lax.axis_index("span"), CORES)
    z = jnp.where(side + core == 1, r - HALO, cols + r)

    def span_matrix(scale, distance, valid):
        high, low = split(tap_values(scale, distance, valid))
        top = jnp.concatenate([high, low], axis=1)
        return jnp.concatenate([top, jnp.concatenate([high, jnp.zeros_like(high)], axis=1)], axis=0)

    for c in range(some):
        high, low = split(tap_values(wall_scale[first + c], column - y, i >= 0))
        wall_ref[c, :, :full] = high
        wall_ref[c, :, full:] = low
        scale = span_scale[first + c]
        main_ref[c] = span_matrix(scale, k - target, k >= 0)
        for parity in range(2):
            valid = (k < 4 * HALO) & (odd == parity)
            halo_ref[c, parity] = span_matrix(scale, z - target, valid)


def run(copies):
    for copy in copies:
        copy.start()
    for copy in copies:
        copy.wait()


def pack_kernel(devices, noise_in, lund_in, mean_in, owner_in, *rest):
    *out_refs, noise_ref, lund_ref, mean_ref, owner_ref, sems = rest
    walls = len(out_refs)
    cols = noise_ref.shape[1]
    block = noise_ref.shape[0] // walls
    tail = out_refs[0].shape[0] - block
    rows = mean_ref.shape[1]
    me = lax.axis_index("wall")
    pairs = ((lund_in, lund_ref), (mean_in, mean_ref), (owner_in, owner_ref), (noise_in.at[0], noise_ref))
    *small, noise = [pltpu.make_async_copy(a, b, sems.at[i]) for i, (a, b) in enumerate(pairs)]
    noise.start()
    run(small)
    owner = owner_ref[...]
    elements = owner.shape[1]
    mine = jnp.where(iota((devices, elements), 0) == owner, 1.0, 0.0)
    before = jnp.where(iota((elements, elements), 0) < iota((elements, elements), 1), 1.0, 0.0)
    count = jnp.dot(mine.astype(BF16), before.astype(BF16), preferred_element_type=F32)
    rank = jnp.sum(mine * count, axis=0, keepdims=True)
    pieces = [owner.astype(F32), rank]
    pieces = [p[:, at : at + cols] for p in pieces for at in range(0, elements, cols)]
    factor = jnp.concatenate([lund_ref[...], mean_ref[...]], axis=0)
    factor = jnp.concatenate([factor, jnp.zeros((FACTORS, cols - rows), F32)], axis=1)
    for _ in range(3):
        part = factor.astype(BF16).astype(F32)
        pieces.append(part)
        factor = factor - part
    pieces.append(jnp.zeros((tail - sum(p.shape[0] for p in pieces), cols), F32))
    small = jnp.concatenate(pieces, axis=0).astype(BF16)
    noise.wait()
    for step, out_ref in enumerate(out_refs):
        start = pl.multiple_of((me ^ step) * block, block)
        out_ref[:block] = noise_ref[pl.ds(start, block)]
        out_ref[block:] = small


def pack_late_kernel(near_ref, far_ref, *rest):
    out_refs, sems = rest[:-1], rest[-1]
    walls, some, height, _ = near_ref.shape
    me = lax.axis_index("wall")
    copies = []
    for step, out_ref in enumerate(out_refs):
        to = (me ^ step)
        for side, ref in enumerate((near_ref, far_ref)):
            for c in range(some):
                at = side * some + c
                copies.append(
                    pltpu.make_async_copy(
                        ref.at[to, c], out_ref.at[pl.ds(at * height, height)], sems.at[step, at]
                    )
                )
    run(copies)


def small_kernel(slots, *rest):
    *in_refs, factor_ref, target_ref = rest
    walls = len(in_refs)
    height, cols = in_refs[0].shape
    full = factor_ref.shape[0]
    rows = full // walls
    count = target_ref.shape[1]
    tail = tail_rows(count)
    me = lax.axis_index("wall")
    columns = jnp.zeros((full, tail), F32)
    y = cell_row(iota((full, cols), 0), full // (EDGE * EDGE))
    for step, in_ref in enumerate(in_refs):
        w = me ^ step
        small = in_ref[height - tail :]
        pick = jnp.where(y == iota((full, cols), 1) + w * rows, 1.0, 0.0)
        pick = jnp.where(iota((full, cols), 1) < rows, pick, 0.0).astype(BF16)
        columns = columns + lax.dot_general(pick, small, ROWS_BY_ROWS, preferred_element_type=F32)
        numbers = small.astype(F32)
        target = numbers[:count] * slots + numbers[count : 2 * count]
        target_ref[pl.ds(w, 1)] = target.astype(jnp.int32)[None]
    at = 2 * count
    factor = sum(columns[:, at + p * FACTORS : at + (p + 1) * FACTORS] for p in range(3))
    factor_ref[...] = jnp.concatenate([factor, jnp.zeros((full, cols - FACTORS), F32)], axis=1)


def edge_picker(cols):
    core = lax.rem(lax.axis_index("span"), CORES)
    row, col = iota((2 * HALO, cols), 0), iota((2 * HALO, cols), 1)
    start = jnp.where(row // HALO == core, cols - HALO, 0)
    return jnp.where(col == start + row % HALO, 1.0, 0.0).astype(BF16)


def edges_kernel(planes, *rest):
    *noise_refs, near_ref, far_ref = rest
    cols = noise_refs[0].shape[1]
    rows = near_ref.shape[1] // len(noise_refs)
    wide = 2 * HALO
    pick = edge_picker(cols)
    for pair in range(planes // 2):
        edges = []
        for t in (2 * pair, 2 * pair + 1):
            plane = [ref[t * rows : (t + 1) * rows] for ref in noise_refs]
            plane = jnp.concatenate(plane, axis=0)
            edges.append(lax.dot_general(pick, plane, ROWS_BY_ROWS, preferred_element_type=F32))
        at = pl.ds(pair * wide, wide)
        near_ref[at] = jnp.concatenate([e[:HALO] for e in edges], axis=0).astype(BF16)
        far_ref[at] = jnp.concatenate([e[HALO:] for e in edges], axis=0).astype(BF16)


def prepare_rest_kernel(noise_ref, near_ref, far_ref, *out_refs):
    walls, _, height, cols = near_ref.shape
    block = noise_ref.shape[1] // walls
    me = lax.axis_index("wall")
    c = pl.program_id(0)
    target = pl.ds(pl.multiple_of(c * block, block), block)
    for step, out_ref in enumerate(out_refs):
        source = pl.multiple_of((me ^ step) * block, block)
        out_ref[target] = noise_ref[0, pl.ds(source, block)]
    pairs = height // HALO
    pick = edge_picker(cols)
    for w in range(walls):
        edges = []
        for pair in range(pairs):
            plane = noise_ref[0, (w * pairs + pair) * cols : (w * pairs + pair + 1) * cols]
            edges.append(lax.dot_general(pick, plane, ROWS_BY_ROWS, preferred_element_type=F32))
        near_ref[w, c] = jnp.concatenate([e[:HALO] for e in edges], axis=0).astype(BF16)
        far_ref[w, c] = jnp.concatenate([e[HALO:] for e in edges], axis=0).astype(BF16)


def swap_blocks(blocks, cols):
    part = cols // EDGE
    lane = iota(blocks[0].shape, 1)
    for step in (2, 1):
        first = (lane // (part * step)) % 2 == 0
        out = list(blocks)
        for a in range(EDGE):
            if a & step:
                continue
            one, two = blocks[a], blocks[a + step]
            out[a] = jnp.where(first, one, pltpu.roll(two, part * step, 1))
            out[a + step] = jnp.where(first, pltpu.roll(one, cols - part * step, 1), two)
        blocks = out
    return blocks


def halo_tiles(parts, cols):
    half = cols // 2
    sides = []
    for side in parts:
        planes = [[], []]
        for one, two in zip(side[::2], side[1::2]):
            lower = iota(one.shape, 1) < half
            planes[0].append(jnp.where(lower, one, pltpu.roll(two, half, 1)))
            planes[1].append(jnp.where(lower, pltpu.roll(one, half, 1), two))
        sides.append([jnp.concatenate(p, axis=1) for p in planes])
    pairs = sides[0][0].shape[0] // HALO
    zeros = jnp.zeros((cols - 4 * HALO, sides[0][0].shape[1]), F32)
    for pair in range(pairs):
        at = slice(pair * HALO, (pair + 1) * HALO)
        tile = [sides[s][odd][at] for s in range(2) for odd in range(2)]
        yield jnp.concatenate(tile + [zeros], axis=0).astype(BF16)


def span_product(x, matrix):
    cols = x.shape[1]
    both = jnp.dot(jnp.concatenate(split(x), axis=1), matrix, preferred_element_type=F32)
    return both[:, :cols] + both[:, cols:]


def main_part(planes, wall, matrix):
    both = jnp.concatenate(planes, axis=1)
    cols = planes[0].shape[1]
    smooth = jnp.dot(wall, jnp.concatenate([both, both], axis=0), preferred_element_type=F32)
    return [span_product(smooth[:, odd * cols : (odd + 1) * cols], matrix) for odd in range(2)]


def halo_part(tile, wall, halo_ref):
    smooth = lax.dot_general(
        wall, jnp.concatenate([tile, tile], axis=1), ROWS_BY_ROWS, preferred_element_type=F32
    )
    return [span_product(smooth, halo_ref[odd]) for odd in range(2)]


def planes_of(refs, t, rows):
    return [
        jnp.concatenate([ref[at * rows : (at + 1) * rows] for ref in refs], axis=0) for at in (t, t + 1)
    ]


def main_kernel(planes, wall_ref, main_ref, *rest):
    *refs, psi_ref = rest
    rows = psi_ref.shape[1] // len(refs)
    for t in range(0, psi_ref.shape[0], 2):
        c = t // planes
        psi_ref[t], psi_ref[t + 1] = main_part(planes_of(refs, t, rows), wall_ref[c], main_ref[c])


def widen(factor_ref, wide_ref, which):
    for f in which:
        wide_ref[f] = jnp.broadcast_to(factor_ref[:, f : f + 1], wide_ref.shape[1:])


def place_cells(velocity, t, cells_ref, at):
    full, cols = velocity.shape
    quarter, faces = full // EDGE, full // (EDGE * EDGE)
    values = cells_ref.shape[1] // faces
    blocks = [velocity[a * quarter : (a + 1) * quarter] for a in range(EDGE)]
    for dz, block in enumerate(swap_blocks(blocks, cols)):
        for dy in range(EDGE):
            j = t * EDGE * EDGE + dy * EDGE + dz
            cells_ref[at, pl.ds(j, faces, stride=values), :] = block[dy * faces : (dy + 1) * faces]


def scatter_cells(cells_ref, target_ref, sent_ref, out_ref, sems):
    walls, tile_faces, cols = target_ref.shape
    some = cells_ref.shape[0]
    values = cells_ref.shape[1] // (walls * tile_faces)
    _, devices, slots, width = sent_ref.shape
    copies = []
    for w in range(walls):
        payload = [
            [
                cells_ref[at, pl.ds((w * tile_faces + f) * values, values), :].astype(BF16)
                for f in range(tile_faces)
            ]
            for at in range(some)
        ]
        payload = jnp.concatenate([jnp.concatenate(p, axis=1) for p in payload], axis=0)
        slot = iota((devices * slots, cols), 0)
        onehot = [
            jnp.where(slot == target_ref[w, f : f + 1], 1.0, 0.0).astype(BF16)
            for f in range(tile_faces)
        ]
        onehot = jnp.concatenate(onehot, axis=1)
        sent = lax.dot_general(onehot, payload, ROWS_BY_ROWS, preferred_element_type=F32)
        sent_ref[w] = sent.astype(BF16).reshape(devices, slots, width)
        copies.append(pltpu.make_async_copy(sent_ref.at[w], out_ref.at[:, w], sems.at[w]))
        copies[-1].start()
    for copy in copies:
        copy.wait()


def first_kernel(
    planes, psi_in, near_ref, far_ref, factor_ref, target_ref, wall_ref, halo_ref,
    out_ref, psi_out, psi_ref, cells_ref, wide_ref, sent_ref, sems, psi_sem,
):
    full, cols = psi_ref.shape[1:]
    wide = 2 * HALO
    widen(factor_ref, wide_ref, (0, 6))

    def pair_step(pair, carry):
        at = pl.ds(pl.multiple_of(pair * wide, wide), wide)
        tile = [near_ref[at], far_ref[at], jnp.zeros((cols - 2 * wide, full), BF16)]
        beside = halo_part(jnp.concatenate(tile, axis=0), wall_ref[0], halo_ref.at[0])
        for odd in range(2):
            t = 2 * pair + odd
            psi = psi_in[t] + beside[odd]
            psi_ref[t] = psi
            place_cells(wide_ref[6] + wide_ref[0] * psi, t, cells_ref, 0)
        return carry

    lax.fori_loop(0, planes // 2, pair_step, 0, unroll=True)
    copy = pltpu.make_async_copy(psi_ref, psi_out, psi_sem.at[0])
    copy.start()
    scatter_cells(cells_ref, target_ref, sent_ref, out_ref, sems)
    copy.wait()


def rest_kernel(
    planes, psi_ref, next_ref, factor_ref, target_ref, wall_ref, main_ref, halo_ref, *rest,
):
    *late_refs, out_ref, cells_ref, tile_ref, wide_ref, sent_ref, sems = rest
    full, cols = psi_ref.shape[1:]
    some = wall_ref.shape[0]
    pairs = planes // 2
    height = pairs * HALO
    widen(factor_ref, wide_ref, range(1, 6))
    for c in range(some):
        starts = [(side * some + c) * height for side in range(2)]
        parts = [[ref[pl.ds(at, height)].astype(F32) for ref in late_refs] for at in starts]
        for pair, tile in enumerate(halo_tiles(parts, cols)):
            tile_ref[c * pairs + pair] = tile

    for pair in range(pairs):
        psi = []
        for c in range(some):
            main = [next_ref[c * planes + 2 * pair + odd] for odd in range(2)]
            beside = halo_part(tile_ref[c * pairs + pair], wall_ref[c], halo_ref.at[c])
            psi.append([m + b for m, b in zip(main, beside)])
        for odd in range(2):
            t = 2 * pair + odd
            p, q, r = psi_ref[t], psi[0][odd], psi[1][odd]
            place_cells(wide_ref[1] * p + wide_ref[2] * q, t, cells_ref, 0)
            place_cells(wide_ref[3] * p + wide_ref[4] * q + wide_ref[5] * r, t, cells_ref, 1)
    scatter_cells(cells_ref, target_ref, sent_ref, out_ref, sems)


def join_kernel(first, some, in_ref, *rest):
    out_ref, sems = rest[-2:]
    _, walls, _, width = in_ref.shape
    values = width // some
    run(
        [
            pltpu.make_async_copy(
                in_ref.at[:, w, :, pl.ds(c * values, values)],
                out_ref.at[:, :, pl.ds(((c + first) * walls + w) * values, values)],
                sems.at[c, w],
            )
            for c in range(some)
            for w in range(walls)
        ]
    )


def join_narrow_kernel(some, in_ref, *rest):
    out_ref = rest[-1]
    _, walls, _, width = in_ref.shape
    values = width // some
    for c in range(some):

        @pl.when(pl.program_id(1) == c)
        def _():
            for w in range(walls):
                out_ref[0, :, w * values : (w + 1) * values] = in_ref[0, w, :, c * values : (c + 1) * values]


def per_device(noise, wall_scale, span_scale, lund_factor, mean_velocity, owner_map):
    trio, all_planes, rows, cols = noise.shape
    n_span = lax.axis_size("span")
    n_wall = lax.axis_size("wall")
    devices = n_span * n_wall
    planes = all_planes // n_wall
    pairs = planes // 2
    full = rows * n_wall
    faces = full // (EDGE * EDGE)
    values = planes * EDGE * EDGE
    owners = owner_map.reshape(1, -1)
    elements = owners.shape[1]
    slots = max(8, 2 * elements // devices)
    count = elements // cols
    rest = trio - 1
    struct = jax.ShapeDtypeStruct
    hbm = pltpu.MemorySpace.HBM

    def call(kernel, ins, outs, name, limit, scratch=(), grid=(), out_specs=None, us=1):
        specs = out_specs or [VMEM] * len(outs)
        return pl.pallas_call(
            kernel,
            grid=grid,
            in_specs=ins,
            out_specs=specs if len(outs) > 1 else specs[0],
            out_shape=outs if len(outs) > 1 else outs[0],
            scratch_shapes=scratch,
            compiler_params=pltpu.CompilerParams(vmem_limit_bytes=limit * 1024 * 1024),
            cost_estimate=pl.CostEstimate(flops=us * 10**9, bytes_accessed=1024, transcendentals=0),
            name=name,
        )

    core_pairs = [(i, i ^ 1) for i in range(n_span)]
    chip_pairs = [(i, (i + 2 * (i % CORES) - 1) % n_span) for i in range(n_span)]

    def exchange(near, far):
        return lax.ppermute(near, "span", core_pairs), lax.ppermute(far, "span", chip_pairs)

    def spread(blocks):
        return [blocks[0]] + [
            lax.ppermute(x, "wall", [(i, i ^ step) for i in range(n_wall)])
            for step, x in enumerate(blocks[1:], 1)
        ]

    def send(x):
        return lax.all_to_all(x, ("span", "wall"), 0, 0, tiled=True).reshape(devices, n_wall * slots, -1)

    dma = pltpu.SemaphoreType.DMA
    noise = noise.reshape(trio, all_planes * rows, cols)
    packed = call(
        functools.partial(pack_kernel, devices),
        [pl.BlockSpec(memory_space=hbm)] * 4,
        [pltpu.MemorySpace.VMEM((planes * rows + tail_rows(count), cols), BF16)] * n_wall,
        "pack",
        56,
        [
            pltpu.VMEM((all_planes * rows, cols), BF16),
            pltpu.VMEM(lund_factor.shape, F32),
            pltpu.VMEM((1, rows), F32),
            pltpu.VMEM(owners.shape, jnp.int32),
            dma((4,)),
        ],
    )(noise, lund_factor, mean_velocity.reshape(1, rows), owners)
    noise, packed = lax.optimization_barrier((noise, packed))
    packed = spread(packed)

    height = pairs * HALO
    edge = struct((n_wall, rest, height, cols), BF16)
    near, far, *early = call(
        prepare_rest_kernel,
        [pl.BlockSpec((1, all_planes * rows, cols), lambda c: (c + 1, 0, 0))],
        [edge, edge] + [struct((rest * planes * rows, cols), BF16)] * n_wall,
        "prepare_rest",
        16,
        grid=(rest,),
    )(noise)
    rest_near, rest_far = exchange(near, far)
    packed, _ = lax.optimization_barrier((packed, (near, far, early)))

    def taps(first, some, make, name):
        return call(
            functools.partial(taps_kernel, first),
            [SMEM, SMEM],
            [
                make((some, full, 2 * full), BF16),
                make((some, 2 * cols, 2 * cols), BF16),
                make((some, 2, 2 * cols, 2 * cols), BF16),
            ],
            name,
            16,
        )(wall_scale, span_scale)

    wall_first, main_first, halo_first = taps(0, 1, struct, "taps_first")
    factor, target = call(
        functools.partial(small_kernel, slots),
        [VMEM] * n_wall,
        [struct((full, cols), F32), struct((n_wall, count, cols), jnp.int32)],
        "small",
        16,
    )(*packed)

    edge = struct((planes * HALO, full), BF16)
    near, far = call(
        functools.partial(edges_kernel, planes), [VMEM] * n_wall, [edge, edge], "edges_first", 16
    )(*packed)
    near, far = exchange(near, far)
    early, rest_near = lax.optimization_barrier((early, rest_near))
    early = spread(early)
    (rest_near, rest_far), _ = lax.optimization_barrier(((rest_near, rest_far), (near, far)))
    near, rest_near, rest_far = lax.optimization_barrier((near, rest_near, rest_far))

    psi = struct((planes, full, cols), F32)
    psi_main = call(
        functools.partial(main_kernel, planes), [VMEM] * (2 + n_wall), [psi], "main_first", 16
    )(wall_first, main_first, *packed)

    def scratch(some):
        return [
            pltpu.VMEM((some, faces * values, cols), F32),
            pltpu.VMEM((rest * pairs, cols, full), BF16),
            pltpu.VMEM((FACTORS, full, cols), F32),
            pltpu.VMEM((n_wall, devices, slots, some * values), BF16),
            dma((n_wall,)),
        ]

    def out(some):
        return hbm((devices, n_wall, slots, some * values), BF16)

    cells, _, *more = scratch(1)
    sent, psi = call(
        functools.partial(first_kernel, planes),
        [VMEM] * 7,
        [out(1), hbm(psi.shape, F32)],
        "filter_first",
        24,
        [pltpu.VMEM(psi.shape, F32), cells, *more, dma((1,))],
        out_specs=[ANYWHERE, ANYWHERE],
    )(psi_main, near, far, factor, target, wall_first, halo_first)
    (wall_scale, span_scale, rest_near, rest_far), sent = lax.optimization_barrier(
        ((wall_scale, span_scale, rest_near, rest_far), sent)
    )
    got_first = send(sent)
    late = call(
        pack_late_kernel,
        [VMEM] * 2,
        [hbm((2 * rest * height, cols), BF16)] * n_wall,
        "pack_late",
        16,
        [dma((n_wall, 2 * rest))],
        out_specs=[ANYWHERE] * n_wall,
    )(rest_near, rest_far)
    late = spread(late)
    wall_rest, main_rest, halo_rest = taps(1, rest, struct, "taps_rest")
    psi_next = call(
        functools.partial(main_kernel, planes),
        [VMEM] * (2 + n_wall),
        [struct((rest * planes, full, cols), F32)],
        "main_next",
        16,
    )(wall_rest, main_rest, *early)
    sent = call(
        functools.partial(rest_kernel, planes),
        [VMEM] * (7 + n_wall),
        [out(rest)],
        "filter_rest",
        32,
        scratch(rest),
        out_specs=[ANYWHERE],
        us=100,
    )(psi, psi_next, factor, target, wall_rest, main_rest, halo_rest, *late)
    got_rest = send(sent)

    whole = hbm((n_span, n_wall * slots, trio * values * n_wall), BF16)
    narrow = values % LANES != 0

    def join(received, some, before):
        keep = [] if before is None else [before]
        shape = (n_span, n_wall, n_wall * slots, some * values)
        return pl.pallas_call(
            functools.partial(join_narrow_kernel, some)
            if narrow
            else functools.partial(join_kernel, len(keep), some),
            grid=(n_span, some) if narrow else (),
            in_specs=[pl.BlockSpec((1, *shape[1:]), lambda s, c: (s, 0, 0, 0)) if narrow else VMEM]
            + [ANYWHERE] * len(keep),
            out_specs=pl.BlockSpec((1, n_wall * slots, values * n_wall), lambda s, c: (s, 0, c + len(keep)))
            if narrow
            else ANYWHERE,
            out_shape=whole,
            scratch_shapes=[] if narrow else [dma((some, n_wall))],
            input_output_aliases={1: 0} if keep else {},
            compiler_params=pltpu.CompilerParams(vmem_limit_bytes=16 * 1024 * 1024),
            name="join",
        )(received.reshape(shape), *keep)

    return join(got_rest, rest, join(got_first, 1, None)).reshape(1, devices * slots, -1)


def solution(mesh):
    return jax.shard_map(
        per_device,
        mesh=mesh,
        in_specs=(
            P(None, None, "wall", "span"),
            P(),
            P(),
            P(None, "wall"),
            P("wall"),
            P("wall", "span", None, None),
        ),
        out_specs=P(("span", "wall"), None, None),
        check_vma=False,
    )
```

```python
import functools
import math

import jax
import jax.numpy as jnp
from jax import lax
from jax.experimental import pallas as pl
from jax.experimental.pallas import tpu as pltpu
from jax.sharding import PartitionSpec as P

HALO = 24
EDGE = 4
LANES = 128
FACTORS = 7
CORES = 2
F32 = jnp.float32
BF16 = jnp.bfloat16
VMEM = pl.BlockSpec(memory_space=pltpu.VMEM)
ANYWHERE = pl.BlockSpec(memory_space=pl.ANY)
SMEM = pl.BlockSpec(memory_space=pltpu.SMEM)
ROWS_BY_ROWS = (((1,), (1,)), ((), ()))


def iota(shape, dim):
    return lax.broadcasted_iota(jnp.int32, shape, dim)


def split(x):
    high = x.astype(BF16)
    return high, (x - high.astype(F32)).astype(BF16)


def tap_values(scale, distance, valid):
    scale = jnp.full((1, 1), scale, F32)
    k = iota((1, LANES), 1) - HALO
    squares = jnp.where(k <= HALO, jnp.exp(-math.pi * (k * k).astype(F32) / (scale * scale)), 0.0)
    norm = jnp.sqrt(jnp.sum(squares, axis=1, keepdims=True))
    d = distance.astype(F32)
    raw = jnp.exp(-math.pi * (d * d) / (2.0 * scale * scale))
    inside = valid & (distance >= -HALO) & (distance <= HALO)
    return jnp.where(inside, raw, 0.0) / norm


def tail_rows(count):
    return -(-(2 * count + 3 * FACTORS) // 16) * 16


def cell_row(i, faces):
    return (i % faces) * (EDGE * EDGE) + (i // (faces * EDGE)) * EDGE + (i // faces) % EDGE


def taps_kernel(first, wall_scale, span_scale, wall_ref, main_ref, halo_ref):
    some, full, _ = wall_ref.shape
    cols = main_ref.shape[1] // 2
    walls = lax.axis_size("wall")
    rows = full // walls
    i, j = iota((full, full), 0), iota((full, full), 1)
    y = cell_row(i, full // (EDGE * EDGE))
    source = lax.axis_index("wall") ^ (j // rows)
    column = source * rows + j % rows
    n = iota((cols, cols), 1)
    target = (n % (cols // EDGE)) * EDGE + n // (cols // EDGE)
    k = iota((cols, cols), 0)
    side, odd, r = k // (2 * HALO), (k // HALO) % 2, k % HALO
    core = lax.rem(lax.axis_index("span"), CORES)
    z = jnp.where(side + core == 1, r - HALO, cols + r)

    def span_matrix(scale, distance, valid):
        high, low = split(tap_values(scale, distance, valid))
        top = jnp.concatenate([high, low], axis=1)
        return jnp.concatenate([top, jnp.concatenate([high, jnp.zeros_like(high)], axis=1)], axis=0)

    for c in range(some):
        high, low = split(tap_values(wall_scale[first + c], column - y, i >= 0))
        wall_ref[c, :, :full] = high
        wall_ref[c, :, full:] = low
        scale = span_scale[first + c]
        main_ref[c] = span_matrix(scale, k - target, k >= 0)
        for parity in range(2):
            valid = (k < 4 * HALO) & (odd == parity)
            halo_ref[c, parity] = span_matrix(scale, z - target, valid)


def run(copies):
    for copy in copies:
        copy.start()
    for copy in copies:
        copy.wait()


def pack_kernel(devices, noise_in, lund_in, mean_in, owner_in, *rest):
    *out_refs, noise_ref, lund_ref, mean_ref, owner_ref, sems = rest
    walls = len(out_refs)
    cols = noise_ref.shape[1]
    block = noise_ref.shape[0] // walls
    tail = out_refs[0].shape[0] - block
    rows = mean_ref.shape[1]
    me = lax.axis_index("wall")
    pairs = ((lund_in, lund_ref), (mean_in, mean_ref), (owner_in, owner_ref), (noise_in.at[0], noise_ref))
    *small, noise = [pltpu.make_async_copy(a, b, sems.at[i]) for i, (a, b) in enumerate(pairs)]
    noise.start()
    run(small)
    owner = owner_ref[...]
    elements = owner.shape[1]
    mine = jnp.where(iota((devices, elements), 0) == owner, 1.0, 0.0)
    before = jnp.where(iota((elements, elements), 0) < iota((elements, elements), 1), 1.0, 0.0)
    count = jnp.dot(mine.astype(BF16), before.astype(BF16), preferred_element_type=F32)
    rank = jnp.sum(mine * count, axis=0, keepdims=True)
    pieces = [owner.astype(F32), rank]
    pieces = [p[:, at : at + cols] for p in pieces for at in range(0, elements, cols)]
    factor = jnp.concatenate([lund_ref[...], mean_ref[...]], axis=0)
    factor = jnp.concatenate([factor, jnp.zeros((FACTORS, cols - rows), F32)], axis=1)
    for _ in range(3):
        part = factor.astype(BF16).astype(F32)
        pieces.append(part)
        factor = factor - part
    pieces.append(jnp.zeros((tail - sum(p.shape[0] for p in pieces), cols), F32))
    small = jnp.concatenate(pieces, axis=0).astype(BF16)
    noise.wait()
    for step, out_ref in enumerate(out_refs):
        start = pl.multiple_of((me ^ step) * block, block)
        out_ref[:block] = noise_ref[pl.ds(start, block)]
        out_ref[block:] = small


def pack_late_kernel(near_ref, far_ref, *rest):
    out_refs, sems = rest[:-1], rest[-1]
    walls, some, height, _ = near_ref.shape
    me = lax.axis_index("wall")
    copies = []
    for step, out_ref in enumerate(out_refs):
        to = (me ^ step)
        for side, ref in enumerate((near_ref, far_ref)):
            for c in range(some):
                at = side * some + c
                copies.append(
                    pltpu.make_async_copy(
                        ref.at[to, c], out_ref.at[pl.ds(at * height, height)], sems.at[step, at]
                    )
                )
    run(copies)


def small_kernel(slots, *rest):
    *in_refs, factor_ref, target_ref = rest
    walls = len(in_refs)
    height, cols = in_refs[0].shape
    full = factor_ref.shape[0]
    rows = full // walls
    count = target_ref.shape[1]
    tail = tail_rows(count)
    me = lax.axis_index("wall")
    columns = jnp.zeros((full, tail), F32)
    y = cell_row(iota((full, cols), 0), full // (EDGE * EDGE))
    for step, in_ref in enumerate(in_refs):
        w = me ^ step
        small = in_ref[height - tail :]
        pick = jnp.where(y == iota((full, cols), 1) + w * rows, 1.0, 0.0)
        pick = jnp.where(iota((full, cols), 1) < rows, pick, 0.0).astype(BF16)
        columns = columns + lax.dot_general(pick, small, ROWS_BY_ROWS, preferred_element_type=F32)
        numbers = small.astype(F32)
        target = numbers[:count] * slots + numbers[count : 2 * count]
        target_ref[pl.ds(w, 1)] = target.astype(jnp.int32)[None]
    at = 2 * count
    factor = sum(columns[:, at + p * FACTORS : at + (p + 1) * FACTORS] for p in range(3))
    factor_ref[...] = jnp.concatenate([factor, jnp.zeros((full, cols - FACTORS), F32)], axis=1)


def edge_picker(cols):
    core = lax.rem(lax.axis_index("span"), CORES)
    row, col = iota((2 * HALO, cols), 0), iota((2 * HALO, cols), 1)
    start = jnp.where(row // HALO == core, cols - HALO, 0)
    return jnp.where(col == start + row % HALO, 1.0, 0.0).astype(BF16)


def edges_kernel(planes, *rest):
    *noise_refs, near_ref, far_ref = rest
    cols = noise_refs[0].shape[1]
    rows = near_ref.shape[1] // len(noise_refs)
    wide = 2 * HALO
    pick = edge_picker(cols)
    for pair in range(planes // 2):
        edges = []
        for t in (2 * pair, 2 * pair + 1):
            plane = [ref[t * rows : (t + 1) * rows] for ref in noise_refs]
            plane = jnp.concatenate(plane, axis=0)
            edges.append(lax.dot_general(pick, plane, ROWS_BY_ROWS, preferred_element_type=F32))
        at = pl.ds(pair * wide, wide)
        near_ref[at] = jnp.concatenate([e[:HALO] for e in edges], axis=0).astype(BF16)
        far_ref[at] = jnp.concatenate([e[HALO:] for e in edges], axis=0).astype(BF16)


def prepare_rest_kernel(noise_ref, near_ref, far_ref, *out_refs):
    walls, _, height, cols = near_ref.shape
    block = noise_ref.shape[1] // walls
    me = lax.axis_index("wall")
    c = pl.program_id(0)
    target = pl.ds(pl.multiple_of(c * block, block), block)
    for step, out_ref in enumerate(out_refs):
        source = pl.multiple_of((me ^ step) * block, block)
        out_ref[target] = noise_ref[0, pl.ds(source, block)]
    pairs = height // HALO
    pick = edge_picker(cols)
    for w in range(walls):
        edges = []
        for pair in range(pairs):
            plane = noise_ref[0, (w * pairs + pair) * cols : (w * pairs + pair + 1) * cols]
            edges.append(lax.dot_general(pick, plane, ROWS_BY_ROWS, preferred_element_type=F32))
        near_ref[w, c] = jnp.concatenate([e[:HALO] for e in edges], axis=0).astype(BF16)
        far_ref[w, c] = jnp.concatenate([e[HALO:] for e in edges], axis=0).astype(BF16)


def swap_blocks(blocks, cols):
    part = cols // EDGE
    lane = iota(blocks[0].shape, 1)
    for step in (2, 1):
        first = (lane // (part * step)) % 2 == 0
        out = list(blocks)
        for a in range(EDGE):
            if a & step:
                continue
            one, two = blocks[a], blocks[a + step]
            out[a] = jnp.where(first, one, pltpu.roll(two, part * step, 1))
            out[a + step] = jnp.where(first, pltpu.roll(one, cols - part * step, 1), two)
        blocks = out
    return blocks


def halo_tiles(parts, cols):
    half = cols // 2
    sides = []
    for side in parts:
        planes = [[], []]
        for one, two in zip(side[::2], side[1::2]):
            lower = iota(one.shape, 1) < half
            planes[0].append(jnp.where(lower, one, pltpu.roll(two, half, 1)))
            planes[1].append(jnp.where(lower, pltpu.roll(one, half, 1), two))
        sides.append([jnp.concatenate(p, axis=1) for p in planes])
    pairs = sides[0][0].shape[0] // HALO
    zeros = jnp.zeros((cols - 4 * HALO, sides[0][0].shape[1]), F32)
    for pair in range(pairs):
        at = slice(pair * HALO, (pair + 1) * HALO)
        tile = [sides[s][odd][at] for s in range(2) for odd in range(2)]
        yield jnp.concatenate(tile + [zeros], axis=0).astype(BF16)


def span_product(x, matrix):
    cols = x.shape[1]
    both = jnp.dot(jnp.concatenate(split(x), axis=1), matrix, preferred_element_type=F32)
    return both[:, :cols] + both[:, cols:]


def main_part(planes, wall, matrix):
    both = jnp.concatenate(planes, axis=1)
    cols = planes[0].shape[1]
    smooth = jnp.dot(wall, jnp.concatenate([both, both], axis=0), preferred_element_type=F32)
    return [span_product(smooth[:, odd * cols : (odd + 1) * cols], matrix) for odd in range(2)]


def halo_part(tile, wall, halo_ref):
    smooth = lax.dot_general(
        wall, jnp.concatenate([tile, tile], axis=1), ROWS_BY_ROWS, preferred_element_type=F32
    )
    return [span_product(smooth, halo_ref[odd]) for odd in range(2)]


def planes_of(refs, t, rows):
    return [
        jnp.concatenate([ref[at * rows : (at + 1) * rows] for ref in refs], axis=0) for at in (t, t + 1)
    ]


def main_kernel(planes, wall_ref, main_ref, *rest):
    *refs, psi_ref = rest
    rows = psi_ref.shape[1] // len(refs)
    for t in range(0, psi_ref.shape[0], 2):
        c = t // planes
        psi_ref[t], psi_ref[t + 1] = main_part(planes_of(refs, t, rows), wall_ref[c], main_ref[c])


def widen(factor_ref, wide_ref, which):
    for f in which:
        wide_ref[f] = jnp.broadcast_to(factor_ref[:, f : f + 1], wide_ref.shape[1:])


def place_cells(velocity, t, cells_ref, at):
    full, cols = velocity.shape
    quarter, faces = full // EDGE, full // (EDGE * EDGE)
    values = cells_ref.shape[1] // faces
    blocks = [velocity[a * quarter : (a + 1) * quarter] for a in range(EDGE)]
    for dz, block in enumerate(swap_blocks(blocks, cols)):
        for dy in range(EDGE):
            j = t * EDGE * EDGE + dy * EDGE + dz
            cells_ref[at, pl.ds(j, faces, stride=values), :] = block[dy * faces : (dy + 1) * faces]


def scatter_cells(cells_ref, target_ref, sent_ref, out_ref, sems):
    walls, tile_faces, cols = target_ref.shape
    some = cells_ref.shape[0]
    values = cells_ref.shape[1] // (walls * tile_faces)
    _, devices, slots, width = sent_ref.shape
    copies = []
    for w in range(walls):
        payload = [
            [
                cells_ref[at, pl.ds((w * tile_faces + f) * values, values), :].astype(BF16)
                for f in range(tile_faces)
            ]
            for at in range(some)
        ]
        payload = jnp.concatenate([jnp.concatenate(p, axis=1) for p in payload], axis=0)
        slot = iota((devices * slots, cols), 0)
        onehot = [
            jnp.where(slot == target_ref[w, f : f + 1], 1.0, 0.0).astype(BF16)
            for f in range(tile_faces)
        ]
        onehot = jnp.concatenate(onehot, axis=1)
        sent = lax.dot_general(onehot, payload, ROWS_BY_ROWS, preferred_element_type=F32)
        sent_ref[w] = sent.astype(BF16).reshape(devices, slots, width)
        copies.append(pltpu.make_async_copy(sent_ref.at[w], out_ref.at[:, w], sems.at[w]))
        copies[-1].start()
    for copy in copies:
        copy.wait()


def first_kernel(
    planes, psi_in, near_ref, far_ref, factor_ref, target_ref, wall_ref, halo_ref,
    out_ref, psi_out, psi_ref, cells_ref, wide_ref, sent_ref, sems, psi_sem,
):
    full, cols = psi_ref.shape[1:]
    wide = 2 * HALO
    widen(factor_ref, wide_ref, (0, 6))

    def psi_copy(pair):
        at = pl.ds(2 * pair, 2)
        return pltpu.make_async_copy(psi_ref.at[at], psi_out.at[at], psi_sem.at[pair])

    def pair_step(pair, carry):
        at = pl.ds(pl.multiple_of(pair * wide, wide), wide)
        tile = [near_ref[at], far_ref[at], jnp.zeros((cols - 2 * wide, full), BF16)]
        beside = halo_part(jnp.concatenate(tile, axis=0), wall_ref[0], halo_ref.at[0])
        for odd in range(2):
            t = 2 * pair + odd
            psi = psi_in[t] + beside[odd]
            psi_ref[t] = psi
            place_cells(wide_ref[6] + wide_ref[0] * psi, t, cells_ref, 0)
        psi_copy(pair).start()
        return carry

    lax.fori_loop(0, planes // 2, pair_step, 0, unroll=True)
    scatter_cells(cells_ref, target_ref, sent_ref, out_ref, sems)
    for pair in range(planes // 2):
        psi_copy(pair).wait()


def rest_kernel(
    planes, psi_ref, next_ref, factor_ref, target_ref, wall_ref, main_ref, halo_ref, *rest,
):
    *late_refs, out_ref, cells_ref, tile_ref, wide_ref, sent_ref, sems = rest
    full, cols = psi_ref.shape[1:]
    some = wall_ref.shape[0]
    pairs = planes // 2
    height = pairs * HALO
    widen(factor_ref, wide_ref, range(1, 6))
    for c in range(some):
        starts = [(side * some + c) * height for side in range(2)]
        parts = [[ref[pl.ds(at, height)].astype(F32) for ref in late_refs] for at in starts]
        for pair, tile in enumerate(halo_tiles(parts, cols)):
            tile_ref[c * pairs + pair] = tile

    for pair in range(pairs):
        psi = []
        for c in range(some):
            main = [next_ref[c * planes + 2 * pair + odd] for odd in range(2)]
            beside = halo_part(tile_ref[c * pairs + pair], wall_ref[c], halo_ref.at[c])
            psi.append([m + b for m, b in zip(main, beside)])
        for odd in range(2):
            t = 2 * pair + odd
            p, q, r = psi_ref[t], psi[0][odd], psi[1][odd]
            place_cells(wide_ref[1] * p + wide_ref[2] * q, t, cells_ref, 0)
            place_cells(wide_ref[3] * p + wide_ref[4] * q + wide_ref[5] * r, t, cells_ref, 1)
    scatter_cells(cells_ref, target_ref, sent_ref, out_ref, sems)


def join_kernel(first, some, in_ref, *rest):
    out_ref, sems = rest[-2:]
    _, walls, _, width = in_ref.shape
    values = width // some
    run(
        [
            pltpu.make_async_copy(
                in_ref.at[:, w, :, pl.ds(c * values, values)],
                out_ref.at[:, :, pl.ds(((c + first) * walls + w) * values, values)],
                sems.at[c, w],
            )
            for c in range(some)
            for w in range(walls)
        ]
    )


def join_narrow_kernel(some, in_ref, *rest):
    out_ref = rest[-1]
    _, walls, _, width = in_ref.shape
    values = width // some
    for c in range(some):

        @pl.when(pl.program_id(1) == c)
        def _():
            for w in range(walls):
                out_ref[0, :, w * values : (w + 1) * values] = in_ref[0, w, :, c * values : (c + 1) * values]


def per_device(noise, wall_scale, span_scale, lund_factor, mean_velocity, owner_map):
    trio, all_planes, rows, cols = noise.shape
    n_span = lax.axis_size("span")
    n_wall = lax.axis_size("wall")
    devices = n_span * n_wall
    planes = all_planes // n_wall
    pairs = planes // 2
    full = rows * n_wall
    faces = full // (EDGE * EDGE)
    values = planes * EDGE * EDGE
    owners = owner_map.reshape(1, -1)
    elements = owners.shape[1]
    slots = max(8, 2 * elements // devices)
    count = elements // cols
    rest = trio - 1
    struct = jax.ShapeDtypeStruct
    hbm = pltpu.MemorySpace.HBM

    def call(kernel, ins, outs, name, limit, scratch=(), grid=(), out_specs=None, us=1):
        specs = out_specs or [VMEM] * len(outs)
        return pl.pallas_call(
            kernel,
            grid=grid,
            in_specs=ins,
            out_specs=specs if len(outs) > 1 else specs[0],
            out_shape=outs if len(outs) > 1 else outs[0],
            scratch_shapes=scratch,
            compiler_params=pltpu.CompilerParams(vmem_limit_bytes=limit * 1024 * 1024),
            cost_estimate=pl.CostEstimate(flops=us * 10**9, bytes_accessed=1024, transcendentals=0),
            name=name,
        )

    core_pairs = [(i, i ^ 1) for i in range(n_span)]
    chip_pairs = [(i, (i + 2 * (i % CORES) - 1) % n_span) for i in range(n_span)]

    def exchange(near, far):
        return lax.ppermute(near, "span", core_pairs), lax.ppermute(far, "span", chip_pairs)

    def spread(blocks):
        return [blocks[0]] + [
            lax.ppermute(x, "wall", [(i, i ^ step) for i in range(n_wall)])
            for step, x in enumerate(blocks[1:], 1)
        ]

    def send(x):
        return lax.all_to_all(x, ("span", "wall"), 0, 0, tiled=True).reshape(devices, n_wall * slots, -1)

    dma = pltpu.SemaphoreType.DMA
    noise = noise.reshape(trio, all_planes * rows, cols)
    packed = call(
        functools.partial(pack_kernel, devices),
        [pl.BlockSpec(memory_space=hbm)] * 4,
        [pltpu.MemorySpace.VMEM((planes * rows + tail_rows(count), cols), BF16)] * n_wall,
        "pack",
        56,
        [
            pltpu.VMEM((all_planes * rows, cols), BF16),
            pltpu.VMEM(lund_factor.shape, F32),
            pltpu.VMEM((1, rows), F32),
            pltpu.VMEM(owners.shape, jnp.int32),
            dma((4,)),
        ],
    )(noise, lund_factor, mean_velocity.reshape(1, rows), owners)
    noise, packed = lax.optimization_barrier((noise, packed))
    packed = spread(packed)

    height = pairs * HALO
    edge = struct((n_wall, rest, height, cols), BF16)
    near, far, *early = call(
        prepare_rest_kernel,
        [pl.BlockSpec((1, all_planes * rows, cols), lambda c: (c + 1, 0, 0))],
        [edge, edge] + [struct((rest * planes * rows, cols), BF16)] * n_wall,
        "prepare_rest",
        16,
        grid=(rest,),
    )(noise)
    rest_near, rest_far = exchange(near, far)
    packed, _ = lax.optimization_barrier((packed, (near, far, early)))

    def taps(first, some, make, name):
        return call(
            functools.partial(taps_kernel, first),
            [SMEM, SMEM],
            [
                make((some, full, 2 * full), BF16),
                make((some, 2 * cols, 2 * cols), BF16),
                make((some, 2, 2 * cols, 2 * cols), BF16),
            ],
            name,
            16,
        )(wall_scale, span_scale)

    wall_first, main_first, halo_first = taps(0, 1, struct, "taps_first")
    factor, target = call(
        functools.partial(small_kernel, slots),
        [VMEM] * n_wall,
        [struct((full, cols), F32), struct((n_wall, count, cols), jnp.int32)],
        "small",
        16,
    )(*packed)

    edge = struct((planes * HALO, full), BF16)
    near, far = call(
        functools.partial(edges_kernel, planes), [VMEM] * n_wall, [edge, edge], "edges_first", 16
    )(*packed)
    near, far = exchange(near, far)
    early, rest_near = lax.optimization_barrier((early, rest_near))
    early = spread(early)
    (rest_near, rest_far), _ = lax.optimization_barrier(((rest_near, rest_far), (near, far)))
    near, rest_near, rest_far = lax.optimization_barrier((near, rest_near, rest_far))

    psi = struct((planes, full, cols), F32)
    psi_main = call(
        functools.partial(main_kernel, planes), [VMEM] * (2 + n_wall), [psi], "main_first", 16
    )(wall_first, main_first, *packed)

    def scratch(some):
        return [
            pltpu.VMEM((some, faces * values, cols), F32),
            pltpu.VMEM((rest * pairs, cols, full), BF16),
            pltpu.VMEM((FACTORS, full, cols), F32),
            pltpu.VMEM((n_wall, devices, slots, some * values), BF16),
            dma((n_wall,)),
        ]

    def out(some):
        return hbm((devices, n_wall, slots, some * values), BF16)

    cells, _, *more = scratch(1)
    sent, psi = call(
        functools.partial(first_kernel, planes),
        [VMEM] * 7,
        [out(1), hbm(psi.shape, F32)],
        "filter_first",
        24,
        [pltpu.VMEM(psi.shape, F32), cells, *more, dma((pairs,))],
        out_specs=[ANYWHERE, ANYWHERE],
    )(psi_main, near, far, factor, target, wall_first, halo_first)
    (wall_scale, span_scale, rest_near, rest_far), sent = lax.optimization_barrier(
        ((wall_scale, span_scale, rest_near, rest_far), sent)
    )
    got_first = send(sent)
    late = call(
        pack_late_kernel,
        [VMEM] * 2,
        [hbm((2 * rest * height, cols), BF16)] * n_wall,
        "pack_late",
        16,
        [dma((n_wall, 2 * rest))],
        out_specs=[ANYWHERE] * n_wall,
    )(rest_near, rest_far)
    late = spread(late)
    wall_rest, main_rest, halo_rest = taps(1, rest, struct, "taps_rest")
    psi_next = call(
        functools.partial(main_kernel, planes),
        [VMEM] * (2 + n_wall),
        [struct((rest * planes, full, cols), F32)],
        "main_next",
        16,
    )(wall_rest, main_rest, *early)
    sent = call(
        functools.partial(rest_kernel, planes),
        [VMEM] * (7 + n_wall),
        [out(rest)],
        "filter_rest",
        32,
        scratch(rest),
        out_specs=[ANYWHERE],
        us=100,
    )(psi, psi_next, factor, target, wall_rest, main_rest, halo_rest, *late)
    got_rest = send(sent)

    whole = hbm((n_span, n_wall * slots, trio * values * n_wall), BF16)
    narrow = values % LANES != 0

    def join(received, some, before):
        keep = [] if before is None else [before]
        shape = (n_span, n_wall, n_wall * slots, some * values)
        return pl.pallas_call(
            functools.partial(join_narrow_kernel, some)
            if narrow
            else functools.partial(join_kernel, len(keep), some),
            grid=(n_span, some) if narrow else (),
            in_specs=[pl.BlockSpec((1, *shape[1:]), lambda s, c: (s, 0, 0, 0)) if narrow else VMEM]
            + [ANYWHERE] * len(keep),
            out_specs=pl.BlockSpec((1, n_wall * slots, values * n_wall), lambda s, c: (s, 0, c + len(keep)))
            if narrow
            else ANYWHERE,
            out_shape=whole,
            scratch_shapes=[] if narrow else [dma((some, n_wall))],
            input_output_aliases={1: 0} if keep else {},
            compiler_params=pltpu.CompilerParams(vmem_limit_bytes=16 * 1024 * 1024),
            name="join",
        )(received.reshape(shape), *keep)

    return join(got_rest, rest, join(got_first, 1, None)).reshape(1, devices * slots, -1)


def solution(mesh):
    return jax.shard_map(
        per_device,
        mesh=mesh,
        in_specs=(
            P(None, None, "wall", "span"),
            P(),
            P(),
            P(None, "wall"),
            P("wall"),
            P("wall", "span", None, None),
        ),
        out_specs=P(("span", "wall"), None, None),
        check_vma=False,
    )
```

```python
import functools
import math

import jax
import jax.numpy as jnp
from jax import lax
from jax.experimental import pallas as pl
from jax.experimental.pallas import tpu as pltpu
from jax.sharding import PartitionSpec as P

HALO = 24
EDGE = 4
LANES = 128
FACTORS = 7
CORES = 2
F32 = jnp.float32
BF16 = jnp.bfloat16
VMEM = pl.BlockSpec(memory_space=pltpu.VMEM)
ANYWHERE = pl.BlockSpec(memory_space=pl.ANY)
SMEM = pl.BlockSpec(memory_space=pltpu.SMEM)
ROWS_BY_ROWS = (((1,), (1,)), ((), ()))


def iota(shape, dim):
    return lax.broadcasted_iota(jnp.int32, shape, dim)


def split(x):
    high = x.astype(BF16)
    return high, (x - high.astype(F32)).astype(BF16)


def tap_values(scale, distance, valid):
    scale = jnp.full((1, 1), scale, F32)
    k = iota((1, LANES), 1) - HALO
    squares = jnp.where(k <= HALO, jnp.exp(-math.pi * (k * k).astype(F32) / (scale * scale)), 0.0)
    norm = jnp.sqrt(jnp.sum(squares, axis=1, keepdims=True))
    d = distance.astype(F32)
    raw = jnp.exp(-math.pi * (d * d) / (2.0 * scale * scale))
    inside = valid & (distance >= -HALO) & (distance <= HALO)
    return jnp.where(inside, raw, 0.0) / norm


def tail_rows(count):
    return -(-(2 * count + 3 * FACTORS) // 16) * 16


def cell_row(i, faces):
    return (i % faces) * (EDGE * EDGE) + (i // (faces * EDGE)) * EDGE + (i // faces) % EDGE


def taps_kernel(first, wall_scale, span_scale, wall_ref, main_ref, halo_ref):
    some, full, _ = wall_ref.shape
    cols = main_ref.shape[1] // 2
    walls = lax.axis_size("wall")
    rows = full // walls
    i, j = iota((full, full), 0), iota((full, full), 1)
    y = cell_row(i, full // (EDGE * EDGE))
    source = lax.axis_index("wall") ^ (j // rows)
    column = source * rows + j % rows
    n = iota((cols, cols), 1)
    target = (n % (cols // EDGE)) * EDGE + n // (cols // EDGE)
    k = iota((cols, cols), 0)
    side, odd, r = k // (2 * HALO), (k // HALO) % 2, k % HALO
    core = lax.rem(lax.axis_index("span"), CORES)
    z = jnp.where(side + core == 1, r - HALO, cols + r)

    def span_matrix(scale, distance, valid):
        high, low = split(tap_values(scale, distance, valid))
        top = jnp.concatenate([high, low], axis=1)
        return jnp.concatenate([top, jnp.concatenate([high, jnp.zeros_like(high)], axis=1)], axis=0)

    for c in range(some):
        high, low = split(tap_values(wall_scale[first + c], column - y, i >= 0))
        wall_ref[c, :, :full] = high
        wall_ref[c, :, full:] = low
        scale = span_scale[first + c]
        main_ref[c] = span_matrix(scale, k - target, k >= 0)
        for parity in range(2):
            valid = (k < 4 * HALO) & (odd == parity)
            halo_ref[c, parity] = span_matrix(scale, z - target, valid)


def run(copies):
    for copy in copies:
        copy.start()
    for copy in copies:
        copy.wait()


def pack_kernel(devices, noise_in, lund_in, mean_in, owner_in, *rest):
    *out_refs, noise_ref, lund_ref, mean_ref, owner_ref, sems = rest
    walls = len(out_refs)
    cols = noise_ref.shape[1]
    block = noise_ref.shape[0] // walls
    tail = out_refs[0].shape[0] - block
    rows = mean_ref.shape[1]
    me = lax.axis_index("wall")
    pairs = ((lund_in, lund_ref), (mean_in, mean_ref), (owner_in, owner_ref), (noise_in.at[0], noise_ref))
    *small, noise = [pltpu.make_async_copy(a, b, sems.at[i]) for i, (a, b) in enumerate(pairs)]
    noise.start()
    run(small)
    owner = owner_ref[...]
    elements = owner.shape[1]
    mine = jnp.where(iota((devices, elements), 0) == owner, 1.0, 0.0)
    before = jnp.where(iota((elements, elements), 0) < iota((elements, elements), 1), 1.0, 0.0)
    count = jnp.dot(mine.astype(BF16), before.astype(BF16), preferred_element_type=F32)
    rank = jnp.sum(mine * count, axis=0, keepdims=True)
    pieces = [owner.astype(F32), rank]
    pieces = [p[:, at : at + cols] for p in pieces for at in range(0, elements, cols)]
    factor = jnp.concatenate([lund_ref[...], mean_ref[...]], axis=0)
    factor = jnp.concatenate([factor, jnp.zeros((FACTORS, cols - rows), F32)], axis=1)
    for _ in range(3):
        part = factor.astype(BF16).astype(F32)
        pieces.append(part)
        factor = factor - part
    pieces.append(jnp.zeros((tail - sum(p.shape[0] for p in pieces), cols), F32))
    small = jnp.concatenate(pieces, axis=0).astype(BF16)
    noise.wait()
    for step, out_ref in enumerate(out_refs):
        start = pl.multiple_of((me ^ step) * block, block)
        out_ref[:block] = noise_ref[pl.ds(start, block)]
        out_ref[block:] = small


def pack_late_kernel(near_ref, far_ref, *rest):
    out_refs, sems = rest[:-1], rest[-1]
    walls, some, height, _ = near_ref.shape
    me = lax.axis_index("wall")
    copies = []
    for step, out_ref in enumerate(out_refs):
        to = (me ^ step)
        for side, ref in enumerate((near_ref, far_ref)):
            for c in range(some):
                at = side * some + c
                copies.append(
                    pltpu.make_async_copy(
                        ref.at[to, c], out_ref.at[pl.ds(at * height, height)], sems.at[step, at]
                    )
                )
    run(copies)


def small_kernel(slots, *rest):
    *in_refs, factor_ref, target_ref = rest
    walls = len(in_refs)
    height, cols = in_refs[0].shape
    full = factor_ref.shape[0]
    rows = full // walls
    count = target_ref.shape[1]
    tail = tail_rows(count)
    me = lax.axis_index("wall")
    columns = jnp.zeros((full, tail), F32)
    y = cell_row(iota((full, cols), 0), full // (EDGE * EDGE))
    for step, in_ref in enumerate(in_refs):
        w = me ^ step
        small = in_ref[height - tail :]
        pick = jnp.where(y == iota((full, cols), 1) + w * rows, 1.0, 0.0)
        pick = jnp.where(iota((full, cols), 1) < rows, pick, 0.0).astype(BF16)
        columns = columns + lax.dot_general(pick, small, ROWS_BY_ROWS, preferred_element_type=F32)
        numbers = small.astype(F32)
        target = numbers[:count] * slots + numbers[count : 2 * count]
        target_ref[pl.ds(w, 1)] = target.astype(jnp.int32)[None]
    at = 2 * count
    factor = sum(columns[:, at + p * FACTORS : at + (p + 1) * FACTORS] for p in range(3))
    factor_ref[...] = jnp.concatenate([factor, jnp.zeros((full, cols - FACTORS), F32)], axis=1)


def edge_picker(cols):
    core = lax.rem(lax.axis_index("span"), CORES)
    row, col = iota((2 * HALO, cols), 0), iota((2 * HALO, cols), 1)
    start = jnp.where(row // HALO == core, cols - HALO, 0)
    return jnp.where(col == start + row % HALO, 1.0, 0.0).astype(BF16)


def edges_kernel(planes, *rest):
    *noise_refs, near_ref, far_ref = rest
    cols = noise_refs[0].shape[1]
    rows = near_ref.shape[1] // len(noise_refs)
    wide = 2 * HALO
    pick = edge_picker(cols)
    for pair in range(planes // 2):
        edges = []
        for t in (2 * pair, 2 * pair + 1):
            plane = [ref[t * rows : (t + 1) * rows] for ref in noise_refs]
            plane = jnp.concatenate(plane, axis=0)
            edges.append(lax.dot_general(pick, plane, ROWS_BY_ROWS, preferred_element_type=F32))
        at = pl.ds(pair * wide, wide)
        near_ref[at] = jnp.concatenate([e[:HALO] for e in edges], axis=0).astype(BF16)
        far_ref[at] = jnp.concatenate([e[HALO:] for e in edges], axis=0).astype(BF16)


def prepare_rest_kernel(noise_ref, near_ref, far_ref, *out_refs):
    walls, _, height, cols = near_ref.shape
    block = noise_ref.shape[1] // walls
    me = lax.axis_index("wall")
    c = pl.program_id(0)
    target = pl.ds(pl.multiple_of(c * block, block), block)
    for step, out_ref in enumerate(out_refs):
        source = pl.multiple_of((me ^ step) * block, block)
        out_ref[target] = noise_ref[0, pl.ds(source, block)]
    pairs = height // HALO
    pick = edge_picker(cols)
    for w in range(walls):
        edges = []
        for pair in range(pairs):
            plane = noise_ref[0, (w * pairs + pair) * cols : (w * pairs + pair + 1) * cols]
            edges.append(lax.dot_general(pick, plane, ROWS_BY_ROWS, preferred_element_type=F32))
        near_ref[w, c] = jnp.concatenate([e[:HALO] for e in edges], axis=0).astype(BF16)
        far_ref[w, c] = jnp.concatenate([e[HALO:] for e in edges], axis=0).astype(BF16)


def swap_blocks(blocks, cols):
    part = cols // EDGE
    lane = iota(blocks[0].shape, 1)
    for step in (2, 1):
        first = (lane // (part * step)) % 2 == 0
        out = list(blocks)
        for a in range(EDGE):
            if a & step:
                continue
            one, two = blocks[a], blocks[a + step]
            out[a] = jnp.where(first, one, pltpu.roll(two, part * step, 1))
            out[a + step] = jnp.where(first, pltpu.roll(one, cols - part * step, 1), two)
        blocks = out
    return blocks


def halo_tiles(parts, cols):
    half = cols // 2
    sides = []
    for side in parts:
        planes = [[], []]
        for one, two in zip(side[::2], side[1::2]):
            lower = iota(one.shape, 1) < half
            planes[0].append(jnp.where(lower, one, pltpu.roll(two, half, 1)))
            planes[1].append(jnp.where(lower, pltpu.roll(one, half, 1), two))
        sides.append([jnp.concatenate(p, axis=1) for p in planes])
    pairs = sides[0][0].shape[0] // HALO
    zeros = jnp.zeros((cols - 4 * HALO, sides[0][0].shape[1]), F32)
    for pair in range(pairs):
        at = slice(pair * HALO, (pair + 1) * HALO)
        tile = [sides[s][odd][at] for s in range(2) for odd in range(2)]
        yield jnp.concatenate(tile + [zeros], axis=0).astype(BF16)


def span_product(x, matrix):
    cols = x.shape[1]
    both = jnp.dot(jnp.concatenate(split(x), axis=1), matrix, preferred_element_type=F32)
    return both[:, :cols] + both[:, cols:]


def main_part(planes, wall, matrix):
    both = jnp.concatenate(planes, axis=1)
    cols = planes[0].shape[1]
    smooth = jnp.dot(wall, jnp.concatenate([both, both], axis=0), preferred_element_type=F32)
    return [span_product(smooth[:, odd * cols : (odd + 1) * cols], matrix) for odd in range(2)]


def halo_part(tile, wall, halo_ref):
    smooth = lax.dot_general(
        wall, jnp.concatenate([tile, tile], axis=1), ROWS_BY_ROWS, preferred_element_type=F32
    )
    return [span_product(smooth, halo_ref[odd]) for odd in range(2)]


def planes_of(refs, t, rows):
    return [
        jnp.concatenate([ref[at * rows : (at + 1) * rows] for ref in refs], axis=0) for at in (t, t + 1)
    ]


def main_kernel(planes, wall_ref, main_ref, *rest):
    *refs, psi_ref = rest
    rows = psi_ref.shape[1] // len(refs)
    for t in range(0, psi_ref.shape[0], 2):
        c = t // planes
        psi_ref[t], psi_ref[t + 1] = main_part(planes_of(refs, t, rows), wall_ref[c], main_ref[c])


def main_and_small_kernel(planes, slots, wall_ref, main_ref, *rest):
    *in_refs, psi_ref, factor_ref, target_ref = rest
    main_kernel(planes, wall_ref, main_ref, *in_refs, psi_ref)
    small_kernel(slots, *in_refs, factor_ref, target_ref)


def widen(factor_ref, wide_ref, which):
    for f in which:
        wide_ref[f] = jnp.broadcast_to(factor_ref[:, f : f + 1], wide_ref.shape[1:])


def place_cells(velocity, t, cells_ref, at):
    full, cols = velocity.shape
    quarter, faces = full // EDGE, full // (EDGE * EDGE)
    values = cells_ref.shape[1] // faces
    blocks = [velocity[a * quarter : (a + 1) * quarter] for a in range(EDGE)]
    for dz, block in enumerate(swap_blocks(blocks, cols)):
        for dy in range(EDGE):
            j = t * EDGE * EDGE + dy * EDGE + dz
            cells_ref[at, pl.ds(j, faces, stride=values), :] = block[dy * faces : (dy + 1) * faces]


def scatter_cells(cells_ref, target_ref, sent_ref, out_ref, sems):
    walls, tile_faces, cols = target_ref.shape
    some = cells_ref.shape[0]
    values = cells_ref.shape[1] // (walls * tile_faces)
    _, devices, slots, width = sent_ref.shape
    copies = []
    for w in range(walls):
        payload = [
            [
                cells_ref[at, pl.ds((w * tile_faces + f) * values, values), :].astype(BF16)
                for f in range(tile_faces)
            ]
            for at in range(some)
        ]
        payload = jnp.concatenate([jnp.concatenate(p, axis=1) for p in payload], axis=0)
        slot = iota((devices * slots, cols), 0)
        onehot = [
            jnp.where(slot == target_ref[w, f : f + 1], 1.0, 0.0).astype(BF16)
            for f in range(tile_faces)
        ]
        onehot = jnp.concatenate(onehot, axis=1)
        sent = lax.dot_general(onehot, payload, ROWS_BY_ROWS, preferred_element_type=F32)
        sent_ref[w] = sent.astype(BF16).reshape(devices, slots, width)
        copies.append(pltpu.make_async_copy(sent_ref.at[w], out_ref.at[:, w], sems.at[w]))
        copies[-1].start()
    for copy in copies:
        copy.wait()


def first_kernel(
    planes, psi_in, near_ref, far_ref, factor_ref, target_ref, wall_ref, halo_ref,
    out_ref, psi_out, psi_ref, cells_ref, wide_ref, sent_ref, sems, psi_sem,
):
    full, cols = psi_ref.shape[1:]
    wide = 2 * HALO
    widen(factor_ref, wide_ref, (0, 6))

    def psi_copy(pair):
        at = pl.ds(2 * pair, 2)
        return pltpu.make_async_copy(psi_ref.at[at], psi_out.at[at], psi_sem.at[pair])

    def pair_step(pair, carry):
        at = pl.ds(pl.multiple_of(pair * wide, wide), wide)
        tile = [near_ref[at], far_ref[at], jnp.zeros((cols - 2 * wide, full), BF16)]
        beside = halo_part(jnp.concatenate(tile, axis=0), wall_ref[0], halo_ref.at[0])
        for odd in range(2):
            t = 2 * pair + odd
            psi = psi_in[t] + beside[odd]
            psi_ref[t] = psi
            place_cells(wide_ref[6] + wide_ref[0] * psi, t, cells_ref, 0)
        psi_copy(pair).start()
        return carry

    lax.fori_loop(0, planes // 2, pair_step, 0, unroll=True)
    scatter_cells(cells_ref, target_ref, sent_ref, out_ref, sems)
    for pair in range(planes // 2):
        psi_copy(pair).wait()


def rest_kernel(
    planes, psi_ref, next_ref, factor_ref, target_ref, wall_ref, main_ref, halo_ref, *rest,
):
    *late_refs, out_ref, cells_ref, tile_ref, wide_ref, sent_ref, sems = rest
    full, cols = psi_ref.shape[1:]
    some = wall_ref.shape[0]
    pairs = planes // 2
    height = pairs * HALO
    widen(factor_ref, wide_ref, range(1, 6))
    for c in range(some):
        starts = [(side * some + c) * height for side in range(2)]
        parts = [[ref[pl.ds(at, height)].astype(F32) for ref in late_refs] for at in starts]
        for pair, tile in enumerate(halo_tiles(parts, cols)):
            tile_ref[c * pairs + pair] = tile

    for pair in range(pairs):
        psi = []
        for c in range(some):
            main = [next_ref[c * planes + 2 * pair + odd] for odd in range(2)]
            beside = halo_part(tile_ref[c * pairs + pair], wall_ref[c], halo_ref.at[c])
            psi.append([m + b for m, b in zip(main, beside)])
        for odd in range(2):
            t = 2 * pair + odd
            p, q, r = psi_ref[t], psi[0][odd], psi[1][odd]
            place_cells(wide_ref[1] * p + wide_ref[2] * q, t, cells_ref, 0)
            place_cells(wide_ref[3] * p + wide_ref[4] * q + wide_ref[5] * r, t, cells_ref, 1)
    scatter_cells(cells_ref, target_ref, sent_ref, out_ref, sems)


def join_kernel(first, some, in_ref, *rest):
    out_ref, sems = rest[-2:]
    _, walls, _, width = in_ref.shape
    values = width // some
    run(
        [
            pltpu.make_async_copy(
                in_ref.at[:, w, :, pl.ds(c * values, values)],
                out_ref.at[:, :, pl.ds(((c + first) * walls + w) * values, values)],
                sems.at[c, w],
            )
            for c in range(some)
            for w in range(walls)
        ]
    )


def join_narrow_kernel(some, in_ref, *rest):
    out_ref = rest[-1]
    _, walls, _, width = in_ref.shape
    values = width // some
    for c in range(some):

        @pl.when(pl.program_id(1) == c)
        def _():
            for w in range(walls):
                out_ref[0, :, w * values : (w + 1) * values] = in_ref[0, w, :, c * values : (c + 1) * values]


def per_device(noise, wall_scale, span_scale, lund_factor, mean_velocity, owner_map):
    trio, all_planes, rows, cols = noise.shape
    n_span = lax.axis_size("span")
    n_wall = lax.axis_size("wall")
    devices = n_span * n_wall
    planes = all_planes // n_wall
    pairs = planes // 2
    full = rows * n_wall
    faces = full // (EDGE * EDGE)
    values = planes * EDGE * EDGE
    owners = owner_map.reshape(1, -1)
    elements = owners.shape[1]
    slots = max(8, 2 * elements // devices)
    count = elements // cols
    rest = trio - 1
    struct = jax.ShapeDtypeStruct
    hbm = pltpu.MemorySpace.HBM

    def call(kernel, ins, outs, name, limit, scratch=(), grid=(), out_specs=None, us=1):
        specs = out_specs or [VMEM] * len(outs)
        return pl.pallas_call(
            kernel,
            grid=grid,
            in_specs=ins,
            out_specs=specs if len(outs) > 1 else specs[0],
            out_shape=outs if len(outs) > 1 else outs[0],
            scratch_shapes=scratch,
            compiler_params=pltpu.CompilerParams(vmem_limit_bytes=limit * 1024 * 1024),
            cost_estimate=pl.CostEstimate(flops=us * 10**9, bytes_accessed=1024, transcendentals=0),
            name=name,
        )

    core_pairs = [(i, i ^ 1) for i in range(n_span)]
    chip_pairs = [(i, (i + 2 * (i % CORES) - 1) % n_span) for i in range(n_span)]

    def exchange(near, far):
        return lax.ppermute(near, "span", core_pairs), lax.ppermute(far, "span", chip_pairs)

    def spread(blocks):
        return [blocks[0]] + [
            lax.ppermute(x, "wall", [(i, i ^ step) for i in range(n_wall)])
            for step, x in enumerate(blocks[1:], 1)
        ]

    def send(x):
        return lax.all_to_all(x, ("span", "wall"), 0, 0, tiled=True).reshape(devices, n_wall * slots, -1)

    dma = pltpu.SemaphoreType.DMA
    noise = noise.reshape(trio, all_planes * rows, cols)
    packed = call(
        functools.partial(pack_kernel, devices),
        [pl.BlockSpec(memory_space=hbm)] * 4,
        [pltpu.MemorySpace.VMEM((planes * rows + tail_rows(count), cols), BF16)] * n_wall,
        "pack",
        56,
        [
            pltpu.VMEM((all_planes * rows, cols), BF16),
            pltpu.VMEM(lund_factor.shape, F32),
            pltpu.VMEM((1, rows), F32),
            pltpu.VMEM(owners.shape, jnp.int32),
            dma((4,)),
        ],
    )(noise, lund_factor, mean_velocity.reshape(1, rows), owners)
    noise, packed = lax.optimization_barrier((noise, packed))
    packed = spread(packed)

    height = pairs * HALO
    edge = struct((n_wall, rest, height, cols), BF16)
    near, far, *early = call(
        prepare_rest_kernel,
        [pl.BlockSpec((1, all_planes * rows, cols), lambda c: (c + 1, 0, 0))],
        [edge, edge] + [struct((rest * planes * rows, cols), BF16)] * n_wall,
        "prepare_rest",
        16,
        grid=(rest,),
    )(noise)
    rest_near, rest_far = exchange(near, far)
    packed, _ = lax.optimization_barrier((packed, (near, far, early)))

    def taps(first, some, make, name):
        return call(
            functools.partial(taps_kernel, first),
            [SMEM, SMEM],
            [
                make((some, full, 2 * full), BF16),
                make((some, 2 * cols, 2 * cols), BF16),
                make((some, 2, 2 * cols, 2 * cols), BF16),
            ],
            name,
            16,
        )(wall_scale, span_scale)

    wall_first, main_first, halo_first = taps(0, 1, struct, "taps_first")

    edge = struct((planes * HALO, full), BF16)
    near, far = call(
        functools.partial(edges_kernel, planes), [VMEM] * n_wall, [edge, edge], "edges_first", 16
    )(*packed)
    near, far = exchange(near, far)
    early, rest_near = lax.optimization_barrier((early, rest_near))
    early = spread(early)
    (rest_near, rest_far), _ = lax.optimization_barrier(((rest_near, rest_far), (near, far)))
    near, rest_near, rest_far = lax.optimization_barrier((near, rest_near, rest_far))

    psi = struct((planes, full, cols), F32)
    psi_main, factor, target = call(
        functools.partial(main_and_small_kernel, planes, slots),
        [VMEM] * (2 + n_wall),
        [psi, struct((full, cols), F32), struct((n_wall, count, cols), jnp.int32)],
        "main_first",
        16,
    )(wall_first, main_first, *packed)

    def scratch(some):
        return [
            pltpu.VMEM((some, faces * values, cols), F32),
            pltpu.VMEM((rest * pairs, cols, full), BF16),
            pltpu.VMEM((FACTORS, full, cols), F32),
            pltpu.VMEM((n_wall, devices, slots, some * values), BF16),
            dma((n_wall,)),
        ]

    def out(some):
        return hbm((devices, n_wall, slots, some * values), BF16)

    cells, _, *more = scratch(1)
    sent, psi = call(
        functools.partial(first_kernel, planes),
        [VMEM] * 7,
        [out(1), hbm(psi.shape, F32)],
        "filter_first",
        24,
        [pltpu.VMEM(psi.shape, F32), cells, *more, dma((pairs,))],
        out_specs=[ANYWHERE, ANYWHERE],
    )(psi_main, near, far, factor, target, wall_first, halo_first)
    (wall_scale, span_scale, rest_near, rest_far), sent = lax.optimization_barrier(
        ((wall_scale, span_scale, rest_near, rest_far), sent)
    )
    got_first = send(sent)
    late = call(
        pack_late_kernel,
        [VMEM] * 2,
        [hbm((2 * rest * height, cols), BF16)] * n_wall,
        "pack_late",
        16,
        [dma((n_wall, 2 * rest))],
        out_specs=[ANYWHERE] * n_wall,
    )(rest_near, rest_far)
    late = spread(late)
    wall_rest, main_rest, halo_rest = taps(1, rest, struct, "taps_rest")
    psi_next = call(
        functools.partial(main_kernel, planes),
        [VMEM] * (2 + n_wall),
        [struct((rest * planes, full, cols), F32)],
        "main_next",
        16,
    )(wall_rest, main_rest, *early)
    sent = call(
        functools.partial(rest_kernel, planes),
        [VMEM] * (7 + n_wall),
        [out(rest)],
        "filter_rest",
        32,
        scratch(rest),
        out_specs=[ANYWHERE],
        us=100,
    )(psi, psi_next, factor, target, wall_rest, main_rest, halo_rest, *late)
    got_rest = send(sent)

    whole = hbm((n_span, n_wall * slots, trio * values * n_wall), BF16)
    narrow = values % LANES != 0

    def join(received, some, before):
        keep = [] if before is None else [before]
        shape = (n_span, n_wall, n_wall * slots, some * values)
        return pl.pallas_call(
            functools.partial(join_narrow_kernel, some)
            if narrow
            else functools.partial(join_kernel, len(keep), some),
            grid=(n_span, some) if narrow else (),
            in_specs=[pl.BlockSpec((1, *shape[1:]), lambda s, c: (s, 0, 0, 0)) if narrow else VMEM]
            + [ANYWHERE] * len(keep),
            out_specs=pl.BlockSpec((1, n_wall * slots, values * n_wall), lambda s, c: (s, 0, c + len(keep)))
            if narrow
            else ANYWHERE,
            out_shape=whole,
            scratch_shapes=[] if narrow else [dma((some, n_wall))],
            input_output_aliases={1: 0} if keep else {},
            compiler_params=pltpu.CompilerParams(vmem_limit_bytes=16 * 1024 * 1024),
            name="join",
        )(received.reshape(shape), *keep)

    return join(got_rest, rest, join(got_first, 1, None)).reshape(1, devices * slots, -1)


def solution(mesh):
    return jax.shard_map(
        per_device,
        mesh=mesh,
        in_specs=(
            P(None, None, "wall", "span"),
            P(),
            P(),
            P(None, "wall"),
            P("wall"),
            P("wall", "span", None, None),
        ),
        out_specs=P(("span", "wall"), None, None),
        check_vma=False,
    )
```
